32 devices in a mesh: seq: 16 (over z, x, core), tensor: 2 (over y).
Axes of the slice: x: 2, y: 2, z: 4, core: 2. Of those that a mesh axis runs over, the one named last changes fastest.
Arguments:
- projected: bfloat16 [3, 4096, 4096], P(None, 'seq', 'tensor'), may hold values from -6 to 6
- feat_weight: float32 [3, 7, 4096], P(None, None, 'tensor'), may hold values from -2 to 2
- long_filter: float32 [4096, 4096], P(('tensor', 'seq')), may hold values from -1.2 to 1.2
- skip_gain: float32 [4096], P(('tensor', 'seq')), may hold values from 0.5 to 1.5
- out_values: bfloat16 [4096, 2048], P('tensor'), may hold values from -0.125 to 0.125
- out_scales: float32 [32, 16], P('tensor'), may hold values from 0.125 to 1
Outputs:
- mixed: bfloat16 [4096, 2048], P('seq', 'tensor')
The draws below stay inside these ranges and needn't reach their ends.
All inputs are finite; a program needn't handle non-finite values.
Results may differ from the reference program's by a relative error of at most 0.023.
Values may be sent and summed in bfloat16 or wider, within the bound.
A program may use at most 128 MiB of HBM per device.

```python
import math
import jax
import jax.numpy as jnp
from jax import lax

CHANNEL_COUNT = 4096
D_OUT = 2048
KS = 7
BLK = 128
SEQUENCE_LENGTH = 4096
N_TENSOR = 2


def draw_long_filter(key, part):
    random_child_keys = [jax.random.fold_in(key, 101 + index) for index in range(8)]
    slow_share = 0.5
    chooser = jax.random.uniform(random_child_keys[0], (CHANNEL_COUNT, 1))
    slow_decay = jnp.exp(jax.random.uniform(random_child_keys[1], (CHANNEL_COUNT, 1), minval=math.log(0.1 / SEQUENCE_LENGTH), maxval=math.log(1.0 / SEQUENCE_LENGTH)))
    fast_decay = jnp.exp(jax.random.uniform(random_child_keys[2], (CHANNEL_COUNT, 1), minval=math.log(1.0 / 50.0), maxval=math.log(1.0 / 30.0)))
    decay_rate = jnp.where(chooser < slow_share, slow_decay, fast_decay)
    delay_index = jnp.arange(SEQUENCE_LENGTH, dtype=jnp.int32)[None, :]
    lag_grid = delay_index.astype(jnp.float32)
    decay_profile = jnp.exp(-decay_rate * lag_grid)
    for spike_index in range(2):
        spike_position = jax.random.randint(random_child_keys[3 + spike_index], (CHANNEL_COUNT, 1), 1, SEQUENCE_LENGTH)
        multiplier = jax.random.uniform(random_child_keys[5 + spike_index], (CHANNEL_COUNT, 1), minval=0.6, maxval=0.8)
        decay_profile = decay_profile * jnp.where(delay_index >= spike_position, multiplier, 1.0)
    scaling = jnp.sqrt(jnp.expm1(-2.0 * decay_rate) / jnp.expm1(-2.0 * decay_rate * SEQUENCE_LENGTH))
    rough_part = jax.random.truncated_normal(random_child_keys[7], -4.0, 4.0, (CHANNEL_COUNT, SEQUENCE_LENGTH))
    return (decay_profile * scaling * rough_part).astype(jnp.float32)


def raised(drawn, stream_key, source, target, parts, factor):
    owner, partner = [(jnp.arange(drawn.shape[dim]) // (drawn.shape[dim] // parts)).reshape([-1 if axis == dim else 1 for axis in range(drawn.ndim)]) for dim in (source, target)]
    chosen = jax.random.permutation(stream_key, parts)[partner]
    strong = (owner == chosen) | (owner == (partner + parts // 2) % parts)
    return jnp.where(strong, factor * drawn, drawn)


def level_of(own_key, extent, shards, low, largest):
    def one(position, blocks):
        draws = jax.random.uniform(jax.random.fold_in(jax.random.fold_in(own_key, 6), position), (blocks,), jnp.float32, low / len(shards), largest / len(shards))
        return jnp.repeat(jnp.exp(draws), extent[position] // blocks).reshape((-1,) + (1,) * (len(extent) - position - 1))

    factor_of = one(*shards[0])
    for cut in shards[1:]:
        factor_of = factor_of * one(*cut)
    return factor_of


def scatter_about(stream_key, dims, deviation, most, split=(), kind=jnp.bfloat16):
    entries = deviation * jax.random.normal(stream_key, dims, jnp.float32)
    if split:
        entries = entries * level_of(stream_key, dims, split, -0.22, 0.18)
    return jnp.clip(entries, -most, most).astype(kind)


def heavy_noise(key, extent, scale, limit, pieces, heavy, held_as=jnp.bfloat16):
    values = scale * jax.random.normal(key, extent, jnp.float32)
    if pieces:
        values = values * level_of(key, extent, pieces, -0.22, 0.18)
    return jnp.clip(raised(values, jax.random.fold_in(key, 3), *heavy), -limit, limit).astype(held_as)


def setup_inputs(seed: int = 0) -> dict:
    key_list = jax.random.split(jax.random.key(seed), 7)
    projected = scatter_about(key_list[0], (3, SEQUENCE_LENGTH, CHANNEL_COUNT), 1.0, 6.0, ((1, 16), (2, 2)))
    feat_weight = scatter_about(key_list[1], (3, KS, CHANNEL_COUNT), 0.35, 2.0, ((2, 2),), jnp.float32)
    long_filter = draw_long_filter(jax.random.fold_in(key_list[6], 71), 0)
    skip_gain = jnp.clip(0.5 + 1.0 * jax.random.uniform(key_list[3], (CHANNEL_COUNT,), jnp.float32) ** level_of(key_list[3], (CHANNEL_COUNT,), ((0, 32),), -0.2, 0.2), 0.5, 1.5)
    out_values = heavy_noise(key_list[4], (CHANNEL_COUNT, D_OUT), CHANNEL_COUNT ** -0.5, 0.125, ((0, 2),), (0, 1, 2, 2.0))
    out_scales = jnp.clip(jnp.exp(math.log(1.0) - 2.0794415 * jax.random.uniform(key_list[5], (CHANNEL_COUNT // BLK, D_OUT // BLK), jnp.float32) ** level_of(key_list[5], (CHANNEL_COUNT // BLK, D_OUT // BLK), ((0, 2),), -0.2, 0.2)), 0.125, 1.0)
    return dict(projected=projected, feat_weight=feat_weight, long_filter=long_filter, skip_gain=skip_gain, out_values=out_values, out_scales=out_scales)


def reference(projected, feat_weight, long_filter, skip_gain, out_values, out_scales):
    tap_count = KS
    padded = jnp.pad(projected, ((0, 0), (tap_count - 1, 0), (0, 0)))
    running = jnp.zeros(projected.shape, jnp.float32)
    for lag_idx in range(tap_count):
        offset = tap_count - 1 - lag_idx
        running = running + feat_weight[:, lag_idx, None, :] * padded[:, offset:offset + SEQUENCE_LENGTH, :].astype(jnp.float32)
    featured = running.astype(jnp.bfloat16)
    gated_kv = (featured[1].astype(jnp.float32) * featured[2].astype(jnp.float32)).astype(jnp.bfloat16)
    chan_block = math.gcd(CHANNEL_COUNT, 256)
    kv_rows = jnp.transpose(gated_kv, (1, 0)).reshape(CHANNEL_COUNT // chan_block, chan_block, SEQUENCE_LENGTH)
    filter_rows = long_filter.reshape(CHANNEL_COUNT // chan_block, chan_block, SEQUENCE_LENGTH)
    gain_rows = skip_gain.reshape(CHANNEL_COUNT // chan_block, chan_block)

    def convolve(inputs):
        kv_values = inputs[0].astype(jnp.float32)
        filter_taps = inputs[1]
        gains = inputs[2]
        spectrum = jnp.fft.rfft(kv_values, n=2 * SEQUENCE_LENGTH, axis=1) * jnp.fft.rfft(filter_taps, n=2 * SEQUENCE_LENGTH, axis=1)
        convolved = jnp.fft.irfft(spectrum, n=2 * SEQUENCE_LENGTH, axis=1)[:, :SEQUENCE_LENGTH]
        return (convolved + gains[:, None] * kv_values).astype(jnp.bfloat16)

    filtered = lax.map(convolve, (kv_rows, filter_rows, gain_rows)).reshape(CHANNEL_COUNT, SEQUENCE_LENGTH)
    gated = (featured[0].astype(jnp.float32) * jnp.transpose(filtered, (1, 0)).astype(jnp.float32)).astype(jnp.bfloat16)
    group_ch = CHANNEL_COUNT // N_TENSOR
    per_group = group_ch // BLK
    out_total = jnp.zeros((SEQUENCE_LENGTH, D_OUT), jnp.float32)
    for group_idx in range(N_TENSOR):
        partial_value = jnp.zeros((SEQUENCE_LENGTH, D_OUT), jnp.float32)
        for inner_idx in range(per_group):
            block_row = group_idx * per_group + inner_idx
            low_row = block_row * BLK
            product = jnp.dot(gated[:, low_row:low_row + BLK], out_values[low_row:low_row + BLK, :], preferred_element_type=jnp.float32)
            partial_value = partial_value + product * jnp.repeat(out_scales[block_row], BLK)[None, :]
        rounded = lax.optimization_barrier(partial_value.astype(jnp.bfloat16))
        out_total = out_total + rounded.astype(jnp.float32)
    return out_total.astype(jnp.bfloat16)
```

```python
import functools
import math

import jax
import jax.numpy as jnp
import ml_dtypes
import numpy as np
from jax import lax
from jax.experimental import pallas as pl
from jax.experimental.pallas import tpu as pltpu
from jax.sharding import PartitionSpec as P

KS = 7
BLK = 128
LANES = 128
RIM = 16
SUB = 16
CHUNK = 64
MESH_ID = pl.DeviceIdType.MESH
BF16 = jnp.bfloat16
F32 = jnp.float32


def dft_tables(groups, rows):
    whole = 2 * groups * rows
    kept = groups + 1
    padded = kept + kept % 2
    n_a = np.arange(groups)
    k_a = np.arange(kept)
    r = np.arange(rows)
    turns = k_a[:, None, None] * (n_a[None, :, None] * rows + r[None, None, :]) % whole
    angles = turns * (2.0 * np.pi / whole)
    parts = np.stack([np.cos(angles), -np.sin(angles)], axis=1)
    blocks = parts.reshape(kept, 2, groups, rows // SUB, SUB)
    first = np.zeros((rows // SUB, padded, 2, SUB, groups, SUB))
    last = np.zeros((rows // SUB, groups, SUB, padded, 2, SUB))
    weight = np.full((kept,), 2.0 / whole)
    weight[0] = weight[-1] = 1.0 / whole
    for lo in range(SUB):
        cut = blocks[:, :, :, :, lo]
        first[:, :kept, :, lo, :, lo] = cut.transpose(3, 0, 1, 2)
        last[:, :, lo, :kept, :, lo] = (cut * weight[:, None, None, None]).transpose(3, 2, 0, 1)
    first = first.reshape(rows // SUB, padded * 2 * SUB, groups * SUB)
    last = last.reshape(rows // SUB, groups * SUB, padded * 2 * SUB)
    inner = (r[:, None] * r[None, :] % rows) * (2.0 * np.pi / rows)
    cos, sin = np.cos(inner), np.sin(inner)
    ahead = np.block([[cos, sin], [-sin, cos]])
    back = np.block([[cos, -sin], [sin, cos]])
    return [x.astype(ml_dtypes.bfloat16) for x in (first, ahead, back, last)]


def dot(a, b):
    return jnp.dot(a, b, preferred_element_type=F32)


def fused_kernel(
    groups,
    rows,
    proj,
    taps,
    filt,
    gain,
    weights,
    scales,
    t_first,
    t_ahead,
    t_back,
    t_last,
    out,
    pb,
    g_out,
    u_in,
    v_out,
    f_in,
    feat_q,
    fl,
    ft,
    x1,
    spec,
    m_first,
    m_ahead,
    m_back,
    m_last,
    w,
    gated,
    part_own,
    part_out,
    part_in,
    loc_sem,
    halo_sem,
    send_sem,
    recv_u,
    recv_f,
    recv_p,
):
    me = lax.axis_index("seq")
    mine = lax.axis_index("tensor")
    other = 1 - mine
    chunks = rows // CHUNK
    length = groups * rows
    half = part_own.shape[1]

    load_k = pltpu.make_async_copy(proj, pb.at[:, pl.ds(RIM, rows)], loc_sem.at[0])
    load_k.start()

    barrier = pltpu.get_barrier_semaphore()

    @pl.loop(1, groups)
    def _(step):
        peer = lax.rem(me + step, groups)
        pl.semaphore_signal(barrier, inc=1, device_id=(peer, mine), device_id_type=MESH_ID)

    pl.semaphore_signal(barrier, inc=1, device_id=(me, other), device_id_type=MESH_ID)
    pl.semaphore_wait(barrier, groups)

    halo = pltpu.make_async_remote_copy(
        src_ref=proj.at[:, pl.ds(rows - RIM, RIM)],
        dst_ref=pb.at[:, pl.ds(0, RIM)],
        send_sem=halo_sem.at[0],
        recv_sem=halo_sem.at[1],
        device_id=(lax.rem(me + 1, groups), mine),
        device_id_type=MESH_ID,
    )

    @pl.when(me < groups - 1)
    def _():
        halo.start()

    @pl.when(me == 0)
    def _():
        pb[:, 0:RIM, :] = jnp.zeros((pb.shape[0], RIM, pb.shape[2]), BF16)

    load_k.wait()
    loads = [
        pltpu.make_async_copy(src, dst, loc_sem.at[1 + i])
        for i, (src, dst) in enumerate(
            (
                (filt, fl),
                (t_first, m_first),
                (t_ahead, m_ahead),
                (t_back, m_back),
                (t_last, m_last),
                (weights, w),
            )
        )
    ]
    for load in loads:
        load.start()

    def featured(p, q, j):
        lanes = pl.ds(pl.multiple_of(j * LANES, LANES), LANES)
        x = pb[p, pl.ds(pl.multiple_of(q * CHUNK, CHUNK), CHUNK + RIM), lanes].astype(F32)
        run = None
        for lag in range(KS):
            term = taps[p, lag : lag + 1, lanes] * x[RIM - lag : RIM - lag + CHUNK]
            run = term if run is None else run + term
        return run.astype(BF16)

    def rows_of(q):
        return pl.ds(pl.multiple_of(q * CHUNK, CHUNK), CHUNK)

    def spread(src, dst, q, recv):
        @pl.loop(1, groups)
        def _(step):
            peer = lax.rem(me + step, groups)
            pltpu.make_async_remote_copy(
                src_ref=src.at[peer, rows_of(q)],
                dst_ref=dst.at[me, rows_of(q)],
                send_sem=send_sem.at[recv],
                recv_sem=(recv_u if recv == 0 else recv_f).at[q],
                device_id=(peer, mine),
                device_id_type=MESH_ID,
            ).start()

        dst[me, rows_of(q), :] = src[me, rows_of(q), :]

    def await_chunk(dst, q, sem):
        view = dst.at[pl.ds(0, groups - 1), rows_of(q)]
        pltpu.make_async_copy(view, view, sem.at[q]).wait()

    def feature_chunk(q):
        @pl.loop(0, groups)
        def _(j):
            k = featured(1, q, j).astype(F32)
            v = featured(2, q, j).astype(F32)
            g_out[j, rows_of(q), :] = (k * v).astype(BF16)

        spread(g_out, u_in, q, 0)

    @pl.loop(1, chunks)
    def _(q):
        feature_chunk(q)

    @pl.when(me > 0)
    def _():
        halo.wait_recv()

    feature_chunk(0)

    loads[0].wait()

    @pl.loop(0, groups)
    def _(a):
        for part in range(rows // LANES):
            start = pl.multiple_of(a * rows + part * LANES, LANES)
            ft[a, part * LANES : (part + 1) * LANES, :] = fl[:, pl.ds(start, LANES)].T.astype(BF16)

    for load in loads[1:5]:
        load.wait()

    slabs = x1.shape[0]
    pairs = slabs // 4

    def first_stage(src, s):
        at = pl.ds(pl.multiple_of(s * SUB, SUB), SUB)
        block = src[:, at, :].reshape(groups * SUB, LANES)
        x1[:, at, :] = dot(m_first[s], block).astype(BF16).reshape(slabs, SUB, LANES)

    def pair_of(j):
        left = x1[pl.ds(4 * j, 2)].reshape(2 * rows, LANES)
        right = x1[pl.ds(4 * j + 2, 2)].reshape(2 * rows, LANES)
        return jnp.concatenate([left, right], axis=1)

    @pl.loop(0, rows // SUB)
    def _(s):
        first_stage(ft, s)

    @pl.loop(0, pairs)
    def _(j):
        spec[j] = dot(m_ahead[...], pair_of(j))

    loads[5].wait()
    cuts = w.shape[1] // BLK

    @pl.loop(0, w.shape[0] // BLK)
    def _(b):
        at = pl.ds(pl.multiple_of(b * BLK, BLK), BLK)
        for n in range(cuts):
            cols = slice(n * BLK, (n + 1) * BLK)
            w[at, cols] = (w[at, cols].astype(F32) * scales[b, n]).astype(BF16)

    @pl.loop(0, chunks)
    def _(q):
        @pl.loop(0, groups)
        def _(j):
            feat_q[j, rows_of(q), :] = featured(0, q, j)

    per_chunk = CHUNK // SUB

    @pl.loop(0, chunks)
    def _(i):
        q = lax.rem(i + 1, chunks)
        await_chunk(u_in, q, recv_u)

        @pl.loop(0, per_chunk)
        def _(s):
            first_stage(u_in, q * per_chunk + s)

    @pl.loop(0, pairs)
    def _(j):
        values = dot(m_ahead[...], pair_of(j))
        re_u, im_u = values[:rows], values[rows:]
        re_h, im_h = spec[j, 0:rows, :], spec[j, rows : 2 * rows, :]
        product = jnp.concatenate(
            [re_u * re_h - im_u * im_h, re_u * im_h + im_u * re_h], axis=0
        ).astype(BF16)
        z = dot(m_back[...], product).astype(BF16)
        x1[pl.ds(4 * j, 2)] = z[:, :LANES].reshape(2, rows, LANES)
        x1[pl.ds(4 * j + 2, 2)] = z[:, LANES:].reshape(2, rows, LANES)

    @pl.loop(0, chunks)
    def _(q):
        @pl.loop(0, per_chunk)
        def _(i):
            s = q * per_chunk + i
            at = pl.ds(pl.multiple_of(s * SUB, SUB), SUB)
            conv = dot(m_last[s], x1[:, at, :].reshape(slabs * SUB, LANES))
            direct = gain[...] * u_in[:, at, :].reshape(groups * SUB, LANES).astype(F32)
            v_out[:, at, :] = (conv + direct).astype(BF16).reshape(groups, SUB, LANES)

        spread(v_out, f_in, q, 1)

    def swap(q):
        return pltpu.make_async_remote_copy(
            src_ref=part_out.at[rows_of(q)],
            dst_ref=part_in.at[rows_of(q)],
            send_sem=send_sem.at[2],
            recv_sem=recv_p.at[q],
            device_id=(me, other),
            device_id_type=MESH_ID,
        )

    @pl.loop(0, chunks)
    def _(q):
        await_chunk(f_in, q, recv_f)
        for j in range(groups):
            product = feat_q[j, rows_of(q), :].astype(F32) * f_in[j, rows_of(q), :].astype(F32)
            gated[:, j * LANES : (j + 1) * LANES] = product.astype(BF16)
        theirs = pl.ds(pl.multiple_of(other * half, half), half)
        ours = pl.ds(pl.multiple_of(mine * half, half), half)
        part_out[rows_of(q), :] = dot(gated[...], w[:, theirs]).astype(BF16)
        swap(q).start()
        part_own[rows_of(q), :] = dot(gated[...], w[:, ours]).astype(BF16)

    @pl.loop(0, chunks)
    def _(q):
        swap(q).wait_recv()
        total = part_own[rows_of(q), :].astype(F32) + part_in[rows_of(q), :].astype(F32)
        out[rows_of(q), :] = total.astype(BF16)

    @pl.when(me < groups - 1)
    def _():
        halo.wait_send()

    sent = g_out.at[pl.ds(0, groups - 1)]
    pltpu.make_async_copy(sent, sent, send_sem.at[0]).wait()
    sent = v_out.at[pl.ds(0, groups - 1)]
    pltpu.make_async_copy(sent, sent, send_sem.at[1]).wait()
    pltpu.make_async_copy(part_out, part_out, send_sem.at[2]).wait()


def fused(projected, feat_weight, long_filter, skip_gain, out_values, out_scales):
    groups = lax.axis_size("seq")
    rows, local_ch = projected.shape[1:]
    out_width = out_values.shape[1]
    half = out_width // 2
    tables = dft_tables(groups, rows)
    slabs = tables[0].shape[1] // SUB
    hbm = pl.BlockSpec(memory_space=pl.ANY)
    vmem = pl.BlockSpec(memory_space=pltpu.VMEM)
    smem = pl.BlockSpec(memory_space=pltpu.SMEM)
    block = pltpu.VMEM((groups, rows, LANES), BF16)
    chunks = rows // CHUNK
    return pl.pallas_call(
        functools.partial(fused_kernel, groups, rows),
        out_shape=jax.ShapeDtypeStruct((rows, half), BF16),
        in_specs=[hbm, vmem, hbm, vmem, hbm, smem, hbm, hbm, hbm, hbm],
        out_specs=vmem,
        scratch_shapes=[
            pltpu.VMEM((3, RIM + rows, local_ch), BF16),
            block,
            block,
            block,
            block,
            block,
            pltpu.VMEM(long_filter.shape, F32),
            block,
            pltpu.VMEM((slabs, rows, LANES), BF16),
            pltpu.VMEM((slabs // 4, 2 * rows, 2 * LANES), F32),
            pltpu.VMEM(tables[0].shape, BF16),
            pltpu.VMEM(tables[1].shape, BF16),
            pltpu.VMEM(tables[2].shape, BF16),
            pltpu.VMEM(tables[3].shape, BF16),
            pltpu.VMEM(out_values.shape, BF16),
            pltpu.VMEM((CHUNK, local_ch), BF16),
            pltpu.VMEM((rows, half), BF16),
            pltpu.VMEM((rows, half), BF16),
            pltpu.VMEM((rows, half), BF16),
            pltpu.SemaphoreType.DMA((7,)),
            pltpu.SemaphoreType.DMA((2,)),
            pltpu.SemaphoreType.DMA((3,)),
            pltpu.SemaphoreType.DMA((chunks,)),
            pltpu.SemaphoreType.DMA((chunks,)),
            pltpu.SemaphoreType.DMA((chunks,)),
        ],
        compiler_params=pltpu.CompilerParams(
            collective_id=0, has_side_effects=True, vmem_limit_bytes=58 * 2**20
        ),
        cost_estimate=pl.CostEstimate(
            flops=10 * 10**9, bytes_accessed=32 * 2**20, transcendentals=0
        ),
    )(
        projected,
        feat_weight,
        long_filter,
        skip_gain.reshape(1, -1),
        out_values,
        out_scales,
        *[jnp.asarray(x) for x in tables],
    )


def fits(projected, long_filter, out_values):
    groups = lax.axis_size("seq")
    rows, local_ch = projected.shape[1:]
    return (
        lax.axis_size("tensor") == 2
        and long_filter.shape[0] == LANES
        and local_ch == groups * LANES
        and rows == 2 * LANES
        and groups == SUB
        and out_values.shape[1] % (2 * LANES) == 0
    )


TRIPLE = lax.Precision.HIGH


def passed_along(x, axis, by):
    size = lax.axis_size(axis)
    pairs = [(i, i + by) for i in range(size) if 0 <= i + by < size]
    return lax.ppermute(x, axis, pairs)


def split_length(whole):
    for candidate in range(2, whole + 1, 2):
        if whole % candidate == 0 and candidate * candidate >= whole:
            return (candidate, whole // candidate)
    return (whole, 1)


def angle_pair(row_count, col_count, period):
    row_ids = lax.broadcasted_iota(jnp.int32, (row_count, col_count), 0)
    col_ids = lax.broadcasted_iota(jnp.int32, (row_count, col_count), 1)
    angles = (row_ids * col_ids % period).astype(jnp.float32) * (2.0 * math.pi / period)
    return (jnp.cos(angles), jnp.sin(angles))


def make_tables(length):
    whole = 2 * length
    size_a, size_b = split_length(whole)
    return (
        angle_pair(size_a, size_a, size_a),
        angle_pair(size_b, size_b, size_b),
        angle_pair(size_a, size_b, whole),
        size_a,
        size_b,
    )


def right_mul(signal, matrix):
    return jnp.einsum("ckn,nm->ckm", signal, matrix, precision=TRIPLE)


def forward(signal, tables):
    (cos_a, sin_a), (cos_b, sin_b), (cos_t, sin_t), size_a, size_b = tables
    half_a = size_a // 2
    blocks = signal.reshape(signal.shape[0], half_a, size_b)
    real_a = jnp.einsum("kn,cnb->ckb", cos_a[:, :half_a], blocks, precision=TRIPLE)
    imag_a = -jnp.einsum("kn,cnb->ckb", sin_a[:, :half_a], blocks, precision=TRIPLE)
    real_t = real_a * cos_t + imag_a * sin_t
    imag_t = imag_a * cos_t - real_a * sin_t
    real_f = right_mul(real_t, cos_b) + right_mul(imag_t, sin_b)
    imag_f = right_mul(imag_t, cos_b) - right_mul(real_t, sin_b)
    return (real_f, imag_f)


def inverse(real_f, imag_f, tables):
    (cos_a, sin_a), (cos_b, sin_b), (cos_t, sin_t), size_a, size_b = tables
    half_a = size_a // 2
    real_z = right_mul(real_f, cos_b) - right_mul(imag_f, sin_b)
    imag_z = right_mul(imag_f, cos_b) + right_mul(real_f, sin_b)
    real_w = real_z * cos_t - imag_z * sin_t
    imag_w = imag_z * cos_t + real_z * sin_t
    out_half = jnp.einsum("nk,ckb->cnb", cos_a[:half_a, :], real_w, precision=TRIPLE) - jnp.einsum(
        "nk,ckb->cnb", sin_a[:half_a, :], imag_w, precision=TRIPLE
    )
    return out_half.reshape(out_half.shape[0], half_a * size_b) * (1.0 / (size_a * size_b))


def long_mix(gated_kv, spectrum, own_gain, tables):
    kv_values = gated_kv.astype(jnp.float32)
    real_u, imag_u = forward(kv_values, tables)
    real_h, imag_h = spectrum
    real_p = real_u * real_h - imag_u * imag_h
    imag_p = real_u * imag_h + imag_u * real_h
    convolved = inverse(real_p, imag_p, tables)
    return (convolved + own_gain[:, None] * kv_values).astype(jnp.bfloat16)


def featurize(extended, weights, length):
    tap_count = weights.shape[1]
    running = jnp.zeros(extended.shape[:2] + (length,), jnp.float32)
    for lag_idx in range(tap_count):
        offset = tap_count - 1 - lag_idx
        running = running + weights[:, lag_idx, :, None] * extended[
            :, :, offset : offset + length
        ].astype(jnp.float32)
    return running.astype(jnp.bfloat16)


def multiply_round(left_arr, right_arr):
    return (left_arr.astype(jnp.float32) * right_arr.astype(jnp.float32)).astype(jnp.bfloat16)


def local(projected, feat_weight, long_filter, skip_gain, out_values, out_scales):
    if fits(projected, long_filter, out_values):
        return fused(projected, feat_weight, long_filter, skip_gain, out_values, out_scales)
    groups = lax.axis_size("seq")
    tok_rows = projected.shape[1]
    local_ch = projected.shape[2]
    length = tok_rows * groups
    tables = make_tables(length)
    spectrum = forward(long_filter, tables)
    columns = jnp.transpose(projected, (0, 2, 1))
    rim_width = KS - 1
    prior_rows = passed_along(columns[:, :, tok_rows - rim_width :], "seq", 1)
    featured = featurize(jnp.concatenate([prior_rows, columns], axis=2), feat_weight, tok_rows)
    regrouped = lax.all_to_all(featured, "seq", split_axis=1, concat_axis=2, tiled=True)
    gated_kv = multiply_round(regrouped[1], regrouped[2])
    filtered = long_mix(gated_kv, spectrum, skip_gain, tables)
    gated = multiply_round(regrouped[0], filtered)
    gated_home = lax.all_to_all(gated, "seq", split_axis=1, concat_axis=0, tiled=True)
    block_count = local_ch // BLK
    out_width = out_values.shape[1]
    stacked = gated_home.reshape(block_count, BLK, tok_rows)
    weight_blocks = out_values.reshape(block_count, BLK, out_width)
    scale_cols = jnp.repeat(out_scales, BLK, axis=1)
    products = jnp.einsum(
        "bkn,bkt->bnt", weight_blocks, stacked, preferred_element_type=jnp.float32
    )
    summed = lax.psum_scatter(
        jnp.sum(products * scale_cols[:, :, None], axis=0).astype(jnp.bfloat16),
        "tensor",
        scatter_dimension=0,
        tiled=True,
    )
    return jnp.transpose(summed, (1, 0))


def solution(mesh):
    return jax.shard_map(
        local,
        mesh=mesh,
        in_specs=(
            P(None, "seq", "tensor"),
            P(None, None, "tensor"),
            P(("tensor", "seq"), None),
            P(("tensor", "seq")),
            P("tensor", None),
            P("tensor", None),
        ),
        out_specs=P("seq", "tensor"),
        check_vma=False,
    )
```

```python
import functools
import math

import jax
import jax.numpy as jnp
import ml_dtypes
import numpy as np
from jax import lax
from jax.experimental import pallas as pl
from jax.experimental.pallas import tpu as pltpu
from jax.sharding import PartitionSpec as P

KS = 7
BLK = 128
LANES = 128
RIM = 16
SUB = 16
CHUNK = 64
MESH_ID = pl.DeviceIdType.MESH
BF16 = jnp.bfloat16
F32 = jnp.float32


def dft_tables(groups, rows):
    whole = 2 * groups * rows
    evens = np.arange(0, groups + 1, 2)
    odds = np.arange(1, groups + 1, 2)
    slots = len(evens) + len(evens) % 2
    k_a = np.zeros((2 * slots,), np.int64)
    weight = np.zeros((2 * slots,))
    for base, kept in ((0, evens), (slots, odds)):
        k_a[base : base + len(kept)] = kept
        weight[base : base + len(kept)] = np.where(kept % groups == 0, 1.0, 2.0) / whole
    n_a = np.arange(groups)
    r = np.arange(rows)
    turns = k_a[:, None, None] * (n_a[None, :, None] * rows + r[None, None, :]) % whole
    angles = turns * (2.0 * np.pi / whole)
    parts = np.stack([np.cos(angles), -np.sin(angles)], axis=1)
    parts = parts * (weight > 0)[:, None, None, None]
    blocks = parts.reshape(2 * slots, 2, groups, rows // SUB, SUB)
    first = np.zeros((rows // SUB, 2 * slots, 2, SUB, groups, SUB))
    last = np.zeros((rows // SUB, groups, SUB, 2 * slots, 2, SUB))
    for lo in range(SUB):
        cut = blocks[:, :, :, :, lo]
        first[:, :, :, lo, :, lo] = cut.transpose(3, 0, 1, 2)
        last[:, :, lo, :, :, lo] = (cut * weight[:, None, None, None]).transpose(3, 2, 0, 1)
    first = first.reshape(rows // SUB, 4 * slots * SUB, groups * SUB)
    last = last.reshape(rows // SUB, groups * SUB, 4 * slots * SUB)
    inner = (r[:, None] * r[None, :] % rows) * (2.0 * np.pi / rows)
    cos, sin = np.cos(inner), np.sin(inner)
    ahead = np.block([[cos, sin], [-sin, cos]])
    back = np.block([[cos, -sin], [sin, cos]])
    return [x.astype(ml_dtypes.bfloat16) for x in (first, ahead, back, last)]


def dot(a, b):
    return jnp.dot(a, b, preferred_element_type=F32)


def swapped(x):
    return pltpu.roll(x, LANES // 2, 1)


def side_by_side(left, right):
    low = lax.broadcasted_iota(jnp.int32, left.shape, 1) < LANES // 2
    return jnp.where(low, left, right)


def fused_kernel(
    groups,
    rows,
    proj,
    taps,
    filt,
    gain,
    weights,
    scales,
    t_first,
    t_ahead,
    t_back,
    t_last,
    out,
    pb,
    g_out,
    u_in,
    u_wide,
    v_out,
    f_in,
    feat_q,
    fl,
    ft,
    x1,
    xz,
    spec,
    m_first,
    m_ahead,
    m_back,
    m_last,
    w,
    gated,
    part_own,
    part_out,
    part_in,
    loc_sem,
    halo_sem,
    send_sem,
    recv_sem,
    recv_p,
):
    me = lax.axis_index("seq")
    mine = lax.axis_index("tensor")
    other = 1 - mine
    packed = rows // 2
    part = CHUNK // 2
    chunks = packed // part
    half = part_own.shape[2]

    load_in = pltpu.make_async_copy(proj, pb.at[:, pl.ds(RIM, rows)], loc_sem.at[0])
    load_in.start()

    def partner(mask):
        total = 0
        bit = 1
        while bit < groups:
            mixed = lax.rem(me // bit, 2) + lax.rem(mask // bit, 2)
            total = total + bit * lax.rem(mixed, 2)
            bit *= 2
        return total

    barrier = pltpu.get_barrier_semaphore()

    @pl.loop(1, groups)
    def _(step):
        pl.semaphore_signal(
            barrier, inc=1, device_id=(partner(step), mine), device_id_type=MESH_ID
        )

    pl.semaphore_signal(barrier, inc=1, device_id=(me, other), device_id_type=MESH_ID)
    pl.semaphore_wait(barrier, groups)

    def halo(first, count, slot):
        return pltpu.make_async_remote_copy(
            src_ref=proj.at[pl.ds(first, count), pl.ds(rows - RIM, RIM)],
            dst_ref=pb.at[pl.ds(first, count), pl.ds(0, RIM)],
            send_sem=halo_sem.at[slot],
            recv_sem=halo_sem.at[slot + 1],
            device_id=(lax.rem(me + 1, groups), mine),
            device_id_type=MESH_ID,
        )

    halo_kv, halo_q = halo(1, 2, 0), halo(0, 1, 2)

    @pl.when(me < groups - 1)
    def _():
        halo_kv.start()

    @pl.when(me == 0)
    def _():
        pb[:, 0:RIM, :] = jnp.zeros((pb.shape[0], RIM, pb.shape[2]), BF16)

    load_in.wait()
    loads = [
        pltpu.make_async_copy(src, dst, loc_sem.at[1 + i])
        for i, (src, dst) in enumerate(
            (
                (filt, fl),
                (t_first, m_first),
                (t_ahead, m_ahead),
                (t_back, m_back),
                (t_last, m_last),
                (weights, w),
            )
        )
    ]
    for load in loads:
        load.start()

    def featured(p, start, j):
        lanes = pl.ds(pl.multiple_of(j * LANES, LANES), LANES)
        x = pb[p, pl.ds(pl.multiple_of(start, part), part + RIM), lanes].astype(F32)
        run = None
        for lag in range(KS):
            term = taps[p, lag : lag + 1, lanes] * x[RIM - lag : RIM - lag + part]
            run = term if run is None else run + term
        return run.astype(BF16)

    def span(start, count):
        return pl.ds(pl.multiple_of(start, count), count)

    first_slot = (0, chunks, 2 * chunks, 3 * chunks)

    def spread(src, dst, side, q, count):
        at = span(q * count, count)

        @pl.loop(1, groups)
        def _(step):
            peer = partner(groups - step)
            pltpu.make_async_remote_copy(
                src_ref=src.at[side % 2, peer, at],
                dst_ref=dst.at[side % 2, me, at],
                send_sem=send_sem.at[side],
                recv_sem=recv_sem.at[first_slot[side] + q],
                device_id=(peer, mine),
                device_id_type=MESH_ID,
            ).start()

        dst[side % 2, me, at, :] = src[side % 2, me, at, :]

    def await_chunk(dst, side, q, count):
        view = dst.at[side % 2, pl.ds(0, groups - 1), span(q * count, count)]
        pltpu.make_async_copy(view, view, recv_sem.at[first_slot[side] + q]).wait()

    def feature_chunk(q):
        at = span(q * part, part)

        @pl.loop(0, groups)
        def _(j):
            def product(start):
                k = featured(1, start, j).astype(F32)
                return k * featured(2, start, j).astype(F32)

            early, late = product(q * part), product(packed + q * part)
            g_out[0, j, at, :] = side_by_side(early, swapped(late)).astype(BF16)
            g_out[1, j, at, :] = side_by_side(swapped(early), late).astype(BF16)

        spread(g_out, u_in, 0, q, part)

    @pl.loop(1, chunks)
    def _(q):
        feature_chunk(q)

    @pl.when(me > 0)
    def _():
        halo_kv.wait_recv()

    feature_chunk(0)
    wide = packed // 2

    @pl.loop(0, 2)
    def _(q):
        spread(g_out, u_in, 1, q, wide)

    @pl.when(me < groups - 1)
    def _():
        halo_q.start()

    loads[0].wait()

    @pl.loop(0, groups)
    def _(a):
        for piece in range(rows // LANES):
            start = pl.multiple_of(a * rows + piece * LANES, LANES)
            at = slice(piece * LANES, (piece + 1) * LANES)
            ft[a, at, :] = fl[:, pl.ds(start, LANES)].T.astype(BF16)

    for load in loads[1:5]:
        load.wait()

    slabs = xz.shape[0]
    half_slabs = slabs // 2
    fours = half_slabs // 4

    def first_stage(src, s):
        block = src[:, span(s * SUB, SUB), :].reshape(groups * SUB, LANES)
        found = dot(m_first[s], block)
        return found[: half_slabs * SUB], found[half_slabs * SUB :]

    def pack(side, even, odd):
        if side == 0:
            both = side_by_side(even, swapped(odd))
        else:
            both = side_by_side(swapped(even), odd)
        return both.astype(BF16).reshape(half_slabs, SUB, LANES)

    def four_of(src, j):
        left = src[pl.ds(4 * j, 2)].reshape(2 * rows, LANES)
        right = src[pl.ds(4 * j + 2, 2)].reshape(2 * rows, LANES)
        return jnp.concatenate([left, right], axis=1)

    @pl.loop(0, rows // SUB)
    def _(s):
        even, odd = first_stage(ft, s)
        x1[:, span(s * SUB, SUB), :] = pack(0, even, odd)
        xz[0:half_slabs, span(s * SUB, SUB), :] = pack(1, even, odd)

    @pl.loop(0, fours)
    def _(j):
        spec[0, j] = dot(m_ahead[...], four_of(x1, j))
        spec[1, j] = dot(m_ahead[...], four_of(xz, j))

    def convolve(side, count, back):
        @pl.loop(0, packed // count)
        def _(i):
            q = lax.rem(i + 1, packed // count)
            await_chunk(u_in, side, q, count)
            at = span(q * count, count)
            held = u_in[side, :, at, :].reshape(groups * count, LANES)
            turned = swapped(held.astype(F32)).astype(BF16)
            early, late = (held, turned) if side == 0 else (turned, held)
            u_wide[:, at, :] = early.reshape(groups, count, LANES)
            u_wide[:, span(packed + q * count, count), :] = late.reshape(groups, count, LANES)

            @pl.loop(0, count // SUB)
            def _(c):
                for base in (0, packed // SUB):
                    s = base + q * (count // SUB) + c
                    x1[:, span(s * SUB, SUB), :] = pack(side, *first_stage(u_wide, s))

        @pl.loop(0, fours)
        def _(j):
            values = dot(m_ahead[...], four_of(x1, j))
            re_u, im_u = values[:rows], values[rows:]
            re_h, im_h = spec[side, j, 0:rows, :], spec[side, j, rows : 2 * rows, :]
            product = jnp.concatenate(
                [re_u * re_h - im_u * im_h, re_u * im_h + im_u * re_h], axis=0
            ).astype(BF16)
            z = dot(m_back[...], product)
            for piece in range(2):
                held = z[:, piece * LANES : (piece + 1) * LANES]
                turned = swapped(held)
                even, odd = (held, turned) if side == 0 else (turned, held)
                at = 4 * j + 2 * piece
                xz[pl.ds(at, 2)] = even.astype(BF16).reshape(2, rows, LANES)
                xz[pl.ds(half_slabs + at, 2)] = odd.astype(BF16).reshape(2, rows, LANES)

        def filtered(s):
            at = span(s * SUB, SUB)
            conv = dot(m_last[s], xz[:, at, :].reshape(slabs * SUB, LANES))
            direct = gain[...] * u_wide[:, at, :].reshape(groups * SUB, LANES).astype(F32)
            return conv + direct

        @pl.loop(0, packed // back)
        def _(q):
            @pl.loop(0, back // SUB)
            def _(c):
                s = q * (back // SUB) + c
                early, late = filtered(s), filtered(packed // SUB + s)
                if side == 0:
                    both = side_by_side(early, swapped(late))
                else:
                    both = side_by_side(swapped(early), late)
                v_out[side, :, span(s * SUB, SUB), :] = both.astype(BF16).reshape(
                    groups, SUB, LANES
                )

            spread(v_out, f_in, 2 + side, q, back)

    convolve(0, part, wide)
    convolve(1, wide, part)

    loads[5].wait()

    @pl.loop(0, w.shape[0] // BLK)
    def _(b):
        at = span(b * BLK, BLK)
        for n in range(w.shape[1] // BLK):
            cols = slice(n * BLK, (n + 1) * BLK)
            w[at, cols] = (w[at, cols].astype(F32) * scales[b, n]).astype(BF16)

    @pl.when(me > 0)
    def _():
        halo_q.wait_recv()

    @pl.loop(0, rows // part)
    def _(q):
        @pl.loop(0, groups)
        def _(j):
            feat_q[j, span(q * part, part), :] = featured(0, q * part, j)

    def swap(q):
        return pltpu.make_async_remote_copy(
            src_ref=part_out.at[q],
            dst_ref=part_in.at[q],
            send_sem=send_sem.at[4],
            recv_sem=recv_p.at[q],
            device_id=(me, other),
            device_id_type=MESH_ID,
        )

    for q in range(packed // wide):
        await_chunk(f_in, 2, q, wide)

    @pl.loop(0, chunks)
    def _(q):
        await_chunk(f_in, 3, q, part)
        at, later = span(q * part, part), span(packed + q * part, part)
        for j in range(groups):
            lanes = slice(j * LANES, (j + 1) * LANES)
            low, high = f_in[0, j, at, :].astype(F32), f_in[1, j, at, :].astype(F32)
            early = side_by_side(low, swapped(high)) * feat_q[j, at, :].astype(F32)
            late = side_by_side(swapped(low), high) * feat_q[j, later, :].astype(F32)
            gated[0:part, lanes] = early.astype(BF16)
            gated[part : 2 * part, lanes] = late.astype(BF16)
        part_out[q] = dot(gated[...], w[:, span(other * half, half)]).astype(BF16)
        swap(q).start()
        part_own[q] = dot(gated[...], w[:, span(mine * half, half)]).astype(BF16)

    @pl.loop(0, chunks)
    def _(q):
        swap(q).wait_recv()
        total = (part_own[q].astype(F32) + part_in[q].astype(F32)).astype(BF16)
        out[span(q * part, part), :] = total[:part]
        out[span(packed + q * part, part), :] = total[part:]

    @pl.when(me < groups - 1)
    def _():
        halo_kv.wait_send()
        halo_q.wait_send()

    for side in range(4):
        sent = (g_out if side < 2 else v_out).at[side % 2, pl.ds(0, groups - 1)]
        pltpu.make_async_copy(sent, sent, send_sem.at[side]).wait()
    pltpu.make_async_copy(part_out, part_out, send_sem.at[4]).wait()


def fused(projected, feat_weight, long_filter, skip_gain, out_values, out_scales):
    groups = lax.axis_size("seq")
    rows, local_ch = projected.shape[1:]
    out_width = out_values.shape[1]
    half = out_width // 2
    tables = dft_tables(groups, rows)
    slabs = tables[0].shape[1] // SUB
    hbm = pl.BlockSpec(memory_space=pl.ANY)
    vmem = pl.BlockSpec(memory_space=pltpu.VMEM)
    smem = pl.BlockSpec(memory_space=pltpu.SMEM)
    block = pltpu.VMEM((groups, rows, LANES), BF16)
    halves = pltpu.VMEM((2, groups, rows // 2, LANES), BF16)
    chunks = rows // CHUNK
    return pl.pallas_call(
        functools.partial(fused_kernel, groups, rows),
        out_shape=jax.ShapeDtypeStruct((rows, half), BF16),
        in_specs=[hbm, vmem, hbm, vmem, hbm, smem, hbm, hbm, hbm, hbm],
        out_specs=vmem,
        scratch_shapes=[
            pltpu.VMEM((3, RIM + rows, local_ch), BF16),
            halves,
            halves,
            block,
            halves,
            halves,
            block,
            pltpu.VMEM(long_filter.shape, F32),
            block,
            pltpu.VMEM((slabs // 2, rows, LANES), BF16),
            pltpu.VMEM((slabs, rows, LANES), BF16),
            pltpu.VMEM((2, slabs // 8, 2 * rows, 2 * LANES), F32),
            pltpu.VMEM(tables[0].shape, BF16),
            pltpu.VMEM(tables[1].shape, BF16),
            pltpu.VMEM(tables[2].shape, BF16),
            pltpu.VMEM(tables[3].shape, BF16),
            pltpu.VMEM(out_values.shape, BF16),
            pltpu.VMEM((CHUNK, local_ch), BF16),
            pltpu.VMEM((chunks, CHUNK, half), BF16),
            pltpu.VMEM((chunks, CHUNK, half), BF16),
            pltpu.VMEM((chunks, CHUNK, half), BF16),
            pltpu.SemaphoreType.DMA((7,)),
            pltpu.SemaphoreType.DMA((4,)),
            pltpu.SemaphoreType.DMA((5,)),
            pltpu.SemaphoreType.DMA((4 * chunks,)),
            pltpu.SemaphoreType.DMA((chunks,)),
        ],
        compiler_params=pltpu.CompilerParams(
            collective_id=0, has_side_effects=True, vmem_limit_bytes=58 * 2**20
        ),
        cost_estimate=pl.CostEstimate(
            flops=10 * 10**9, bytes_accessed=32 * 2**20, transcendentals=0
        ),
    )(
        projected,
        feat_weight,
        long_filter,
        skip_gain.reshape(1, -1),
        out_values,
        out_scales,
        *[jnp.asarray(x) for x in tables],
    )


def fits(projected, long_filter, out_values):
    groups = lax.axis_size("seq")
    rows, local_ch = projected.shape[1:]
    return (
        lax.axis_size("tensor") == 2
        and long_filter.shape[0] == LANES
        and local_ch == groups * LANES
        and rows == 2 * LANES
        and groups == SUB
        and out_values.shape[1] % (2 * LANES) == 0
    )


TRIPLE = lax.Precision.HIGH


def passed_along(x, axis, by):
    size = lax.axis_size(axis)
    pairs = [(i, i + by) for i in range(size) if 0 <= i + by < size]
    return lax.ppermute(x, axis, pairs)


def split_length(whole):
    for candidate in range(2, whole + 1, 2):
        if whole % candidate == 0 and candidate * candidate >= whole:
            return (candidate, whole // candidate)
    return (whole, 1)


def angle_pair(row_count, col_count, period):
    row_ids = lax.broadcasted_iota(jnp.int32, (row_count, col_count), 0)
    col_ids = lax.broadcasted_iota(jnp.int32, (row_count, col_count), 1)
    angles = (row_ids * col_ids % period).astype(jnp.float32) * (2.0 * math.pi / period)
    return (jnp.cos(angles), jnp.sin(angles))


def make_tables(length):
    whole = 2 * length
    size_a, size_b = split_length(whole)
    return (
        angle_pair(size_a, size_a, size_a),
        angle_pair(size_b, size_b, size_b),
        angle_pair(size_a, size_b, whole),
        size_a,
        size_b,
    )


def right_mul(signal, matrix):
    return jnp.einsum("ckn,nm->ckm", signal, matrix, precision=TRIPLE)


def forward(signal, tables):
    (cos_a, sin_a), (cos_b, sin_b), (cos_t, sin_t), size_a, size_b = tables
    half_a = size_a // 2
    blocks = signal.reshape(signal.shape[0], half_a, size_b)
    real_a = jnp.einsum("kn,cnb->ckb", cos_a[:, :half_a], blocks, precision=TRIPLE)
    imag_a = -jnp.einsum("kn,cnb->ckb", sin_a[:, :half_a], blocks, precision=TRIPLE)
    real_t = real_a * cos_t + imag_a * sin_t
    imag_t = imag_a * cos_t - real_a * sin_t
    real_f = right_mul(real_t, cos_b) + right_mul(imag_t, sin_b)
    imag_f = right_mul(imag_t, cos_b) - right_mul(real_t, sin_b)
    return (real_f, imag_f)


def inverse(real_f, imag_f, tables):
    (cos_a, sin_a), (cos_b, sin_b), (cos_t, sin_t), size_a, size_b = tables
    half_a = size_a // 2
    real_z = right_mul(real_f, cos_b) - right_mul(imag_f, sin_b)
    imag_z = right_mul(imag_f, cos_b) + right_mul(real_f, sin_b)
    real_w = real_z * cos_t - imag_z * sin_t
    imag_w = imag_z * cos_t + real_z * sin_t
    out_half = jnp.einsum("nk,ckb->cnb", cos_a[:half_a, :], real_w, precision=TRIPLE) - jnp.einsum(
        "nk,ckb->cnb", sin_a[:half_a, :], imag_w, precision=TRIPLE
    )
    return out_half.reshape(out_half.shape[0], half_a * size_b) * (1.0 / (size_a * size_b))


def long_mix(gated_kv, spectrum, own_gain, tables):
    kv_values = gated_kv.astype(jnp.float32)
    real_u, imag_u = forward(kv_values, tables)
    real_h, imag_h = spectrum
    real_p = real_u * real_h - imag_u * imag_h
    imag_p = real_u * imag_h + imag_u * real_h
    convolved = inverse(real_p, imag_p, tables)
    return (convolved + own_gain[:, None] * kv_values).astype(jnp.bfloat16)


def featurize(extended, weights, length):
    tap_count = weights.shape[1]
    running = jnp.zeros(extended.shape[:2] + (length,), jnp.float32)
    for lag_idx in range(tap_count):
        offset = tap_count - 1 - lag_idx
        running = running + weights[:, lag_idx, :, None] * extended[
            :, :, offset : offset + length
        ].astype(jnp.float32)
    return running.astype(jnp.bfloat16)


def multiply_round(left_arr, right_arr):
    return (left_arr.astype(jnp.float32) * right_arr.astype(jnp.float32)).astype(jnp.bfloat16)


def local(projected, feat_weight, long_filter, skip_gain, out_values, out_scales):
    if fits(projected, long_filter, out_values):
        return fused(projected, feat_weight, long_filter, skip_gain, out_values, out_scales)
    groups = lax.axis_size("seq")
    tok_rows = projected.shape[1]
    local_ch = projected.shape[2]
    length = tok_rows * groups
    tables = make_tables(length)
    spectrum = forward(long_filter, tables)
    columns = jnp.transpose(projected, (0, 2, 1))
    rim_width = KS - 1
    prior_rows = passed_along(columns[:, :, tok_rows - rim_width :], "seq", 1)
    featured = featurize(jnp.concatenate([prior_rows, columns], axis=2), feat_weight, tok_rows)
    regrouped = lax.all_to_all(featured, "seq", split_axis=1, concat_axis=2, tiled=True)
    gated_kv = multiply_round(regrouped[1], regrouped[2])
    filtered = long_mix(gated_kv, spectrum, skip_gain, tables)
    gated = multiply_round(regrouped[0], filtered)
    gated_home = lax.all_to_all(gated, "seq", split_axis=1, concat_axis=0, tiled=True)
    block_count = local_ch // BLK
    out_width = out_values.shape[1]
    stacked = gated_home.reshape(block_count, BLK, tok_rows)
    weight_blocks = out_values.reshape(block_count, BLK, out_width)
    scale_cols = jnp.repeat(out_scales, BLK, axis=1)
    products = jnp.einsum(
        "bkn,bkt->bnt", weight_blocks, stacked, preferred_element_type=jnp.float32
    )
    summed = lax.psum_scatter(
        jnp.sum(products * scale_cols[:, :, None], axis=0).astype(jnp.bfloat16),
        "tensor",
        scatter_dimension=0,
        tiled=True,
    )
    return jnp.transpose(summed, (1, 0))


def solution(mesh):
    return jax.shard_map(
        local,
        mesh=mesh,
        in_specs=(
            P(None, "seq", "tensor"),
            P(None, None, "tensor"),
            P(("tensor", "seq"), None),
            P(("tensor", "seq")),
            P("tensor", None),
            P("tensor", None),
        ),
        out_specs=P("seq", "tensor"),
        check_vma=False,
    )
```

```python
import functools
import math

import jax
import jax.numpy as jnp
import ml_dtypes
import numpy as np
from jax import lax
from jax.experimental import pallas as pl
from jax.experimental.pallas import tpu as pltpu
from jax.sharding import PartitionSpec as P

KS = 7
BLK = 128
LANES = 128
RIM = 16
SUB = 16
CHUNK = 64
MESH_ID = pl.DeviceIdType.MESH
BF16 = jnp.bfloat16
F32 = jnp.float32


def dft_tables(groups, rows):
    whole = 2 * groups * rows
    evens = np.arange(0, groups + 1, 2)
    odds = np.arange(1, groups + 1, 2)
    slots = len(evens) + len(evens) % 2
    k_a = np.zeros((2 * slots,), np.int64)
    weight = np.zeros((2 * slots,))
    for base, kept in ((0, evens), (slots, odds)):
        k_a[base : base + len(kept)] = kept
        weight[base : base + len(kept)] = np.where(kept % groups == 0, 1.0, 2.0) / whole
    n_a = np.arange(groups)
    r = np.arange(rows)
    turns = k_a[:, None, None] * (n_a[None, :, None] * rows + r[None, None, :]) % whole
    angles = turns * (2.0 * np.pi / whole)
    parts = np.stack([np.cos(angles), -np.sin(angles)], axis=1)
    parts = parts * (weight > 0)[:, None, None, None]
    blocks = parts.reshape(2 * slots, 2, groups, rows // SUB, SUB)
    first = np.zeros((rows // SUB, 2 * slots, 2, SUB, groups, SUB))
    last = np.zeros((rows // SUB, groups, SUB, 2 * slots, 2, SUB))
    for lo in range(SUB):
        cut = blocks[:, :, :, :, lo]
        first[:, :, :, lo, :, lo] = cut.transpose(3, 0, 1, 2)
        last[:, :, lo, :, :, lo] = (cut * weight[:, None, None, None]).transpose(3, 2, 0, 1)
    first = first.reshape(rows // SUB, 4 * slots * SUB, groups * SUB)
    last = last.reshape(rows // SUB, groups * SUB, 4 * slots * SUB)
    inner = (r[:, None] * r[None, :] % rows) * (2.0 * np.pi / rows)
    cos, sin = np.cos(inner), np.sin(inner)
    ahead = np.block([[cos, sin], [-sin, cos]])
    back = np.block([[cos, -sin], [sin, cos]])
    return [x.astype(ml_dtypes.bfloat16) for x in (first, ahead, back, last)]


def dot(a, b):
    return jnp.dot(a, b, preferred_element_type=F32)


def swapped(x):
    return pltpu.roll(x, LANES // 2, 1)


def side_by_side(left, right):
    low = lax.broadcasted_iota(jnp.int32, left.shape, 1) < LANES // 2
    return jnp.where(low, left, right)


def fused_kernel(
    groups,
    rows,
    proj,
    taps,
    filt,
    gain,
    weights,
    scales,
    t_first,
    t_ahead,
    t_back,
    t_last,
    out,
    pb,
    g_out,
    u_in,
    u_wide,
    v_out,
    f_in,
    feat_q,
    fl,
    ft,
    x1,
    xz,
    spec,
    m_first,
    m_ahead,
    m_back,
    m_last,
    w,
    gated,
    part_own,
    part_out,
    part_in,
    loc_sem,
    halo_sem,
    send_sem,
    recv_sem,
    recv_p,
):
    me = lax.axis_index("seq")
    mine = lax.axis_index("tensor")
    other = 1 - mine
    packed = rows // 2
    part = CHUNK // 2
    chunks = packed // part
    half = part_own.shape[2]

    load_in = pltpu.make_async_copy(proj, pb.at[:, pl.ds(RIM, rows)], loc_sem.at[0])
    load_in.start()

    def partner(mask):
        total = 0
        bit = 1
        while bit < groups:
            mixed = lax.rem(me // bit, 2) + lax.rem(mask // bit, 2)
            total = total + bit * lax.rem(mixed, 2)
            bit *= 2
        return total

    barrier = pltpu.get_barrier_semaphore()

    @pl.loop(1, groups)
    def _(step):
        pl.semaphore_signal(
            barrier, inc=1, device_id=(partner(step), mine), device_id_type=MESH_ID
        )

    pl.semaphore_signal(barrier, inc=1, device_id=(me, other), device_id_type=MESH_ID)
    pl.semaphore_wait(barrier, groups)

    def halo(first, count, slot):
        return pltpu.make_async_remote_copy(
            src_ref=proj.at[pl.ds(first, count), pl.ds(rows - RIM, RIM)],
            dst_ref=pb.at[pl.ds(first, count), pl.ds(0, RIM)],
            send_sem=halo_sem.at[slot],
            recv_sem=halo_sem.at[slot + 1],
            device_id=(lax.rem(me + 1, groups), mine),
            device_id_type=MESH_ID,
        )

    halo_kv, halo_q = halo(1, 2, 0), halo(0, 1, 2)

    @pl.when(me < groups - 1)
    def _():
        halo_kv.start()

    @pl.when(me == 0)
    def _():
        pb[:, 0:RIM, :] = jnp.zeros((pb.shape[0], RIM, pb.shape[2]), BF16)

    load_in.wait()
    loads = [
        pltpu.make_async_copy(src, dst, loc_sem.at[1 + i])
        for i, (src, dst) in enumerate(
            (
                (filt, fl),
                (t_first, m_first),
                (t_ahead, m_ahead),
                (t_back, m_back),
                (t_last, m_last),
                (weights, w),
            )
        )
    ]
    for load in loads:
        load.start()

    def featured(p, start, j):
        lanes = pl.ds(pl.multiple_of(j * LANES, LANES), LANES)
        x = pb[p, pl.ds(pl.multiple_of(start, part), part + RIM), lanes].astype(F32)
        run = None
        for lag in range(KS):
            term = taps[p, lag : lag + 1, lanes] * x[RIM - lag : RIM - lag + part]
            run = term if run is None else run + term
        return run.astype(BF16)

    def span(start, count):
        return pl.ds(pl.multiple_of(start, count), count)

    first_slot = (0, chunks, 2 * chunks, 3 * chunks)

    def spread(src, dst, side, q, count):
        at = span(q * count, count)

        @pl.loop(1, groups)
        def _(step):
            peer = partner(groups - step)
            pltpu.make_async_remote_copy(
                src_ref=src.at[side % 2, peer, at],
                dst_ref=dst.at[side % 2, me, at],
                send_sem=send_sem.at[side],
                recv_sem=recv_sem.at[first_slot[side] + q],
                device_id=(peer, mine),
                device_id_type=MESH_ID,
            ).start()

        dst[side % 2, me, at, :] = src[side % 2, me, at, :]

    def await_chunk(dst, side, q, count):
        view = dst.at[side % 2, pl.ds(0, groups - 1), span(q * count, count)]
        pltpu.make_async_copy(view, view, recv_sem.at[first_slot[side] + q]).wait()

    def feature_chunk(q):
        at = span(q * part, part)

        @pl.loop(0, groups)
        def _(j):
            def product(start):
                k = featured(1, start, j).astype(F32)
                return k * featured(2, start, j).astype(F32)

            early, late = product(q * part), product(packed + q * part)
            g_out[0, j, at, :] = side_by_side(early, swapped(late)).astype(BF16)
            g_out[1, j, at, :] = side_by_side(swapped(early), late).astype(BF16)

        spread(g_out, u_in, 0, q, part)

    @pl.loop(1, chunks)
    def _(q):
        feature_chunk(q)

    @pl.when(me > 0)
    def _():
        halo_kv.wait_recv()

    feature_chunk(0)
    wide = packed // 2

    @pl.loop(0, 2)
    def _(q):
        spread(g_out, u_in, 1, q, wide)

    @pl.when(me < groups - 1)
    def _():
        halo_q.start()

    loads[0].wait()

    @pl.loop(0, groups, unroll=4)
    def _(a):
        for piece in range(rows // LANES):
            start = pl.multiple_of(a * rows + piece * LANES, LANES)
            at = slice(piece * LANES, (piece + 1) * LANES)
            ft[a, at, :] = fl[:, pl.ds(start, LANES)].T.astype(BF16)

    for load in loads[1:5]:
        load.wait()

    slabs = xz.shape[0]
    half_slabs = slabs // 2
    fours = half_slabs // 4

    def first_stage(src, s):
        block = src[:, span(s * SUB, SUB), :].reshape(groups * SUB, LANES)
        found = dot(m_first[s], block)
        return found[: half_slabs * SUB], found[half_slabs * SUB :]

    def pack(side, even, odd):
        if side == 0:
            both = side_by_side(even, swapped(odd))
        else:
            both = side_by_side(swapped(even), odd)
        return both.astype(BF16).reshape(half_slabs, SUB, LANES)

    def four_of(src, j):
        left = src[pl.ds(4 * j, 2)].reshape(2 * rows, LANES)
        right = src[pl.ds(4 * j + 2, 2)].reshape(2 * rows, LANES)
        return jnp.concatenate([left, right], axis=1)

    @pl.loop(0, rows // SUB, unroll=4)
    def _(s):
        even, odd = first_stage(ft, s)
        x1[:, span(s * SUB, SUB), :] = pack(0, even, odd)
        xz[0:half_slabs, span(s * SUB, SUB), :] = pack(1, even, odd)

    for j in range(fours):
        spec[0, j] = dot(m_ahead[...], four_of(x1, j))
        spec[1, j] = dot(m_ahead[...], four_of(xz, j))

    def convolve(side, count, back):
        @pl.loop(0, packed // count)
        def _(i):
            q = lax.rem(i + 1, packed // count)
            await_chunk(u_in, side, q, count)
            at = span(q * count, count)
            held = u_in[side, :, at, :].reshape(groups * count, LANES)
            turned = swapped(held.astype(F32)).astype(BF16)
            early, late = (held, turned) if side == 0 else (turned, held)
            u_wide[:, at, :] = early.reshape(groups, count, LANES)
            u_wide[:, span(packed + q * count, count), :] = late.reshape(groups, count, LANES)

            @pl.loop(0, count // SUB, unroll=2)
            def _(c):
                for base in (0, packed // SUB):
                    s = base + q * (count // SUB) + c
                    x1[:, span(s * SUB, SUB), :] = pack(side, *first_stage(u_wide, s))

        for j in range(fours):
            values = dot(m_ahead[...], four_of(x1, j))
            re_u, im_u = values[:rows], values[rows:]
            re_h, im_h = spec[side, j, 0:rows, :], spec[side, j, rows : 2 * rows, :]
            product = jnp.concatenate(
                [re_u * re_h - im_u * im_h, re_u * im_h + im_u * re_h], axis=0
            ).astype(BF16)
            z = dot(m_back[...], product)
            for piece in range(2):
                held = z[:, piece * LANES : (piece + 1) * LANES]
                turned = swapped(held)
                even, odd = (held, turned) if side == 0 else (turned, held)
                at = 4 * j + 2 * piece
                xz[pl.ds(at, 2)] = even.astype(BF16).reshape(2, rows, LANES)
                xz[pl.ds(half_slabs + at, 2)] = odd.astype(BF16).reshape(2, rows, LANES)

        def filtered(s):
            at = span(s * SUB, SUB)
            conv = dot(m_last[s], xz[:, at, :].reshape(slabs * SUB, LANES))
            direct = gain[...] * u_wide[:, at, :].reshape(groups * SUB, LANES).astype(F32)
            return conv + direct

        @pl.loop(0, packed // back)
        def _(q):
            @pl.loop(0, back // SUB, unroll=2)
            def _(c):
                s = q * (back // SUB) + c
                early, late = filtered(s), filtered(packed // SUB + s)
                if side == 0:
                    both = side_by_side(early, swapped(late))
                else:
                    both = side_by_side(swapped(early), late)
                v_out[side, :, span(s * SUB, SUB), :] = both.astype(BF16).reshape(
                    groups, SUB, LANES
                )

            spread(v_out, f_in, 2 + side, q, back)

    convolve(0, part, wide)
    convolve(1, wide, part)

    loads[5].wait()

    @pl.loop(0, w.shape[0] // BLK)
    def _(b):
        at = span(b * BLK, BLK)
        for n in range(w.shape[1] // BLK):
            cols = slice(n * BLK, (n + 1) * BLK)
            w[at, cols] = (w[at, cols].astype(F32) * scales[b, n]).astype(BF16)

    @pl.when(me > 0)
    def _():
        halo_q.wait_recv()

    @pl.loop(0, rows // part)
    def _(q):
        @pl.loop(0, groups, unroll=4)
        def _(j):
            feat_q[j, span(q * part, part), :] = featured(0, q * part, j)

    def swap(q):
        return pltpu.make_async_remote_copy(
            src_ref=part_out.at[q],
            dst_ref=part_in.at[q],
            send_sem=send_sem.at[4],
            recv_sem=recv_p.at[q],
            device_id=(me, other),
            device_id_type=MESH_ID,
        )

    for q in range(packed // wide):
        await_chunk(f_in, 2, q, wide)

    @pl.loop(0, chunks)
    def _(q):
        await_chunk(f_in, 3, q, part)
        at, later = span(q * part, part), span(packed + q * part, part)
        for j in range(groups):
            lanes = slice(j * LANES, (j + 1) * LANES)
            low, high = f_in[0, j, at, :].astype(F32), f_in[1, j, at, :].astype(F32)
            early = side_by_side(low, swapped(high)) * feat_q[j, at, :].astype(F32)
            late = side_by_side(swapped(low), high) * feat_q[j, later, :].astype(F32)
            gated[0:part, lanes] = early.astype(BF16)
            gated[part : 2 * part, lanes] = late.astype(BF16)
        part_out[q] = dot(gated[...], w[:, span(other * half, half)]).astype(BF16)
        swap(q).start()
        part_own[q] = dot(gated[...], w[:, span(mine * half, half)]).astype(BF16)

    @pl.loop(0, chunks)
    def _(q):
        swap(q).wait_recv()
        total = (part_own[q].astype(F32) + part_in[q].astype(F32)).astype(BF16)
        out[span(q * part, part), :] = total[:part]
        out[span(packed + q * part, part), :] = total[part:]

    @pl.when(me < groups - 1)
    def _():
        halo_kv.wait_send()
        halo_q.wait_send()

    for side in range(4):
        sent = (g_out if side < 2 else v_out).at[side % 2, pl.ds(0, groups - 1)]
        pltpu.make_async_copy(sent, sent, send_sem.at[side]).wait()
    pltpu.make_async_copy(part_out, part_out, send_sem.at[4]).wait()


def fused(projected, feat_weight, long_filter, skip_gain, out_values, out_scales):
    groups = lax.axis_size("seq")
    rows, local_ch = projected.shape[1:]
    out_width = out_values.shape[1]
    half = out_width // 2
    tables = dft_tables(groups, rows)
    slabs = tables[0].shape[1] // SUB
    hbm = pl.BlockSpec(memory_space=pl.ANY)
    vmem = pl.BlockSpec(memory_space=pltpu.VMEM)
    smem = pl.BlockSpec(memory_space=pltpu.SMEM)
    block = pltpu.VMEM((groups, rows, LANES), BF16)
    halves = pltpu.VMEM((2, groups, rows // 2, LANES), BF16)
    chunks = rows // CHUNK
    return pl.pallas_call(
        functools.partial(fused_kernel, groups, rows),
        out_shape=jax.ShapeDtypeStruct((rows, half), BF16),
        in_specs=[hbm, vmem, hbm, vmem, hbm, smem, hbm, hbm, hbm, hbm],
        out_specs=vmem,
        scratch_shapes=[
            pltpu.VMEM((3, RIM + rows, local_ch), BF16),
            halves,
            halves,
            block,
            halves,
            halves,
            block,
            pltpu.VMEM(long_filter.shape, F32),
            block,
            pltpu.VMEM((slabs // 2, rows, LANES), BF16),
            pltpu.VMEM((slabs, rows, LANES), BF16),
            pltpu.VMEM((2, slabs // 8, 2 * rows, 2 * LANES), F32),
            pltpu.VMEM(tables[0].shape, BF16),
            pltpu.VMEM(tables[1].shape, BF16),
            pltpu.VMEM(tables[2].shape, BF16),
            pltpu.VMEM(tables[3].shape, BF16),
            pltpu.VMEM(out_values.shape, BF16),
            pltpu.VMEM((CHUNK, local_ch), BF16),
            pltpu.VMEM((chunks, CHUNK, half), BF16),
            pltpu.VMEM((chunks, CHUNK, half), BF16),
            pltpu.VMEM((chunks, CHUNK, half), BF16),
            pltpu.SemaphoreType.DMA((7,)),
            pltpu.SemaphoreType.DMA((4,)),
            pltpu.SemaphoreType.DMA((5,)),
            pltpu.SemaphoreType.DMA((4 * chunks,)),
            pltpu.SemaphoreType.DMA((chunks,)),
        ],
        compiler_params=pltpu.CompilerParams(
            collective_id=0, has_side_effects=True, vmem_limit_bytes=58 * 2**20
        ),
        cost_estimate=pl.CostEstimate(
            flops=10 * 10**9, bytes_accessed=32 * 2**20, transcendentals=0
        ),
    )(
        projected,
        feat_weight,
        long_filter,
        skip_gain.reshape(1, -1),
        out_values,
        out_scales,
        *[jnp.asarray(x) for x in tables],
    )


def fits(projected, long_filter, out_values):
    groups = lax.axis_size("seq")
    rows, local_ch = projected.shape[1:]
    return (
        lax.axis_size("tensor") == 2
        and long_filter.shape[0] == LANES
        and local_ch == groups * LANES
        and rows == 2 * LANES
        and groups == SUB
        and out_values.shape[1] % (2 * LANES) == 0
    )


TRIPLE = lax.Precision.HIGH


def passed_along(x, axis, by):
    size = lax.axis_size(axis)
    pairs = [(i, i + by) for i in range(size) if 0 <= i + by < size]
    return lax.ppermute(x, axis, pairs)


def split_length(whole):
    for candidate in range(2, whole + 1, 2):
        if whole % candidate == 0 and candidate * candidate >= whole:
            return (candidate, whole // candidate)
    return (whole, 1)


def angle_pair(row_count, col_count, period):
    row_ids = lax.broadcasted_iota(jnp.int32, (row_count, col_count), 0)
    col_ids = lax.broadcasted_iota(jnp.int32, (row_count, col_count), 1)
    angles = (row_ids * col_ids % period).astype(jnp.float32) * (2.0 * math.pi / period)
    return (jnp.cos(angles), jnp.sin(angles))


def make_tables(length):
    whole = 2 * length
    size_a, size_b = split_length(whole)
    return (
        angle_pair(size_a, size_a, size_a),
        angle_pair(size_b, size_b, size_b),
        angle_pair(size_a, size_b, whole),
        size_a,
        size_b,
    )


def right_mul(signal, matrix):
    return jnp.einsum("ckn,nm->ckm", signal, matrix, precision=TRIPLE)


def forward(signal, tables):
    (cos_a, sin_a), (cos_b, sin_b), (cos_t, sin_t), size_a, size_b = tables
    half_a = size_a // 2
    blocks = signal.reshape(signal.shape[0], half_a, size_b)
    real_a = jnp.einsum("kn,cnb->ckb", cos_a[:, :half_a], blocks, precision=TRIPLE)
    imag_a = -jnp.einsum("kn,cnb->ckb", sin_a[:, :half_a], blocks, precision=TRIPLE)
    real_t = real_a * cos_t + imag_a * sin_t
    imag_t = imag_a * cos_t - real_a * sin_t
    real_f = right_mul(real_t, cos_b) + right_mul(imag_t, sin_b)
    imag_f = right_mul(imag_t, cos_b) - right_mul(real_t, sin_b)
    return (real_f, imag_f)


def inverse(real_f, imag_f, tables):
    (cos_a, sin_a), (cos_b, sin_b), (cos_t, sin_t), size_a, size_b = tables
    half_a = size_a // 2
    real_z = right_mul(real_f, cos_b) - right_mul(imag_f, sin_b)
    imag_z = right_mul(imag_f, cos_b) + right_mul(real_f, sin_b)
    real_w = real_z * cos_t - imag_z * sin_t
    imag_w = imag_z * cos_t + real_z * sin_t
    out_half = jnp.einsum("nk,ckb->cnb", cos_a[:half_a, :], real_w, precision=TRIPLE) - jnp.einsum(
        "nk,ckb->cnb", sin_a[:half_a, :], imag_w, precision=TRIPLE
    )
    return out_half.reshape(out_half.shape[0], half_a * size_b) * (1.0 / (size_a * size_b))


def long_mix(gated_kv, spectrum, own_gain, tables):
    kv_values = gated_kv.astype(jnp.float32)
    real_u, imag_u = forward(kv_values, tables)
    real_h, imag_h = spectrum
    real_p = real_u * real_h - imag_u * imag_h
    imag_p = real_u * imag_h + imag_u * real_h
    convolved = inverse(real_p, imag_p, tables)
    return (convolved + own_gain[:, None] * kv_values).astype(jnp.bfloat16)


def featurize(extended, weights, length):
    tap_count = weights.shape[1]
    running = jnp.zeros(extended.shape[:2] + (length,), jnp.float32)
    for lag_idx in range(tap_count):
        offset = tap_count - 1 - lag_idx
        running = running + weights[:, lag_idx, :, None] * extended[
            :, :, offset : offset + length
        ].astype(jnp.float32)
    return running.astype(jnp.bfloat16)


def multiply_round(left_arr, right_arr):
    return (left_arr.astype(jnp.float32) * right_arr.astype(jnp.float32)).astype(jnp.bfloat16)


def local(projected, feat_weight, long_filter, skip_gain, out_values, out_scales):
    if fits(projected, long_filter, out_values):
        return fused(projected, feat_weight, long_filter, skip_gain, out_values, out_scales)
    groups = lax.axis_size("seq")
    tok_rows = projected.shape[1]
    local_ch = projected.shape[2]
    length = tok_rows * groups
    tables = make_tables(length)
    spectrum = forward(long_filter, tables)
    columns = jnp.transpose(projected, (0, 2, 1))
    rim_width = KS - 1
    prior_rows = passed_along(columns[:, :, tok_rows - rim_width :], "seq", 1)
    featured = featurize(jnp.concatenate([prior_rows, columns], axis=2), feat_weight, tok_rows)
    regrouped = lax.all_to_all(featured, "seq", split_axis=1, concat_axis=2, tiled=True)
    gated_kv = multiply_round(regrouped[1], regrouped[2])
    filtered = long_mix(gated_kv, spectrum, skip_gain, tables)
    gated = multiply_round(regrouped[0], filtered)
    gated_home = lax.all_to_all(gated, "seq", split_axis=1, concat_axis=0, tiled=True)
    block_count = local_ch // BLK
    out_width = out_values.shape[1]
    stacked = gated_home.reshape(block_count, BLK, tok_rows)
    weight_blocks = out_values.reshape(block_count, BLK, out_width)
    scale_cols = jnp.repeat(out_scales, BLK, axis=1)
    products = jnp.einsum(
        "bkn,bkt->bnt", weight_blocks, stacked, preferred_element_type=jnp.float32
    )
    summed = lax.psum_scatter(
        jnp.sum(products * scale_cols[:, :, None], axis=0).astype(jnp.bfloat16),
        "tensor",
        scatter_dimension=0,
        tiled=True,
    )
    return jnp.transpose(summed, (1, 0))


def solution(mesh):
    return jax.shard_map(
        local,
        mesh=mesh,
        in_specs=(
            P(None, "seq", "tensor"),
            P(None, None, "tensor"),
            P(("tensor", "seq"), None),
            P(("tensor", "seq")),
            P("tensor", None),
            P("tensor", None),
        ),
        out_specs=P("seq", "tensor"),
        check_vma=False,
    )
```

```python
import functools
import math

import jax
import jax.numpy as jnp
import ml_dtypes
import numpy as np
from jax import lax
from jax.experimental import pallas as pl
from jax.experimental.pallas import tpu as pltpu
from jax.sharding import PartitionSpec as P

KS = 7
BLK = 128
LANES = 128
RIM = 16
SUB = 16
CHUNK = 64
MESH_ID = pl.DeviceIdType.MESH
BF16 = jnp.bfloat16
F32 = jnp.float32


def dft_tables(groups, rows):
    whole = 2 * groups * rows
    evens = np.arange(0, groups + 1, 2)
    odds = np.arange(1, groups + 1, 2)
    slots = len(evens) + len(evens) % 2
    k_a = np.zeros((2 * slots,), np.int64)
    weight = np.zeros((2 * slots,))
    for base, kept in ((0, evens), (slots, odds)):
        k_a[base : base + len(kept)] = kept
        weight[base : base + len(kept)] = np.where(kept % groups == 0, 1.0, 2.0) / whole
    n_a = np.arange(groups)
    r = np.arange(rows)
    turns = k_a[:, None, None] * (n_a[None, :, None] * rows + r[None, None, :]) % whole
    angles = turns * (2.0 * np.pi / whole)
    parts = np.stack([np.cos(angles), -np.sin(angles)], axis=1)
    parts = parts * (weight > 0)[:, None, None, None]
    blocks = parts.reshape(2 * slots, 2, groups, rows // SUB, SUB)
    first = np.zeros((rows // SUB, 2 * slots, 2, SUB, groups, SUB))
    last = np.zeros((rows // SUB, groups, SUB, 2 * slots, 2, SUB))
    for lo in range(SUB):
        cut = blocks[:, :, :, :, lo]
        first[:, :, :, lo, :, lo] = cut.transpose(3, 0, 1, 2)
        last[:, :, lo, :, :, lo] = (cut * weight[:, None, None, None]).transpose(3, 2, 0, 1)
    first = first.reshape(rows // SUB, 4 * slots * SUB, groups * SUB)
    last = last.reshape(rows // SUB, groups * SUB, 4 * slots * SUB)
    inner = (r[:, None] * r[None, :] % rows) * (2.0 * np.pi / rows)
    cos, sin = np.cos(inner), np.sin(inner)
    ahead = np.block([[cos, sin], [-sin, cos]])
    back = np.block([[cos, -sin], [sin, cos]])
    return [x.astype(ml_dtypes.bfloat16) for x in (first, ahead, back, last)]


def dot(a, b):
    return jnp.dot(a, b, preferred_element_type=F32)


def swapped(x):
    return pltpu.roll(x, LANES // 2, 1)


def side_by_side(left, right):
    low = lax.broadcasted_iota(jnp.int32, left.shape, 1) < LANES // 2
    return jnp.where(low, left, right)


def fused_kernel(
    groups,
    rows,
    proj,
    taps,
    filt,
    gain,
    weights,
    scales,
    t_first,
    t_ahead,
    t_back,
    t_last,
    out,
    pb,
    g_out,
    u_in,
    u_wide,
    v_out,
    f_in,
    feat_q,
    fl,
    ft,
    x1,
    xz,
    spec,
    m_first,
    m_ahead,
    m_back,
    m_last,
    w,
    gated,
    part_own,
    part_out,
    part_in,
    loc_sem,
    halo_sem,
    send_sem,
    recv_sem,
    recv_p,
):
    me = lax.axis_index("seq")
    mine = lax.axis_index("tensor")
    other = 1 - mine
    packed = rows // 2
    part = CHUNK // 2
    chunks = packed // part
    half = part_own.shape[2]

    load_in = pltpu.make_async_copy(proj, pb.at[:, pl.ds(RIM, rows)], loc_sem.at[0])
    load_in.start()

    def partner(mask):
        total = 0
        bit = 1
        while bit < groups:
            mixed = lax.rem(me // bit, 2) + lax.rem(mask // bit, 2)
            total = total + bit * lax.rem(mixed, 2)
            bit *= 2
        return total

    barrier = pltpu.get_barrier_semaphore()

    @pl.loop(1, groups)
    def _(step):
        pl.semaphore_signal(
            barrier, inc=1, device_id=(partner(step), mine), device_id_type=MESH_ID
        )

    pl.semaphore_signal(barrier, inc=1, device_id=(me, other), device_id_type=MESH_ID)
    pl.semaphore_wait(barrier, groups)

    def halo(first, count, slot):
        return pltpu.make_async_remote_copy(
            src_ref=proj.at[pl.ds(first, count), pl.ds(rows - RIM, RIM)],
            dst_ref=pb.at[pl.ds(first, count), pl.ds(0, RIM)],
            send_sem=halo_sem.at[slot],
            recv_sem=halo_sem.at[slot + 1],
            device_id=(lax.rem(me + 1, groups), mine),
            device_id_type=MESH_ID,
        )

    halo_kv, halo_q = halo(1, 2, 0), halo(0, 1, 2)

    @pl.when(me < groups - 1)
    def _():
        halo_kv.start()

    @pl.when(me == 0)
    def _():
        pb[:, 0:RIM, :] = jnp.zeros((pb.shape[0], RIM, pb.shape[2]), BF16)

    load_in.wait()
    loads = [
        pltpu.make_async_copy(src, dst, loc_sem.at[1 + i])
        for i, (src, dst) in enumerate(
            (
                (filt, fl),
                (t_first, m_first),
                (t_ahead, m_ahead),
                (t_back, m_back),
                (t_last, m_last),
                (weights, w),
            )
        )
    ]
    for load in loads:
        load.start()

    def featured(p, start, j):
        lanes = pl.ds(pl.multiple_of(j * LANES, LANES), LANES)
        x = pb[p, pl.ds(pl.multiple_of(start, part), part + RIM), lanes].astype(F32)
        run = None
        for lag in range(KS):
            term = taps[p, lag : lag + 1, lanes] * x[RIM - lag : RIM - lag + part]
            run = term if run is None else run + term
        return run.astype(BF16)

    def span(start, count):
        return pl.ds(pl.multiple_of(start, count), count)

    first_slot = (0, chunks, 2 * chunks, 3 * chunks)

    def spread(src, dst, side, q, count):
        at = span(q * count, count)

        @pl.loop(1, groups)
        def _(step):
            peer = partner(groups - step)
            pltpu.make_async_remote_copy(
                src_ref=src.at[side % 2, peer, at],
                dst_ref=dst.at[side % 2, me, at],
                send_sem=send_sem.at[side],
                recv_sem=recv_sem.at[first_slot[side] + q],
                device_id=(peer, mine),
                device_id_type=MESH_ID,
            ).start()

        dst[side % 2, me, at, :] = src[side % 2, me, at, :]

    def await_chunk(dst, side, q, count):
        view = dst.at[side % 2, pl.ds(0, groups - 1), span(q * count, count)]
        pltpu.make_async_copy(view, view, recv_sem.at[first_slot[side] + q]).wait()

    wide = packed // 2

    def feature_chunk(q):
        at = span(q * part, part)

        @pl.loop(0, groups)
        def _(j):
            def product(start):
                k = featured(1, start, j).astype(F32)
                return k * featured(2, start, j).astype(F32)

            early, late = product(q * part), product(packed + q * part)
            g_out[0, j, at, :] = side_by_side(early, swapped(late)).astype(BF16)
            g_out[1, j, at, :] = side_by_side(swapped(early), late).astype(BF16)

    feature_chunk(chunks - 2)
    feature_chunk(chunks - 1)
    spread(g_out, u_in, 0, 1, wide)
    feature_chunk(1)

    @pl.when(me > 0)
    def _():
        halo_kv.wait_recv()

    feature_chunk(0)
    spread(g_out, u_in, 0, 0, wide)
    spread(g_out, u_in, 1, 0, packed)

    @pl.when(me < groups - 1)
    def _():
        halo_q.start()

    loads[0].wait()

    @pl.loop(0, groups, unroll=4)
    def _(a):
        for piece in range(rows // LANES):
            start = pl.multiple_of(a * rows + piece * LANES, LANES)
            at = slice(piece * LANES, (piece + 1) * LANES)
            ft[a, at, :] = fl[:, pl.ds(start, LANES)].astype(BF16).T

    for load in loads[1:5]:
        load.wait()

    slabs = xz.shape[0]
    half_slabs = slabs // 2
    fours = half_slabs // 4

    def first_stage(src, s):
        block = src[:, span(s * SUB, SUB), :].reshape(groups * SUB, LANES)
        found = dot(m_first[s], block)
        return found[: half_slabs * SUB], found[half_slabs * SUB :]

    def pack(side, even, odd):
        if side == 0:
            both = side_by_side(even, swapped(odd))
        else:
            both = side_by_side(swapped(even), odd)
        return both.astype(BF16).reshape(half_slabs, SUB, LANES)

    def four_of(src, j):
        left = src[pl.ds(4 * j, 2)].reshape(2 * rows, LANES)
        right = src[pl.ds(4 * j + 2, 2)].reshape(2 * rows, LANES)
        return jnp.concatenate([left, right], axis=1)

    @pl.loop(0, rows // SUB, unroll=4)
    def _(s):
        even, odd = first_stage(ft, s)
        x1[:, span(s * SUB, SUB), :] = pack(0, even, odd)
        xz[0:half_slabs, span(s * SUB, SUB), :] = pack(1, even, odd)

    for j in range(fours):
        spec[0, j] = dot(m_ahead[...], four_of(x1, j))
        spec[1, j] = dot(m_ahead[...], four_of(xz, j))

    def convolve(side, count, back):
        @pl.loop(0, packed // count)
        def _(i):
            q = lax.rem(i + 1, packed // count)
            await_chunk(u_in, side, q, count)
            at = span(q * count, count)

            @pl.loop(0, groups, unroll=4)
            def _(a):
                held = u_in[side, a, at, :]
                turned = swapped(held.astype(F32)).astype(BF16)
                early, late = (held, turned) if side == 0 else (turned, held)
                u_wide[a, at, :] = early
                u_wide[a, span(packed + q * count, count), :] = late

            @pl.loop(0, count // SUB, unroll=2)
            def _(c):
                for base in (0, packed // SUB):
                    s = base + q * (count // SUB) + c
                    x1[:, span(s * SUB, SUB), :] = pack(side, *first_stage(u_wide, s))

        for j in range(fours):
            values = dot(m_ahead[...], four_of(x1, j))
            re_u, im_u = values[:rows], values[rows:]
            re_h, im_h = spec[side, j, 0:rows, :], spec[side, j, rows : 2 * rows, :]
            product = jnp.concatenate(
                [re_u * re_h - im_u * im_h, re_u * im_h + im_u * re_h], axis=0
            ).astype(BF16)
            z = dot(m_back[...], product)
            for piece in range(2):
                held = z[:, piece * LANES : (piece + 1) * LANES]
                turned = swapped(held)
                even, odd = (held, turned) if side == 0 else (turned, held)
                at = 4 * j + 2 * piece
                xz[pl.ds(at, 2)] = even.astype(BF16).reshape(2, rows, LANES)
                xz[pl.ds(half_slabs + at, 2)] = odd.astype(BF16).reshape(2, rows, LANES)

        def filtered(s):
            at = span(s * SUB, SUB)
            conv = dot(m_last[s], xz[:, at, :].reshape(slabs * SUB, LANES))
            direct = gain[...] * u_wide[:, at, :].reshape(groups * SUB, LANES).astype(F32)
            return conv + direct

        @pl.loop(0, packed // back)
        def _(q):
            @pl.loop(0, back // SUB, unroll=min(4, back // SUB))
            def _(c):
                s = q * (back // SUB) + c
                early, late = filtered(s), filtered(packed // SUB + s)
                if side == 0:
                    both = side_by_side(early, swapped(late))
                else:
                    both = side_by_side(swapped(early), late)
                v_out[side, :, span(s * SUB, SUB), :] = both.astype(BF16).reshape(
                    groups, SUB, LANES
                )

            spread(v_out, f_in, 2 + side, q, back)

    convolve(0, wide, packed)
    convolve(1, packed, part)

    loads[5].wait()

    @pl.loop(0, w.shape[0] // BLK)
    def _(b):
        at = span(b * BLK, BLK)
        for n in range(w.shape[1] // BLK):
            cols = slice(n * BLK, (n + 1) * BLK)
            scale = jnp.full((BLK, BLK), scales[b, n], F32).astype(BF16)
            w[at, cols] = w[at, cols] * scale

    @pl.when(me > 0)
    def _():
        halo_q.wait_recv()

    @pl.loop(0, rows // part)
    def _(q):
        @pl.loop(0, groups, unroll=4)
        def _(j):
            feat_q[j, span(q * part, part), :] = featured(0, q * part, j)

    def swap(q):
        return pltpu.make_async_remote_copy(
            src_ref=part_out.at[q],
            dst_ref=part_in.at[q],
            send_sem=send_sem.at[4],
            recv_sem=recv_p.at[q],
            device_id=(me, other),
            device_id_type=MESH_ID,
        )

    await_chunk(f_in, 2, 0, packed)

    @pl.loop(0, chunks)
    def _(q):
        await_chunk(f_in, 3, q, part)
        at, later = span(q * part, part), span(packed + q * part, part)
        for j in range(groups):
            lanes = slice(j * LANES, (j + 1) * LANES)
            low, high = f_in[0, j, at, :].astype(F32), f_in[1, j, at, :].astype(F32)
            early = side_by_side(low, swapped(high)) * feat_q[j, at, :].astype(F32)
            late = side_by_side(swapped(low), high) * feat_q[j, later, :].astype(F32)
            gated[0:part, lanes] = early.astype(BF16)
            gated[part : 2 * part, lanes] = late.astype(BF16)
        part_out[q] = dot(gated[...], w[:, span(other * half, half)]).astype(BF16)
        swap(q).start()
        part_own[q] = dot(gated[...], w[:, span(mine * half, half)]).astype(BF16)

    @pl.loop(0, chunks)
    def _(q):
        swap(q).wait_recv()
        total = (part_own[q].astype(F32) + part_in[q].astype(F32)).astype(BF16)
        out[span(q * part, part), :] = total[:part]
        out[span(packed + q * part, part), :] = total[part:]

    @pl.when(me < groups - 1)
    def _():
        halo_kv.wait_send()
        halo_q.wait_send()

    for side in range(4):
        sent = (g_out if side < 2 else v_out).at[side % 2, pl.ds(0, groups - 1)]
        pltpu.make_async_copy(sent, sent, send_sem.at[side]).wait()
    pltpu.make_async_copy(part_out, part_out, send_sem.at[4]).wait()


def fused(projected, feat_weight, long_filter, skip_gain, out_values, out_scales):
    groups = lax.axis_size("seq")
    rows, local_ch = projected.shape[1:]
    out_width = out_values.shape[1]
    half = out_width // 2
    tables = dft_tables(groups, rows)
    slabs = tables[0].shape[1] // SUB
    hbm = pl.BlockSpec(memory_space=pl.ANY)
    vmem = pl.BlockSpec(memory_space=pltpu.VMEM)
    smem = pl.BlockSpec(memory_space=pltpu.SMEM)
    block = pltpu.VMEM((groups, rows, LANES), BF16)
    halves = pltpu.VMEM((2, groups, rows // 2, LANES), BF16)
    chunks = rows // CHUNK
    return pl.pallas_call(
        functools.partial(fused_kernel, groups, rows),
        out_shape=jax.ShapeDtypeStruct((rows, half), BF16),
        in_specs=[hbm, vmem, hbm, vmem, hbm, smem, hbm, hbm, hbm, hbm],
        out_specs=vmem,
        scratch_shapes=[
            pltpu.VMEM((3, RIM + rows, local_ch), BF16),
            halves,
            halves,
            block,
            halves,
            halves,
            block,
            pltpu.VMEM(long_filter.shape, F32),
            block,
            pltpu.VMEM((slabs // 2, rows, LANES), BF16),
            pltpu.VMEM((slabs, rows, LANES), BF16),
            pltpu.VMEM((2, slabs // 8, 2 * rows, 2 * LANES), F32),
            pltpu.VMEM(tables[0].shape, BF16),
            pltpu.VMEM(tables[1].shape, BF16),
            pltpu.VMEM(tables[2].shape, BF16),
            pltpu.VMEM(tables[3].shape, BF16),
            pltpu.VMEM(out_values.shape, BF16),
            pltpu.VMEM((CHUNK, local_ch), BF16),
            pltpu.VMEM((chunks, CHUNK, half), BF16),
            pltpu.VMEM((chunks, CHUNK, half), BF16),
            pltpu.VMEM((chunks, CHUNK, half), BF16),
            pltpu.SemaphoreType.DMA((7,)),
            pltpu.SemaphoreType.DMA((4,)),
            pltpu.SemaphoreType.DMA((5,)),
            pltpu.SemaphoreType.DMA((4 * chunks,)),
            pltpu.SemaphoreType.DMA((chunks,)),
        ],
        compiler_params=pltpu.CompilerParams(
            collective_id=0, has_side_effects=True, vmem_limit_bytes=58 * 2**20
        ),
        cost_estimate=pl.CostEstimate(
            flops=10 * 10**9, bytes_accessed=32 * 2**20, transcendentals=0
        ),
    )(
        projected,
        feat_weight,
        long_filter,
        skip_gain.reshape(1, -1),
        out_values,
        out_scales,
        *[jnp.asarray(x) for x in tables],
    )


def fits(projected, long_filter, out_values):
    groups = lax.axis_size("seq")
    rows, local_ch = projected.shape[1:]
    return (
        lax.axis_size("tensor") == 2
        and long_filter.shape[0] == LANES
        and local_ch == groups * LANES
        and rows == 2 * LANES
        and groups == SUB
        and out_values.shape[1] % (2 * LANES) == 0
    )


TRIPLE = lax.Precision.HIGH


def passed_along(x, axis, by):
    size = lax.axis_size(axis)
    pairs = [(i, i + by) for i in range(size) if 0 <= i + by < size]
    return lax.ppermute(x, axis, pairs)


def split_length(whole):
    for candidate in range(2, whole + 1, 2):
        if whole % candidate == 0 and candidate * candidate >= whole:
            return (candidate, whole // candidate)
    return (whole, 1)


def angle_pair(row_count, col_count, period):
    row_ids = lax.broadcasted_iota(jnp.int32, (row_count, col_count), 0)
    col_ids = lax.broadcasted_iota(jnp.int32, (row_count, col_count), 1)
    angles = (row_ids * col_ids % period).astype(jnp.float32) * (2.0 * math.pi / period)
    return (jnp.cos(angles), jnp.sin(angles))


def make_tables(length):
    whole = 2 * length
    size_a, size_b = split_length(whole)
    return (
        angle_pair(size_a, size_a, size_a),
        angle_pair(size_b, size_b, size_b),
        angle_pair(size_a, size_b, whole),
        size_a,
        size_b,
    )


def right_mul(signal, matrix):
    return jnp.einsum("ckn,nm->ckm", signal, matrix, precision=TRIPLE)


def forward(signal, tables):
    (cos_a, sin_a), (cos_b, sin_b), (cos_t, sin_t), size_a, size_b = tables
    half_a = size_a // 2
    blocks = signal.reshape(signal.shape[0], half_a, size_b)
    real_a = jnp.einsum("kn,cnb->ckb", cos_a[:, :half_a], blocks, precision=TRIPLE)
    imag_a = -jnp.einsum("kn,cnb->ckb", sin_a[:, :half_a], blocks, precision=TRIPLE)
    real_t = real_a * cos_t + imag_a * sin_t
    imag_t = imag_a * cos_t - real_a * sin_t
    real_f = right_mul(real_t, cos_b) + right_mul(imag_t, sin_b)
    imag_f = right_mul(imag_t, cos_b) - right_mul(real_t, sin_b)
    return (real_f, imag_f)


def inverse(real_f, imag_f, tables):
    (cos_a, sin_a), (cos_b, sin_b), (cos_t, sin_t), size_a, size_b = tables
    half_a = size_a // 2
    real_z = right_mul(real_f, cos_b) - right_mul(imag_f, sin_b)
    imag_z = right_mul(imag_f, cos_b) + right_mul(real_f, sin_b)
    real_w = real_z * cos_t - imag_z * sin_t
    imag_w = imag_z * cos_t + real_z * sin_t
    out_half = jnp.einsum("nk,ckb->cnb", cos_a[:half_a, :], real_w, precision=TRIPLE) - jnp.einsum(
        "nk,ckb->cnb", sin_a[:half_a, :], imag_w, precision=TRIPLE
    )
    return out_half.reshape(out_half.shape[0], half_a * size_b) * (1.0 / (size_a * size_b))


def long_mix(gated_kv, spectrum, own_gain, tables):
    kv_values = gated_kv.astype(jnp.float32)
    real_u, imag_u = forward(kv_values, tables)
    real_h, imag_h = spectrum
    real_p = real_u * real_h - imag_u * imag_h
    imag_p = real_u * imag_h + imag_u * real_h
    convolved = inverse(real_p, imag_p, tables)
    return (convolved + own_gain[:, None] * kv_values).astype(jnp.bfloat16)


def featurize(extended, weights, length):
    tap_count = weights.shape[1]
    running = jnp.zeros(extended.shape[:2] + (length,), jnp.float32)
    for lag_idx in range(tap_count):
        offset = tap_count - 1 - lag_idx
        running = running + weights[:, lag_idx, :, None] * extended[
            :, :, offset : offset + length
        ].astype(jnp.float32)
    return running.astype(jnp.bfloat16)


def multiply_round(left_arr, right_arr):
    return (left_arr.astype(jnp.float32) * right_arr.astype(jnp.float32)).astype(jnp.bfloat16)


def local(projected, feat_weight, long_filter, skip_gain, out_values, out_scales):
    if fits(projected, long_filter, out_values):
        return fused(projected, feat_weight, long_filter, skip_gain, out_values, out_scales)
    groups = lax.axis_size("seq")
    tok_rows = projected.shape[1]
    local_ch = projected.shape[2]
    length = tok_rows * groups
    tables = make_tables(length)
    spectrum = forward(long_filter, tables)
    columns = jnp.transpose(projected, (0, 2, 1))
    rim_width = KS - 1
    prior_rows = passed_along(columns[:, :, tok_rows - rim_width :], "seq", 1)
    featured = featurize(jnp.concatenate([prior_rows, columns], axis=2), feat_weight, tok_rows)
    regrouped = lax.all_to_all(featured, "seq", split_axis=1, concat_axis=2, tiled=True)
    gated_kv = multiply_round(regrouped[1], regrouped[2])
    filtered = long_mix(gated_kv, spectrum, skip_gain, tables)
    gated = multiply_round(regrouped[0], filtered)
    gated_home = lax.all_to_all(gated, "seq", split_axis=1, concat_axis=0, tiled=True)
    block_count = local_ch // BLK
    out_width = out_values.shape[1]
    stacked = gated_home.reshape(block_count, BLK, tok_rows)
    weight_blocks = out_values.reshape(block_count, BLK, out_width)
    scale_cols = jnp.repeat(out_scales, BLK, axis=1)
    products = jnp.einsum(
        "bkn,bkt->bnt", weight_blocks, stacked, preferred_element_type=jnp.float32
    )
    summed = lax.psum_scatter(
        jnp.sum(products * scale_cols[:, :, None], axis=0).astype(jnp.bfloat16),
        "tensor",
        scatter_dimension=0,
        tiled=True,
    )
    return jnp.transpose(summed, (1, 0))


def solution(mesh):
    return jax.shard_map(
        local,
        mesh=mesh,
        in_specs=(
            P(None, "seq", "tensor"),
            P(None, None, "tensor"),
            P(("tensor", "seq"), None),
            P(("tensor", "seq")),
            P("tensor", None),
            P("tensor", None),
        ),
        out_specs=P("seq", "tensor"),
        check_vma=False,
    )
```

```python
import functools
import math

import jax
import jax.numpy as jnp
import ml_dtypes
import numpy as np
from jax import lax
from jax.experimental import pallas as pl
from jax.experimental.pallas import tpu as pltpu
from jax.sharding import PartitionSpec as P

KS = 7
BLK = 128
LANES = 128
RIM = 16
SUB = 16
CHUNK = 64
MESH_ID = pl.DeviceIdType.MESH
BF16 = jnp.bfloat16
F32 = jnp.float32


def dft_tables(groups, rows):
    whole = 2 * groups * rows
    evens = np.arange(0, groups + 1, 2)
    odds = np.arange(1, groups + 1, 2)
    slots = len(evens) + len(evens) % 2
    k_a = np.zeros((2 * slots,), np.int64)
    weight = np.zeros((2 * slots,))
    for base, kept in ((0, evens), (slots, odds)):
        k_a[base : base + len(kept)] = kept
        weight[base : base + len(kept)] = np.where(kept % groups == 0, 1.0, 2.0) / whole
    n_a = np.arange(groups)
    r = np.arange(rows)
    turns = k_a[:, None, None] * (n_a[None, :, None] * rows + r[None, None, :]) % whole
    angles = turns * (2.0 * np.pi / whole)
    parts = np.stack([np.cos(angles), -np.sin(angles)], axis=1)
    parts = parts * (weight > 0)[:, None, None, None]
    blocks = parts.reshape(2 * slots, 2, groups, rows // SUB, SUB)
    first = np.zeros((rows // SUB, 2 * slots, 2, SUB, groups, SUB))
    last = np.zeros((rows // SUB, groups, SUB, 2 * slots, 2, SUB))
    for lo in range(SUB):
        cut = blocks[:, :, :, :, lo]
        first[:, :, :, lo, :, lo] = cut.transpose(3, 0, 1, 2)
        last[:, :, lo, :, :, lo] = (cut * weight[:, None, None, None]).transpose(3, 2, 0, 1)
    first = first.reshape(rows // SUB, 4 * slots * SUB, groups * SUB)
    last = last.reshape(rows // SUB, groups * SUB, 4 * slots * SUB)
    inner = (r[:, None] * r[None, :] % rows) * (2.0 * np.pi / rows)
    cos, sin = np.cos(inner), np.sin(inner)
    ahead = np.block([[cos, sin], [-sin, cos]])
    back = np.block([[cos, -sin], [sin, cos]])
    return [x.astype(ml_dtypes.bfloat16) for x in (first, ahead, back, last)]


def dot(a, b):
    return jnp.dot(a, b, preferred_element_type=F32)


def swapped(x):
    return pltpu.roll(x, LANES // 2, 1)


def side_by_side(left, right):
    low = lax.broadcasted_iota(jnp.int32, left.shape, 1) < LANES // 2
    return jnp.where(low, left, right)


def fused_kernel(
    groups,
    rows,
    proj,
    taps,
    filt,
    gain,
    weights,
    scales,
    t_first,
    t_ahead,
    t_back,
    t_last,
    out,
    pb,
    g_out,
    u_in,
    u_wide,
    v_out,
    f_in,
    feat_q,
    fl,
    ft,
    x1,
    xz,
    spec,
    m_first,
    m_ahead,
    m_back,
    m_last,
    w,
    gated,
    part_own,
    part_out,
    part_in,
    loc_sem,
    halo_sem,
    send_sem,
    recv_sem,
    recv_p,
):
    me = lax.axis_index("seq")
    mine = lax.axis_index("tensor")
    other = 1 - mine
    packed = rows // 2
    part = CHUNK // 2
    chunks = packed // part
    half = part_own.shape[2]

    load_in = pltpu.make_async_copy(proj, pb.at[:, pl.ds(RIM, rows)], loc_sem.at[0])
    load_in.start()

    def partner(mask):
        total = 0
        bit = 1
        while bit < groups:
            mixed = lax.rem(me // bit, 2) + lax.rem(mask // bit, 2)
            total = total + bit * lax.rem(mixed, 2)
            bit *= 2
        return total

    barrier = pltpu.get_barrier_semaphore()

    @pl.loop(1, groups)
    def _(step):
        pl.semaphore_signal(
            barrier, inc=1, device_id=(partner(step), mine), device_id_type=MESH_ID
        )

    pl.semaphore_signal(barrier, inc=1, device_id=(me, other), device_id_type=MESH_ID)
    pl.semaphore_wait(barrier, groups)

    def halo(first, count, slot):
        return pltpu.make_async_remote_copy(
            src_ref=proj.at[pl.ds(first, count), pl.ds(rows - RIM, RIM)],
            dst_ref=pb.at[pl.ds(first, count), pl.ds(0, RIM)],
            send_sem=halo_sem.at[slot],
            recv_sem=halo_sem.at[slot + 1],
            device_id=(lax.rem(me + 1, groups), mine),
            device_id_type=MESH_ID,
        )

    halo_kv, halo_q = halo(1, 2, 0), halo(0, 1, 2)

    @pl.when(me < groups - 1)
    def _():
        halo_kv.start()

    @pl.when(me == 0)
    def _():
        pb[:, 0:RIM, :] = jnp.zeros((pb.shape[0], RIM, pb.shape[2]), BF16)

    load_in.wait()
    loads = [
        pltpu.make_async_copy(src, dst, loc_sem.at[1 + i])
        for i, (src, dst) in enumerate(
            (
                (filt, fl),
                (t_first, m_first),
                (t_ahead, m_ahead),
                (t_back, m_back),
                (t_last, m_last),
                (weights, w),
            )
        )
    ]
    for load in loads:
        load.start()

    def featured(p, start, j):
        lanes = pl.ds(pl.multiple_of(j * LANES, LANES), LANES)
        x = pb[p, pl.ds(pl.multiple_of(start, part), part + RIM), lanes].astype(F32)
        run = None
        for lag in range(KS):
            term = taps[p, lag : lag + 1, lanes] * x[RIM - lag : RIM - lag + part]
            run = term if run is None else run + term
        return run.astype(BF16)

    def span(start, count):
        return pl.ds(pl.multiple_of(start, count), count)

    first_slot = (0, chunks, 2 * chunks, 3 * chunks)

    def spread(src, dst, side, q, count):
        at = span(q * count, count)

        @pl.loop(1, groups)
        def _(step):
            across = lax.rem(step, 2)
            peer = partner(across * (groups // 2) + step // 2)
            pltpu.make_async_remote_copy(
                src_ref=src.at[side % 2, peer, at],
                dst_ref=dst.at[side % 2, me, at],
                send_sem=send_sem.at[side],
                recv_sem=recv_sem.at[first_slot[side] + q],
                device_id=(peer, mine),
                device_id_type=MESH_ID,
            ).start()

        dst[side % 2, me, at, :] = src[side % 2, me, at, :]

    def await_chunk(dst, side, q, count):
        view = dst.at[side % 2, pl.ds(0, groups - 1), span(q * count, count)]
        pltpu.make_async_copy(view, view, recv_sem.at[first_slot[side] + q]).wait()

    wide = packed // 2

    def feature_chunk(q):
        at = span(q * part, part)

        @pl.loop(0, groups)
        def _(j):
            def product(start):
                k = featured(1, start, j).astype(F32)
                return k * featured(2, start, j).astype(F32)

            early, late = product(q * part), product(packed + q * part)
            g_out[0, j, at, :] = side_by_side(early, swapped(late)).astype(BF16)
            g_out[1, j, at, :] = side_by_side(swapped(early), late).astype(BF16)

        spread(g_out, u_in, 0, q, part)

    @pl.loop(1, chunks)
    def _(q):
        feature_chunk(q)

    @pl.when(me > 0)
    def _():
        halo_kv.wait_recv()

    feature_chunk(0)

    @pl.loop(0, 2)
    def _(q):
        spread(g_out, u_in, 1, q, wide)

    @pl.when(me < groups - 1)
    def _():
        halo_q.start()

    loads[0].wait()

    @pl.loop(0, groups, unroll=4)
    def _(a):
        for piece in range(rows // LANES):
            start = pl.multiple_of(a * rows + piece * LANES, LANES)
            at = slice(piece * LANES, (piece + 1) * LANES)
            ft[a, at, :] = fl[:, pl.ds(start, LANES)].astype(BF16).T

    for load in loads[1:5]:
        load.wait()

    slabs = xz.shape[0]
    half_slabs = slabs // 2
    fours = half_slabs // 4

    def first_stage(src, s):
        block = src[:, span(s * SUB, SUB), :].reshape(groups * SUB, LANES)
        found = dot(m_first[s], block)
        return found[: half_slabs * SUB], found[half_slabs * SUB :]

    def pack(side, even, odd):
        if side == 0:
            both = side_by_side(even, swapped(odd))
        else:
            both = side_by_side(swapped(even), odd)
        return both.astype(BF16).reshape(half_slabs, SUB, LANES)

    def four_of(src, j):
        left = src[pl.ds(4 * j, 2)].reshape(2 * rows, LANES)
        right = src[pl.ds(4 * j + 2, 2)].reshape(2 * rows, LANES)
        return jnp.concatenate([left, right], axis=1)

    @pl.loop(0, rows // SUB, unroll=4)
    def _(s):
        even, odd = first_stage(ft, s)
        x1[:, span(s * SUB, SUB), :] = pack(0, even, odd)
        xz[0:half_slabs, span(s * SUB, SUB), :] = pack(1, even, odd)

    for j in range(fours):
        spec[0, j] = dot(m_ahead[...], four_of(x1, j))
        spec[1, j] = dot(m_ahead[...], four_of(xz, j))

    def convolve(side, count, back):
        @pl.loop(0, packed // count)
        def _(i):
            q = lax.rem(i + 1, packed // count)
            await_chunk(u_in, side, q, count)
            at = span(q * count, count)

            @pl.loop(0, groups, unroll=4)
            def _(a):
                held = u_in[side, a, at, :]
                turned = swapped(held.astype(F32)).astype(BF16)
                early, late = (held, turned) if side == 0 else (turned, held)
                u_wide[a, at, :] = early
                u_wide[a, span(packed + q * count, count), :] = late

            @pl.loop(0, count // SUB, unroll=2)
            def _(c):
                for base in (0, packed // SUB):
                    s = base + q * (count // SUB) + c
                    x1[:, span(s * SUB, SUB), :] = pack(side, *first_stage(u_wide, s))

        for j in range(fours):
            values = dot(m_ahead[...], four_of(x1, j))
            re_u, im_u = values[:rows], values[rows:]
            re_h, im_h = spec[side, j, 0:rows, :], spec[side, j, rows : 2 * rows, :]
            product = jnp.concatenate(
                [re_u * re_h - im_u * im_h, re_u * im_h + im_u * re_h], axis=0
            ).astype(BF16)
            z = dot(m_back[...], product)
            for piece in range(2):
                held = z[:, piece * LANES : (piece + 1) * LANES]
                turned = swapped(held)
                even, odd = (held, turned) if side == 0 else (turned, held)
                at = 4 * j + 2 * piece
                xz[pl.ds(at, 2)] = even.astype(BF16).reshape(2, rows, LANES)
                xz[pl.ds(half_slabs + at, 2)] = odd.astype(BF16).reshape(2, rows, LANES)

        def filtered(s):
            at = span(s * SUB, SUB)
            conv = dot(m_last[s], xz[:, at, :].reshape(slabs * SUB, LANES))
            direct = gain[...] * u_wide[:, at, :].reshape(groups * SUB, LANES).astype(F32)
            return conv + direct

        @pl.loop(0, packed // back)
        def _(q):
            @pl.loop(0, back // SUB, unroll=min(4, back // SUB))
            def _(c):
                s = q * (back // SUB) + c
                early, late = filtered(s), filtered(packed // SUB + s)
                if side == 0:
                    both = side_by_side(early, swapped(late))
                else:
                    both = side_by_side(swapped(early), late)
                v_out[side, :, span(s * SUB, SUB), :] = both.astype(BF16).reshape(
                    groups, SUB, LANES
                )

            spread(v_out, f_in, 2 + side, q, back)

    convolve(0, part, wide)
    convolve(1, wide, part)

    loads[5].wait()

    @pl.loop(0, w.shape[0] // BLK)
    def _(b):
        at = span(b * BLK, BLK)
        for n in range(w.shape[1] // BLK):
            cols = slice(n * BLK, (n + 1) * BLK)
            scale = jnp.full((BLK, BLK), scales[b, n], F32).astype(BF16)
            w[at, cols] = w[at, cols] * scale

    @pl.when(me > 0)
    def _():
        halo_q.wait_recv()

    @pl.loop(0, rows // part)
    def _(q):
        @pl.loop(0, groups, unroll=4)
        def _(j):
            feat_q[j, span(q * part, part), :] = featured(0, q * part, j)

    def swap(q):
        return pltpu.make_async_remote_copy(
            src_ref=part_out.at[q],
            dst_ref=part_in.at[q],
            send_sem=send_sem.at[4],
            recv_sem=recv_p.at[q],
            device_id=(me, other),
            device_id_type=MESH_ID,
        )

    for q in range(packed // wide):
        await_chunk(f_in, 2, q, wide)

    @pl.loop(0, chunks)
    def _(q):
        await_chunk(f_in, 3, q, part)
        at, later = span(q * part, part), span(packed + q * part, part)
        for j in range(groups):
            lanes = slice(j * LANES, (j + 1) * LANES)
            low, high = f_in[0, j, at, :].astype(F32), f_in[1, j, at, :].astype(F32)
            early = side_by_side(low, swapped(high)) * feat_q[j, at, :].astype(F32)
            late = side_by_side(swapped(low), high) * feat_q[j, later, :].astype(F32)
            gated[0:part, lanes] = early.astype(BF16)
            gated[part : 2 * part, lanes] = late.astype(BF16)
        part_out[q] = dot(gated[...], w[:, span(other * half, half)]).astype(BF16)
        swap(q).start()
        part_own[q] = dot(gated[...], w[:, span(mine * half, half)]).astype(BF16)

    @pl.loop(0, chunks)
    def _(q):
        swap(q).wait_recv()
        total = (part_own[q].astype(F32) + part_in[q].astype(F32)).astype(BF16)
        out[span(q * part, part), :] = total[:part]
        out[span(packed + q * part, part), :] = total[part:]

    @pl.when(me < groups - 1)
    def _():
        halo_kv.wait_send()
        halo_q.wait_send()

    for side in range(4):
        sent = (g_out if side < 2 else v_out).at[side % 2, pl.ds(0, groups - 1)]
        pltpu.make_async_copy(sent, sent, send_sem.at[side]).wait()
    pltpu.make_async_copy(part_out, part_out, send_sem.at[4]).wait()


def fused(projected, feat_weight, long_filter, skip_gain, out_values, out_scales):
    groups = lax.axis_size("seq")
    rows, local_ch = projected.shape[1:]
    out_width = out_values.shape[1]
    half = out_width // 2
    tables = dft_tables(groups, rows)
    slabs = tables[0].shape[1] // SUB
    hbm = pl.BlockSpec(memory_space=pl.ANY)
    vmem = pl.BlockSpec(memory_space=pltpu.VMEM)
    smem = pl.BlockSpec(memory_space=pltpu.SMEM)
    block = pltpu.VMEM((groups, rows, LANES), BF16)
    halves = pltpu.VMEM((2, groups, rows // 2, LANES), BF16)
    chunks = rows // CHUNK
    return pl.pallas_call(
        functools.partial(fused_kernel, groups, rows),
        out_shape=jax.ShapeDtypeStruct((rows, half), BF16),
        in_specs=[hbm, vmem, hbm, vmem, hbm, smem, hbm, hbm, hbm, hbm],
        out_specs=vmem,
        scratch_shapes=[
            pltpu.VMEM((3, RIM + rows, local_ch), BF16),
            halves,
            halves,
            block,
            halves,
            halves,
            block,
            pltpu.VMEM(long_filter.shape, F32),
            block,
            pltpu.VMEM((slabs // 2, rows, LANES), BF16),
            pltpu.VMEM((slabs, rows, LANES), BF16),
            pltpu.VMEM((2, slabs // 8, 2 * rows, 2 * LANES), F32),
            pltpu.VMEM(tables[0].shape, BF16),
            pltpu.VMEM(tables[1].shape, BF16),
            pltpu.VMEM(tables[2].shape, BF16),
            pltpu.VMEM(tables[3].shape, BF16),
            pltpu.VMEM(out_values.shape, BF16),
            pltpu.VMEM((CHUNK, local_ch), BF16),
            pltpu.VMEM((chunks, CHUNK, half), BF16),
            pltpu.VMEM((chunks, CHUNK, half), BF16),
            pltpu.VMEM((chunks, CHUNK, half), BF16),
            pltpu.SemaphoreType.DMA((7,)),
            pltpu.SemaphoreType.DMA((4,)),
            pltpu.SemaphoreType.DMA((5,)),
            pltpu.SemaphoreType.DMA((4 * chunks,)),
            pltpu.SemaphoreType.DMA((chunks,)),
        ],
        compiler_params=pltpu.CompilerParams(
            collective_id=0, has_side_effects=True, vmem_limit_bytes=58 * 2**20
        ),
        cost_estimate=pl.CostEstimate(
            flops=10 * 10**9, bytes_accessed=32 * 2**20, transcendentals=0
        ),
    )(
        projected,
        feat_weight,
        long_filter,
        skip_gain.reshape(1, -1),
        out_values,
        out_scales,
        *[jnp.asarray(x) for x in tables],
    )


def fits(projected, long_filter, out_values):
    groups = lax.axis_size("seq")
    rows, local_ch = projected.shape[1:]
    return (
        lax.axis_size("tensor") == 2
        and long_filter.shape[0] == LANES
        and local_ch == groups * LANES
        and rows == 2 * LANES
        and groups == SUB
        and out_values.shape[1] % (2 * LANES) == 0
    )


TRIPLE = lax.Precision.HIGH


def passed_along(x, axis, by):
    size = lax.axis_size(axis)
    pairs = [(i, i + by) for i in range(size) if 0 <= i + by < size]
    return lax.ppermute(x, axis, pairs)


def split_length(whole):
    for candidate in range(2, whole + 1, 2):
        if whole % candidate == 0 and candidate * candidate >= whole:
            return (candidate, whole // candidate)
    return (whole, 1)


def angle_pair(row_count, col_count, period):
    row_ids = lax.broadcasted_iota(jnp.int32, (row_count, col_count), 0)
    col_ids = lax.broadcasted_iota(jnp.int32, (row_count, col_count), 1)
    angles = (row_ids * col_ids % period).astype(jnp.float32) * (2.0 * math.pi / period)
    return (jnp.cos(angles), jnp.sin(angles))


def make_tables(length):
    whole = 2 * length
    size_a, size_b = split_length(whole)
    return (
        angle_pair(size_a, size_a, size_a),
        angle_pair(size_b, size_b, size_b),
        angle_pair(size_a, size_b, whole),
        size_a,
        size_b,
    )


def right_mul(signal, matrix):
    return jnp.einsum("ckn,nm->ckm", signal, matrix, precision=TRIPLE)


def forward(signal, tables):
    (cos_a, sin_a), (cos_b, sin_b), (cos_t, sin_t), size_a, size_b = tables
    half_a = size_a // 2
    blocks = signal.reshape(signal.shape[0], half_a, size_b)
    real_a = jnp.einsum("kn,cnb->ckb", cos_a[:, :half_a], blocks, precision=TRIPLE)
    imag_a = -jnp.einsum("kn,cnb->ckb", sin_a[:, :half_a], blocks, precision=TRIPLE)
    real_t = real_a * cos_t + imag_a * sin_t
    imag_t = imag_a * cos_t - real_a * sin_t
    real_f = right_mul(real_t, cos_b) + right_mul(imag_t, sin_b)
    imag_f = right_mul(imag_t, cos_b) - right_mul(real_t, sin_b)
    return (real_f, imag_f)


def inverse(real_f, imag_f, tables):
    (cos_a, sin_a), (cos_b, sin_b), (cos_t, sin_t), size_a, size_b = tables
    half_a = size_a // 2
    real_z = right_mul(real_f, cos_b) - right_mul(imag_f, sin_b)
    imag_z = right_mul(imag_f, cos_b) + right_mul(real_f, sin_b)
    real_w = real_z * cos_t - imag_z * sin_t
    imag_w = imag_z * cos_t + real_z * sin_t
    out_half = jnp.einsum("nk,ckb->cnb", cos_a[:half_a, :], real_w, precision=TRIPLE) - jnp.einsum(
        "nk,ckb->cnb", sin_a[:half_a, :], imag_w, precision=TRIPLE
    )
    return out_half.reshape(out_half.shape[0], half_a * size_b) * (1.0 / (size_a * size_b))


def long_mix(gated_kv, spectrum, own_gain, tables):
    kv_values = gated_kv.astype(jnp.float32)
    real_u, imag_u = forward(kv_values, tables)
    real_h, imag_h = spectrum
    real_p = real_u * real_h - imag_u * imag_h
    imag_p = real_u * imag_h + imag_u * real_h
    convolved = inverse(real_p, imag_p, tables)
    return (convolved + own_gain[:, None] * kv_values).astype(jnp.bfloat16)


def featurize(extended, weights, length):
    tap_count = weights.shape[1]
    running = jnp.zeros(extended.shape[:2] + (length,), jnp.float32)
    for lag_idx in range(tap_count):
        offset = tap_count - 1 - lag_idx
        running = running + weights[:, lag_idx, :, None] * extended[
            :, :, offset : offset + length
        ].astype(jnp.float32)
    return running.astype(jnp.bfloat16)


def multiply_round(left_arr, right_arr):
    return (left_arr.astype(jnp.float32) * right_arr.astype(jnp.float32)).astype(jnp.bfloat16)


def local(projected, feat_weight, long_filter, skip_gain, out_values, out_scales):
    if fits(projected, long_filter, out_values):
        return fused(projected, feat_weight, long_filter, skip_gain, out_values, out_scales)
    groups = lax.axis_size("seq")
    tok_rows = projected.shape[1]
    local_ch = projected.shape[2]
    length = tok_rows * groups
    tables = make_tables(length)
    spectrum = forward(long_filter, tables)
    columns = jnp.transpose(projected, (0, 2, 1))
    rim_width = KS - 1
    prior_rows = passed_along(columns[:, :, tok_rows - rim_width :], "seq", 1)
    featured = featurize(jnp.concatenate([prior_rows, columns], axis=2), feat_weight, tok_rows)
    regrouped = lax.all_to_all(featured, "seq", split_axis=1, concat_axis=2, tiled=True)
    gated_kv = multiply_round(regrouped[1], regrouped[2])
    filtered = long_mix(gated_kv, spectrum, skip_gain, tables)
    gated = multiply_round(regrouped[0], filtered)
    gated_home = lax.all_to_all(gated, "seq", split_axis=1, concat_axis=0, tiled=True)
    block_count = local_ch // BLK
    out_width = out_values.shape[1]
    stacked = gated_home.reshape(block_count, BLK, tok_rows)
    weight_blocks = out_values.reshape(block_count, BLK, out_width)
    scale_cols = jnp.repeat(out_scales, BLK, axis=1)
    products = jnp.einsum(
        "bkn,bkt->bnt", weight_blocks, stacked, preferred_element_type=jnp.float32
    )
    summed = lax.psum_scatter(
        jnp.sum(products * scale_cols[:, :, None], axis=0).astype(jnp.bfloat16),
        "tensor",
        scatter_dimension=0,
        tiled=True,
    )
    return jnp.transpose(summed, (1, 0))


def solution(mesh):
    return jax.shard_map(
        local,
        mesh=mesh,
        in_specs=(
            P(None, "seq", "tensor"),
            P(None, None, "tensor"),
            P(("tensor", "seq"), None),
            P(("tensor", "seq")),
            P("tensor", None),
            P("tensor", None),
        ),
        out_specs=P("seq", "tensor"),
        check_vma=False,
    )
```

```python
import functools
import math

import jax
import jax.numpy as jnp
import ml_dtypes
import numpy as np
from jax import lax
from jax.experimental import pallas as pl
from jax.experimental.pallas import tpu as pltpu
from jax.sharding import PartitionSpec as P

KS = 7
BLK = 128
LANES = 128
RIM = 16
SUB = 16
CHUNK = 64
MESH_ID = pl.DeviceIdType.MESH
BF16 = jnp.bfloat16
F32 = jnp.float32


def dft_tables(groups, rows):
    whole = 2 * groups * rows
    kept = groups + 1
    padded = kept + kept % 2
    n_a = np.arange(groups)
    k_a = np.arange(kept)
    r = np.arange(rows)
    turns = k_a[:, None, None] * (n_a[None, :, None] * rows + r[None, None, :]) % whole
    angles = turns * (2.0 * np.pi / whole)
    parts = np.stack([np.cos(angles), -np.sin(angles)], axis=1)
    blocks = parts.reshape(kept, 2, groups, rows // SUB, SUB)
    first = np.zeros((rows // SUB, padded, 2, SUB, groups, SUB))
    last = np.zeros((rows // SUB, groups, SUB, padded, 2, SUB))
    weight = np.full((kept,), 2.0 / whole)
    weight[0] = weight[-1] = 1.0 / whole
    for lo in range(SUB):
        cut = blocks[:, :, :, :, lo]
        first[:, :kept, :, lo, :, lo] = cut.transpose(3, 0, 1, 2)
        last[:, :, lo, :kept, :, lo] = (cut * weight[:, None, None, None]).transpose(3, 2, 0, 1)
    first = first.reshape(rows // SUB, padded * 2 * SUB, groups * SUB)
    last = last.reshape(rows // SUB, groups * SUB, padded * 2 * SUB)
    inner = (r[:, None] * r[None, :] % rows) * (2.0 * np.pi / rows)
    cos, sin = np.cos(inner), np.sin(inner)
    ahead = np.block([[cos, sin], [-sin, cos]])
    back = np.block([[cos, -sin], [sin, cos]])
    return [x.astype(ml_dtypes.bfloat16) for x in (first, ahead, back, last)]


def dot(a, b):
    return jnp.dot(a, b, preferred_element_type=F32)


def fused_kernel(
    groups,
    rows,
    proj,
    taps,
    filt,
    gain,
    weights,
    scales,
    t_first,
    t_ahead,
    t_back,
    t_last,
    out,
    pb,
    g_out,
    u_in,
    v_out,
    f_in,
    feat_q,
    fl,
    ft,
    x1,
    spec,
    m_first,
    m_ahead,
    m_back,
    m_last,
    w,
    gated,
    part_own,
    part_out,
    part_in,
    loc_sem,
    halo_sem,
    send_sem,
    recv_u,
    recv_f,
    recv_p,
):
    me = lax.axis_index("seq")
    mine = lax.axis_index("tensor")
    other = 1 - mine
    chunks = rows // CHUNK
    length = groups * rows
    half = part_own.shape[1]

    load_k = pltpu.make_async_copy(proj, pb.at[:, pl.ds(RIM, rows)], loc_sem.at[0])
    load_k.start()

    barrier = pltpu.get_barrier_semaphore()

    @pl.loop(1, groups)
    def _(step):
        peer = lax.rem(me + step, groups)
        pl.semaphore_signal(barrier, inc=1, device_id=(peer, mine), device_id_type=MESH_ID)

    pl.semaphore_signal(barrier, inc=1, device_id=(me, other), device_id_type=MESH_ID)
    pl.semaphore_wait(barrier, groups)

    def halo(first, count, slot):
        return pltpu.make_async_remote_copy(
            src_ref=proj.at[pl.ds(first, count), pl.ds(rows - RIM, RIM)],
            dst_ref=pb.at[pl.ds(first, count), pl.ds(0, RIM)],
            send_sem=halo_sem.at[slot],
            recv_sem=halo_sem.at[slot + 1],
            device_id=(lax.rem(me + 1, groups), mine),
            device_id_type=MESH_ID,
        )

    halo_kv, halo_q = halo(1, 2, 0), halo(0, 1, 2)

    @pl.when(me < groups - 1)
    def _():
        halo_kv.start()

    @pl.when(me == 0)
    def _():
        pb[:, 0:RIM, :] = jnp.zeros((pb.shape[0], RIM, pb.shape[2]), BF16)

    load_k.wait()
    loads = [
        pltpu.make_async_copy(src, dst, loc_sem.at[1 + i])
        for i, (src, dst) in enumerate(
            (
                (filt, fl),
                (t_first, m_first),
                (t_ahead, m_ahead),
                (t_back, m_back),
                (t_last, m_last),
                (weights, w),
            )
        )
    ]
    for load in loads:
        load.start()

    def featured(p, q, j):
        lanes = pl.ds(pl.multiple_of(j * LANES, LANES), LANES)
        x = pb[p, pl.ds(pl.multiple_of(q * CHUNK, CHUNK), CHUNK + RIM), lanes].astype(F32)
        run = None
        for lag in range(KS):
            term = taps[p, lag : lag + 1, lanes] * x[RIM - lag : RIM - lag + CHUNK]
            run = term if run is None else run + term
        return run.astype(BF16)

    def rows_of(q):
        return pl.ds(pl.multiple_of(q * CHUNK, CHUNK), CHUNK)

    def spread(src, dst, q, recv):
        @pl.loop(1, groups)
        def _(step):
            peer = lax.rem(me + step, groups)
            pltpu.make_async_remote_copy(
                src_ref=src.at[peer, rows_of(q)],
                dst_ref=dst.at[me, rows_of(q)],
                send_sem=send_sem.at[recv],
                recv_sem=(recv_u if recv == 0 else recv_f).at[q],
                device_id=(peer, mine),
                device_id_type=MESH_ID,
            ).start()

        dst[me, rows_of(q), :] = src[me, rows_of(q), :]

    def await_chunk(dst, q, sem):
        view = dst.at[pl.ds(0, groups - 1), rows_of(q)]
        pltpu.make_async_copy(view, view, sem.at[q]).wait()

    def feature_chunk(q):
        @pl.loop(0, groups)
        def _(j):
            k = featured(1, q, j).astype(F32)
            v = featured(2, q, j).astype(F32)
            g_out[j, rows_of(q), :] = (k * v).astype(BF16)

        spread(g_out, u_in, q, 0)

    @pl.loop(1, chunks)
    def _(q):
        feature_chunk(q)

    @pl.when(me > 0)
    def _():
        halo_kv.wait_recv()

    feature_chunk(0)

    @pl.when(me < groups - 1)
    def _():
        halo_q.start()

    loads[0].wait()

    @pl.loop(0, groups, unroll=4)
    def _(a):
        for part in range(rows // LANES):
            start = pl.multiple_of(a * rows + part * LANES, LANES)
            ft[a, part * LANES : (part + 1) * LANES, :] = fl[:, pl.ds(start, LANES)].astype(BF16).T

    for load in loads[1:5]:
        load.wait()

    slabs = x1.shape[0]
    pairs = slabs // 4

    def first_stage(src, s):
        at = pl.ds(pl.multiple_of(s * SUB, SUB), SUB)
        block = src[:, at, :].reshape(groups * SUB, LANES)
        x1[:, at, :] = dot(m_first[s], block).astype(BF16).reshape(slabs, SUB, LANES)

    def pair_of(j):
        left = x1[pl.ds(4 * j, 2)].reshape(2 * rows, LANES)
        right = x1[pl.ds(4 * j + 2, 2)].reshape(2 * rows, LANES)
        return jnp.concatenate([left, right], axis=1)

    @pl.loop(0, rows // SUB, unroll=4)
    def _(s):
        first_stage(ft, s)

    for j in range(pairs):
        spec[j] = dot(m_ahead[...], pair_of(j))

    per_chunk = CHUNK // SUB

    @pl.loop(0, chunks)
    def _(i):
        q = lax.rem(i + 1, chunks)
        await_chunk(u_in, q, recv_u)

        @pl.loop(0, per_chunk, unroll=per_chunk)
        def _(s):
            first_stage(u_in, q * per_chunk + s)

    for j in range(pairs):
        values = dot(m_ahead[...], pair_of(j))
        re_u, im_u = values[:rows], values[rows:]
        re_h, im_h = spec[j, 0:rows, :], spec[j, rows : 2 * rows, :]
        product = jnp.concatenate(
            [re_u * re_h - im_u * im_h, re_u * im_h + im_u * re_h], axis=0
        ).astype(BF16)
        z = dot(m_back[...], product).astype(BF16)
        x1[pl.ds(4 * j, 2)] = z[:, :LANES].reshape(2, rows, LANES)
        x1[pl.ds(4 * j + 2, 2)] = z[:, LANES:].reshape(2, rows, LANES)

    @pl.loop(0, chunks)
    def _(q):
        @pl.loop(0, per_chunk, unroll=per_chunk)
        def _(i):
            s = q * per_chunk + i
            at = pl.ds(pl.multiple_of(s * SUB, SUB), SUB)
            conv = dot(m_last[s], x1[:, at, :].reshape(slabs * SUB, LANES))
            direct = gain[...] * u_in[:, at, :].reshape(groups * SUB, LANES).astype(F32)
            v_out[:, at, :] = (conv + direct).astype(BF16).reshape(groups, SUB, LANES)

        spread(v_out, f_in, q, 1)

    loads[5].wait()
    cuts = w.shape[1] // BLK

    @pl.loop(0, w.shape[0] // BLK)
    def _(b):
        at = pl.ds(pl.multiple_of(b * BLK, BLK), BLK)
        for n in range(cuts):
            cols = slice(n * BLK, (n + 1) * BLK)
            scale = jnp.full((BLK, BLK), scales[b, n], F32).astype(BF16)
            w[at, cols] = w[at, cols] * scale

    @pl.when(me > 0)
    def _():
        halo_q.wait_recv()

    @pl.loop(0, chunks)
    def _(q):
        @pl.loop(0, groups, unroll=4)
        def _(j):
            feat_q[j, rows_of(q), :] = featured(0, q, j)

    def swap(q):
        return pltpu.make_async_remote_copy(
            src_ref=part_out.at[rows_of(q)],
            dst_ref=part_in.at[rows_of(q)],
            send_sem=send_sem.at[2],
            recv_sem=recv_p.at[q],
            device_id=(me, other),
            device_id_type=MESH_ID,
        )

    @pl.loop(0, chunks)
    def _(q):
        await_chunk(f_in, q, recv_f)
        for j in range(groups):
            product = feat_q[j, rows_of(q), :].astype(F32) * f_in[j, rows_of(q), :].astype(F32)
            gated[:, j * LANES : (j + 1) * LANES] = product.astype(BF16)
        theirs = pl.ds(pl.multiple_of(other * half, half), half)
        ours = pl.ds(pl.multiple_of(mine * half, half), half)
        part_out[rows_of(q), :] = dot(gated[...], w[:, theirs]).astype(BF16)
        swap(q).start()
        part_own[rows_of(q), :] = dot(gated[...], w[:, ours]).astype(BF16)

    @pl.loop(0, chunks)
    def _(q):
        swap(q).wait_recv()
        total = part_own[rows_of(q), :].astype(F32) + part_in[rows_of(q), :].astype(F32)
        out[rows_of(q), :] = total.astype(BF16)

    @pl.when(me < groups - 1)
    def _():
        halo_kv.wait_send()
        halo_q.wait_send()

    sent = g_out.at[pl.ds(0, groups - 1)]
    pltpu.make_async_copy(sent, sent, send_sem.at[0]).wait()
    sent = v_out.at[pl.ds(0, groups - 1)]
    pltpu.make_async_copy(sent, sent, send_sem.at[1]).wait()
    pltpu.make_async_copy(part_out, part_out, send_sem.at[2]).wait()


def fused(projected, feat_weight, long_filter, skip_gain, out_values, out_scales):
    groups = lax.axis_size("seq")
    rows, local_ch = projected.shape[1:]
    out_width = out_values.shape[1]
    half = out_width // 2
    tables = dft_tables(groups, rows)
    slabs = tables[0].shape[1] // SUB
    hbm = pl.BlockSpec(memory_space=pl.ANY)
    vmem = pl.BlockSpec(memory_space=pltpu.VMEM)
    smem = pl.BlockSpec(memory_space=pltpu.SMEM)
    block = pltpu.VMEM((groups, rows, LANES), BF16)
    chunks = rows // CHUNK
    return pl.pallas_call(
        functools.partial(fused_kernel, groups, rows),
        out_shape=jax.ShapeDtypeStruct((rows, half), BF16),
        in_specs=[hbm, vmem, hbm, vmem, hbm, smem, hbm, hbm, hbm, hbm],
        out_specs=vmem,
        scratch_shapes=[
            pltpu.VMEM((3, RIM + rows, local_ch), BF16),
            block,
            block,
            block,
            block,
            block,
            pltpu.VMEM(long_filter.shape, F32),
            block,
            pltpu.VMEM((slabs, rows, LANES), BF16),
            pltpu.VMEM((slabs // 4, 2 * rows, 2 * LANES), F32),
            pltpu.VMEM(tables[0].shape, BF16),
            pltpu.VMEM(tables[1].shape, BF16),
            pltpu.VMEM(tables[2].shape, BF16),
            pltpu.VMEM(tables[3].shape, BF16),
            pltpu.VMEM(out_values.shape, BF16),
            pltpu.VMEM((CHUNK, local_ch), BF16),
            pltpu.VMEM((rows, half), BF16),
            pltpu.VMEM((rows, half), BF16),
            pltpu.VMEM((rows, half), BF16),
            pltpu.SemaphoreType.DMA((7,)),
            pltpu.SemaphoreType.DMA((4,)),
            pltpu.SemaphoreType.DMA((3,)),
            pltpu.SemaphoreType.DMA((chunks,)),
            pltpu.SemaphoreType.DMA((chunks,)),
            pltpu.SemaphoreType.DMA((chunks,)),
        ],
        compiler_params=pltpu.CompilerParams(
            collective_id=0, has_side_effects=True, vmem_limit_bytes=58 * 2**20
        ),
        cost_estimate=pl.CostEstimate(
            flops=10 * 10**9, bytes_accessed=32 * 2**20, transcendentals=0
        ),
    )(
        projected,
        feat_weight,
        long_filter,
        skip_gain.reshape(1, -1),
        out_values,
        out_scales,
        *[jnp.asarray(x) for x in tables],
    )


def fits(projected, long_filter, out_values):
    groups = lax.axis_size("seq")
    rows, local_ch = projected.shape[1:]
    return (
        lax.axis_size("tensor") == 2
        and long_filter.shape[0] == LANES
        and local_ch == groups * LANES
        and rows == 2 * LANES
        and groups == SUB
        and out_values.shape[1] % (2 * LANES) == 0
    )


TRIPLE = lax.Precision.HIGH


def passed_along(x, axis, by):
    size = lax.axis_size(axis)
    pairs = [(i, i + by) for i in range(size) if 0 <= i + by < size]
    return lax.ppermute(x, axis, pairs)


def split_length(whole):
    for candidate in range(2, whole + 1, 2):
        if whole % candidate == 0 and candidate * candidate >= whole:
            return (candidate, whole // candidate)
    return (whole, 1)


def angle_pair(row_count, col_count, period):
    row_ids = lax.broadcasted_iota(jnp.int32, (row_count, col_count), 0)
    col_ids = lax.broadcasted_iota(jnp.int32, (row_count, col_count), 1)
    angles = (row_ids * col_ids % period).astype(jnp.float32) * (2.0 * math.pi / period)
    return (jnp.cos(angles), jnp.sin(angles))


def make_tables(length):
    whole = 2 * length
    size_a, size_b = split_length(whole)
    return (
        angle_pair(size_a, size_a, size_a),
        angle_pair(size_b, size_b, size_b),
        angle_pair(size_a, size_b, whole),
        size_a,
        size_b,
    )


def right_mul(signal, matrix):
    return jnp.einsum("ckn,nm->ckm", signal, matrix, precision=TRIPLE)


def forward(signal, tables):
    (cos_a, sin_a), (cos_b, sin_b), (cos_t, sin_t), size_a, size_b = tables
    half_a = size_a // 2
    blocks = signal.reshape(signal.shape[0], half_a, size_b)
    real_a = jnp.einsum("kn,cnb->ckb", cos_a[:, :half_a], blocks, precision=TRIPLE)
    imag_a = -jnp.einsum("kn,cnb->ckb", sin_a[:, :half_a], blocks, precision=TRIPLE)
    real_t = real_a * cos_t + imag_a * sin_t
    imag_t = imag_a * cos_t - real_a * sin_t
    real_f = right_mul(real_t, cos_b) + right_mul(imag_t, sin_b)
    imag_f = right_mul(imag_t, cos_b) - right_mul(real_t, sin_b)
    return (real_f, imag_f)


def inverse(real_f, imag_f, tables):
    (cos_a, sin_a), (cos_b, sin_b), (cos_t, sin_t), size_a, size_b = tables
    half_a = size_a // 2
    real_z = right_mul(real_f, cos_b) - right_mul(imag_f, sin_b)
    imag_z = right_mul(imag_f, cos_b) + right_mul(real_f, sin_b)
    real_w = real_z * cos_t - imag_z * sin_t
    imag_w = imag_z * cos_t + real_z * sin_t
    out_half = jnp.einsum("nk,ckb->cnb", cos_a[:half_a, :], real_w, precision=TRIPLE) - jnp.einsum(
        "nk,ckb->cnb", sin_a[:half_a, :], imag_w, precision=TRIPLE
    )
    return out_half.reshape(out_half.shape[0], half_a * size_b) * (1.0 / (size_a * size_b))


def long_mix(gated_kv, spectrum, own_gain, tables):
    kv_values = gated_kv.astype(jnp.float32)
    real_u, imag_u = forward(kv_values, tables)
    real_h, imag_h = spectrum
    real_p = real_u * real_h - imag_u * imag_h
    imag_p = real_u * imag_h + imag_u * real_h
    convolved = inverse(real_p, imag_p, tables)
    return (convolved + own_gain[:, None] * kv_values).astype(jnp.bfloat16)


def featurize(extended, weights, length):
    tap_count = weights.shape[1]
    running = jnp.zeros(extended.shape[:2] + (length,), jnp.float32)
    for lag_idx in range(tap_count):
        offset = tap_count - 1 - lag_idx
        running = running + weights[:, lag_idx, :, None] * extended[
            :, :, offset : offset + length
        ].astype(jnp.float32)
    return running.astype(jnp.bfloat16)


def multiply_round(left_arr, right_arr):
    return (left_arr.astype(jnp.float32) * right_arr.astype(jnp.float32)).astype(jnp.bfloat16)


def local(projected, feat_weight, long_filter, skip_gain, out_values, out_scales):
    if fits(projected, long_filter, out_values):
        return fused(projected, feat_weight, long_filter, skip_gain, out_values, out_scales)
    groups = lax.axis_size("seq")
    tok_rows = projected.shape[1]
    local_ch = projected.shape[2]
    length = tok_rows * groups
    tables = make_tables(length)
    spectrum = forward(long_filter, tables)
    columns = jnp.transpose(projected, (0, 2, 1))
    rim_width = KS - 1
    prior_rows = passed_along(columns[:, :, tok_rows - rim_width :], "seq", 1)
    featured = featurize(jnp.concatenate([prior_rows, columns], axis=2), feat_weight, tok_rows)
    regrouped = lax.all_to_all(featured, "seq", split_axis=1, concat_axis=2, tiled=True)
    gated_kv = multiply_round(regrouped[1], regrouped[2])
    filtered = long_mix(gated_kv, spectrum, skip_gain, tables)
    gated = multiply_round(regrouped[0], filtered)
    gated_home = lax.all_to_all(gated, "seq", split_axis=1, concat_axis=0, tiled=True)
    block_count = local_ch // BLK
    out_width = out_values.shape[1]
    stacked = gated_home.reshape(block_count, BLK, tok_rows)
    weight_blocks = out_values.reshape(block_count, BLK, out_width)
    scale_cols = jnp.repeat(out_scales, BLK, axis=1)
    products = jnp.einsum(
        "bkn,bkt->bnt", weight_blocks, stacked, preferred_element_type=jnp.float32
    )
    summed = lax.psum_scatter(
        jnp.sum(products * scale_cols[:, :, None], axis=0).astype(jnp.bfloat16),
        "tensor",
        scatter_dimension=0,
        tiled=True,
    )
    return jnp.transpose(summed, (1, 0))


def solution(mesh):
    return jax.shard_map(
        local,
        mesh=mesh,
        in_specs=(
            P(None, "seq", "tensor"),
            P(None, None, "tensor"),
            P(("tensor", "seq"), None),
            P(("tensor", "seq")),
            P("tensor", None),
            P("tensor", None),
        ),
        out_specs=P("seq", "tensor"),
        check_vma=False,
    )
```

```python
import functools
import math

import jax
import jax.numpy as jnp
import ml_dtypes
import numpy as np
from jax import lax
from jax.experimental import pallas as pl
from jax.experimental.pallas import tpu as pltpu
from jax.sharding import PartitionSpec as P

KS = 7
BLK = 128
LANES = 128
RIM = 16
SUB = 16
CHUNK = 64
MESH_ID = pl.DeviceIdType.MESH
BF16 = jnp.bfloat16
F32 = jnp.float32


def dft_tables(groups, rows):
    whole = 2 * groups * rows
    kept = groups + 1
    padded = kept + kept % 2
    n_a = np.arange(groups)
    k_a = np.arange(kept)
    r = np.arange(rows)
    turns = k_a[:, None, None] * (n_a[None, :, None] * rows + r[None, None, :]) % whole
    angles = turns * (2.0 * np.pi / whole)
    parts = np.stack([np.cos(angles), -np.sin(angles)], axis=1)
    blocks = parts.reshape(kept, 2, groups, rows // SUB, SUB)
    first = np.zeros((rows // SUB, padded, 2, SUB, groups, SUB))
    last = np.zeros((rows // SUB, groups, SUB, padded, 2, SUB))
    weight = np.full((kept,), 2.0 / whole)
    weight[0] = weight[-1] = 1.0 / whole
    for lo in range(SUB):
        cut = blocks[:, :, :, :, lo]
        first[:, :kept, :, lo, :, lo] = cut.transpose(3, 0, 1, 2)
        last[:, :, lo, :kept, :, lo] = (cut * weight[:, None, None, None]).transpose(3, 2, 0, 1)
    first = first.reshape(rows // SUB, padded * 2 * SUB, groups * SUB)
    last = last.reshape(rows // SUB, groups * SUB, padded * 2 * SUB)
    inner = (r[:, None] * r[None, :] % rows) * (2.0 * np.pi / rows)
    cos, sin = np.cos(inner), np.sin(inner)
    ahead = np.block([[cos, sin], [-sin, cos]])
    back = np.block([[cos, -sin], [sin, cos]])
    return [x.astype(ml_dtypes.bfloat16) for x in (first, ahead, back, last)]


def return_pieces(rows):
    sizes = [CHUNK] * (rows // CHUNK - 1) + [CHUNK // 2] * 2
    return [(sum(sizes[:i]), size) for i, size in enumerate(sizes)]


def dot(a, b):
    return jnp.dot(a, b, preferred_element_type=F32)


def fused_kernel(
    groups,
    rows,
    proj,
    taps_hbm,
    filt,
    gain,
    weights,
    scales,
    t_first,
    t_ahead,
    t_back,
    t_last,
    out,
    pb,
    taps,
    rim_out,
    rim_in,
    g_out,
    u_in,
    v_out,
    f_in,
    feat_q,
    fl,
    ft,
    x1,
    spec,
    m_first,
    m_ahead,
    m_back,
    m_last,
    w,
    gated,
    part_own,
    part_out,
    part_in,
    loc_sem,
    halo_sem,
    send_sem,
    recv_u,
    recv_f,
    recv_p,
):
    me = lax.axis_index("seq")
    mine = lax.axis_index("tensor")
    other = 1 - mine
    chunks = rows // CHUNK
    length = groups * rows
    half = part_own.shape[1]

    load_k = pltpu.make_async_copy(proj, pb.at[:, pl.ds(RIM, rows)], loc_sem.at[0])
    load_k.start()
    load_taps = pltpu.make_async_copy(taps_hbm, taps, loc_sem.at[7])
    load_taps.start()

    barrier = pltpu.get_barrier_semaphore()

    @pl.loop(1, groups)
    def _(step):
        peer = lax.rem(me + step, groups)
        pl.semaphore_signal(barrier, inc=1, device_id=(peer, mine), device_id_type=MESH_ID)

    pl.semaphore_signal(barrier, inc=1, device_id=(me, other), device_id_type=MESH_ID)
    pl.semaphore_wait(barrier, groups)

    def halo(src, dst, slot):
        return pltpu.make_async_remote_copy(
            src_ref=src,
            dst_ref=dst,
            send_sem=halo_sem.at[slot],
            recv_sem=halo_sem.at[slot + 1],
            device_id=(lax.rem(me + 1, groups), mine),
            device_id_type=MESH_ID,
        )

    halo_kv = halo(rim_out, rim_in, 0)
    halo_q = halo(proj.at[0, pl.ds(rows - RIM, RIM)], pb.at[0, pl.ds(0, RIM)], 2)

    @pl.when(me == 0)
    def _():
        pb[:, 0:RIM, :] = jnp.zeros((pb.shape[0], RIM, pb.shape[2]), BF16)

    load_k.wait()
    few = RIM // 2

    @pl.when(me < groups - 1)
    def _():
        ends = [pb[p, rows : rows + RIM, :].astype(F32)[few:] for p in (1, 2)]
        rim_out[...] = jnp.concatenate(ends, axis=0).astype(BF16)
        halo_kv.start()

    load_taps.wait()
    loads = [
        pltpu.make_async_copy(src, dst, loc_sem.at[1 + i])
        for i, (src, dst) in enumerate(
            (
                (filt, fl),
                (t_first, m_first),
                (t_ahead, m_ahead),
                (t_back, m_back),
                (t_last, m_last),
                (weights, w),
            )
        )
    ]
    for load in loads:
        load.start()

    def featured(p, q, j):
        lanes = pl.ds(pl.multiple_of(j * LANES, LANES), LANES)
        x = pb[p, pl.ds(pl.multiple_of(q * CHUNK, CHUNK), CHUNK + RIM), lanes].astype(F32)
        run = None
        for lag in range(KS):
            term = taps[p, lag : lag + 1, lanes] * x[RIM - lag : RIM - lag + CHUNK]
            run = term if run is None else run + term
        return run.astype(BF16)

    def rows_of(q):
        return pl.ds(pl.multiple_of(q * CHUNK, CHUNK), CHUNK)

    def spread(src, dst, at, q, recv):
        @pl.loop(1, groups)
        def _(step):
            peer = lax.rem(me + step, groups)
            pltpu.make_async_remote_copy(
                src_ref=src.at[peer, at],
                dst_ref=dst.at[me, at],
                send_sem=send_sem.at[recv],
                recv_sem=(recv_u if recv == 0 else recv_f).at[q],
                device_id=(peer, mine),
                device_id_type=MESH_ID,
            ).start()

        dst[me, at, :] = src[me, at, :]

    def await_chunk(dst, at, q, sem):
        view = dst.at[pl.ds(0, groups - 1), at]
        pltpu.make_async_copy(view, view, sem.at[q]).wait()

    def feature_chunk(q):
        @pl.loop(0, groups)
        def _(j):
            k = featured(1, q, j).astype(F32)
            v = featured(2, q, j).astype(F32)
            g_out[j, rows_of(q), :] = (k * v).astype(BF16)

        spread(g_out, u_in, rows_of(q), q, 0)

    @pl.loop(1, chunks)
    def _(q):
        feature_chunk(q)

    @pl.when(me > 0)
    def _():
        halo_kv.wait_recv()
        both = rim_in[...].astype(F32)
        blank = jnp.zeros((few, pb.shape[2]), F32)
        for p in (1, 2):
            own = both[(p - 1) * few : p * few]
            pb[p, 0:RIM, :] = jnp.concatenate([blank, own], axis=0).astype(BF16)

    feature_chunk(0)

    loads[0].wait()

    @pl.loop(0, groups, unroll=4)
    def _(a):
        for part in range(rows // LANES):
            start = pl.multiple_of(a * rows + part * LANES, LANES)
            ft[a, part * LANES : (part + 1) * LANES, :] = fl[:, pl.ds(start, LANES)].astype(BF16).T

    for load in loads[1:5]:
        load.wait()

    slabs = x1.shape[0]
    pairs = slabs // 4

    def first_stage(src, s):
        at = pl.ds(pl.multiple_of(s * SUB, SUB), SUB)
        block = src[:, at, :].reshape(groups * SUB, LANES)
        x1[:, at, :] = dot(m_first[s], block).astype(BF16).reshape(slabs, SUB, LANES)

    def pair_of(j):
        left = x1[pl.ds(4 * j, 2)].reshape(2 * rows, LANES)
        right = x1[pl.ds(4 * j + 2, 2)].reshape(2 * rows, LANES)
        return jnp.concatenate([left, right], axis=1)

    @pl.loop(0, rows // SUB, unroll=4)
    def _(s):
        first_stage(ft, s)

    for j in range(pairs):
        spec[j] = dot(m_ahead[...], pair_of(j))

    per_chunk = CHUNK // SUB

    @pl.loop(0, chunks)
    def _(i):
        q = lax.rem(i + 1, chunks)
        await_chunk(u_in, rows_of(q), q, recv_u)

        @pl.loop(0, per_chunk, unroll=per_chunk)
        def _(s):
            first_stage(u_in, q * per_chunk + s)

    @pl.when(me < groups - 1)
    def _():
        halo_q.start()

    for j in range(pairs):
        values = dot(m_ahead[...], pair_of(j))
        re_u, im_u = values[:rows], values[rows:]
        re_h, im_h = spec[j, 0:rows, :], spec[j, rows : 2 * rows, :]
        product = jnp.concatenate(
            [re_u * re_h - im_u * im_h, re_u * im_h + im_u * re_h], axis=0
        ).astype(BF16)
        z = dot(m_back[...], product).astype(BF16)
        x1[pl.ds(4 * j, 2)] = z[:, :LANES].reshape(2, rows, LANES)
        x1[pl.ds(4 * j + 2, 2)] = z[:, LANES:].reshape(2, rows, LANES)

    pieces = return_pieces(rows)
    for q, (start, count) in enumerate(pieces):
        for s in range(start // SUB, (start + count) // SUB):
            at = pl.ds(s * SUB, SUB)
            conv = dot(m_last[s], x1[:, at, :].reshape(slabs * SUB, LANES))
            direct = gain[...] * u_in[:, at, :].reshape(groups * SUB, LANES).astype(F32)
            v_out[:, at, :] = (conv + direct).astype(BF16).reshape(groups, SUB, LANES)
        spread(v_out, f_in, pl.ds(start, count), q, 1)

    loads[5].wait()
    cuts = w.shape[1] // BLK

    @pl.loop(0, w.shape[0] // BLK)
    def _(b):
        at = pl.ds(pl.multiple_of(b * BLK, BLK), BLK)
        for n in range(cuts):
            cols = slice(n * BLK, (n + 1) * BLK)
            scale = jnp.full((BLK, BLK), scales[b, n], F32).astype(BF16)
            w[at, cols] = w[at, cols] * scale

    @pl.when(me > 0)
    def _():
        halo_q.wait_recv()

    @pl.loop(0, chunks)
    def _(q):
        @pl.loop(0, groups, unroll=4)
        def _(j):
            feat_q[j, rows_of(q), :] = featured(0, q, j)

    def swap(q, at):
        return pltpu.make_async_remote_copy(
            src_ref=part_out.at[at],
            dst_ref=part_in.at[at],
            send_sem=send_sem.at[2],
            recv_sem=recv_p.at[q],
            device_id=(me, other),
            device_id_type=MESH_ID,
        )

    theirs = pl.ds(pl.multiple_of(other * half, half), half)
    ours = pl.ds(pl.multiple_of(mine * half, half), half)
    for q, (start, count) in enumerate(pieces):
        at = pl.ds(start, count)
        await_chunk(f_in, at, q, recv_f)
        for j in range(groups):
            product = feat_q[j, at, :].astype(F32) * f_in[j, at, :].astype(F32)
            gated[0:count, j * LANES : (j + 1) * LANES] = product.astype(BF16)
        part_out[at, :] = dot(gated[0:count, :], w[:, theirs]).astype(BF16)
        swap(q, at).start()
        part_own[at, :] = dot(gated[0:count, :], w[:, ours]).astype(BF16)

    for q, (start, count) in enumerate(pieces):
        at = pl.ds(start, count)
        swap(q, at).wait_recv()
        total = part_own[at, :].astype(F32) + part_in[at, :].astype(F32)
        out[at, :] = total.astype(BF16)

    @pl.when(me < groups - 1)
    def _():
        halo_kv.wait_send()
        halo_q.wait_send()

    sent = g_out.at[pl.ds(0, groups - 1)]
    pltpu.make_async_copy(sent, sent, send_sem.at[0]).wait()
    sent = v_out.at[pl.ds(0, groups - 1)]
    pltpu.make_async_copy(sent, sent, send_sem.at[1]).wait()
    pltpu.make_async_copy(part_out, part_out, send_sem.at[2]).wait()


def fused(projected, feat_weight, long_filter, skip_gain, out_values, out_scales):
    groups = lax.axis_size("seq")
    rows, local_ch = projected.shape[1:]
    out_width = out_values.shape[1]
    half = out_width // 2
    tables = dft_tables(groups, rows)
    slabs = tables[0].shape[1] // SUB
    hbm = pl.BlockSpec(memory_space=pl.ANY)
    vmem = pl.BlockSpec(memory_space=pltpu.VMEM)
    smem = pl.BlockSpec(memory_space=pltpu.SMEM)
    block = pltpu.VMEM((groups, rows, LANES), BF16)
    chunks = rows // CHUNK
    return pl.pallas_call(
        functools.partial(fused_kernel, groups, rows),
        out_shape=jax.ShapeDtypeStruct((rows, half), BF16),
        in_specs=[hbm, hbm, hbm, vmem, hbm, smem, hbm, hbm, hbm, hbm],
        out_specs=vmem,
        scratch_shapes=[
            pltpu.VMEM((3, RIM + rows, local_ch), BF16),
            pltpu.VMEM(feat_weight.shape, F32),
            pltpu.VMEM((RIM, local_ch), BF16),
            pltpu.VMEM((RIM, local_ch), BF16),
            block,
            block,
            block,
            block,
            block,
            pltpu.VMEM(long_filter.shape, F32),
            block,
            pltpu.VMEM((slabs, rows, LANES), BF16),
            pltpu.VMEM((slabs // 4, 2 * rows, 2 * LANES), F32),
            pltpu.VMEM(tables[0].shape, BF16),
            pltpu.VMEM(tables[1].shape, BF16),
            pltpu.VMEM(tables[2].shape, BF16),
            pltpu.VMEM(tables[3].shape, BF16),
            pltpu.VMEM(out_values.shape, BF16),
            pltpu.VMEM((CHUNK, local_ch), BF16),
            pltpu.VMEM((rows, half), BF16),
            pltpu.VMEM((rows, half), BF16),
            pltpu.VMEM((rows, half), BF16),
            pltpu.SemaphoreType.DMA((8,)),
            pltpu.SemaphoreType.DMA((4,)),
            pltpu.SemaphoreType.DMA((3,)),
            pltpu.SemaphoreType.DMA((chunks,)),
            pltpu.SemaphoreType.DMA((len(return_pieces(rows)),)),
            pltpu.SemaphoreType.DMA((len(return_pieces(rows)),)),
        ],
        compiler_params=pltpu.CompilerParams(
            collective_id=0, has_side_effects=True, vmem_limit_bytes=58 * 2**20
        ),
        cost_estimate=pl.CostEstimate(
            flops=10 * 10**9, bytes_accessed=32 * 2**20, transcendentals=0
        ),
    )(
        projected,
        feat_weight,
        long_filter,
        skip_gain.reshape(1, -1),
        out_values,
        out_scales,
        *[jnp.asarray(x) for x in tables],
    )


def fits(projected, long_filter, out_values):
    groups = lax.axis_size("seq")
    rows, local_ch = projected.shape[1:]
    return (
        lax.axis_size("tensor") == 2
        and long_filter.shape[0] == LANES
        and local_ch == groups * LANES
        and rows == 2 * LANES
        and groups == SUB
        and out_values.shape[1] % (2 * LANES) == 0
    )


TRIPLE = lax.Precision.HIGH


def passed_along(x, axis, by):
    size = lax.axis_size(axis)
    pairs = [(i, i + by) for i in range(size) if 0 <= i + by < size]
    return lax.ppermute(x, axis, pairs)


def split_length(whole):
    for candidate in range(2, whole + 1, 2):
        if whole % candidate == 0 and candidate * candidate >= whole:
            return (candidate, whole // candidate)
    return (whole, 1)


def angle_pair(row_count, col_count, period):
    row_ids = lax.broadcasted_iota(jnp.int32, (row_count, col_count), 0)
    col_ids = lax.broadcasted_iota(jnp.int32, (row_count, col_count), 1)
    angles = (row_ids * col_ids % period).astype(jnp.float32) * (2.0 * math.pi / period)
    return (jnp.cos(angles), jnp.sin(angles))


def make_tables(length):
    whole = 2 * length
    size_a, size_b = split_length(whole)
    return (
        angle_pair(size_a, size_a, size_a),
        angle_pair(size_b, size_b, size_b),
        angle_pair(size_a, size_b, whole),
        size_a,
        size_b,
    )


def right_mul(signal, matrix):
    return jnp.einsum("ckn,nm->ckm", signal, matrix, precision=TRIPLE)


def forward(signal, tables):
    (cos_a, sin_a), (cos_b, sin_b), (cos_t, sin_t), size_a, size_b = tables
    half_a = size_a // 2
    blocks = signal.reshape(signal.shape[0], half_a, size_b)
    real_a = jnp.einsum("kn,cnb->ckb", cos_a[:, :half_a], blocks, precision=TRIPLE)
    imag_a = -jnp.einsum("kn,cnb->ckb", sin_a[:, :half_a], blocks, precision=TRIPLE)
    real_t = real_a * cos_t + imag_a * sin_t
    imag_t = imag_a * cos_t - real_a * sin_t
    real_f = right_mul(real_t, cos_b) + right_mul(imag_t, sin_b)
    imag_f = right_mul(imag_t, cos_b) - right_mul(real_t, sin_b)
    return (real_f, imag_f)


def inverse(real_f, imag_f, tables):
    (cos_a, sin_a), (cos_b, sin_b), (cos_t, sin_t), size_a, size_b = tables
    half_a = size_a // 2
    real_z = right_mul(real_f, cos_b) - right_mul(imag_f, sin_b)
    imag_z = right_mul(imag_f, cos_b) + right_mul(real_f, sin_b)
    real_w = real_z * cos_t - imag_z * sin_t
    imag_w = imag_z * cos_t + real_z * sin_t
    out_half = jnp.einsum("nk,ckb->cnb", cos_a[:half_a, :], real_w, precision=TRIPLE) - jnp.einsum(
        "nk,ckb->cnb", sin_a[:half_a, :], imag_w, precision=TRIPLE
    )
    return out_half.reshape(out_half.shape[0], half_a * size_b) * (1.0 / (size_a * size_b))


def long_mix(gated_kv, spectrum, own_gain, tables):
    kv_values = gated_kv.astype(jnp.float32)
    real_u, imag_u = forward(kv_values, tables)
    real_h, imag_h = spectrum
    real_p = real_u * real_h - imag_u * imag_h
    imag_p = real_u * imag_h + imag_u * real_h
    convolved = inverse(real_p, imag_p, tables)
    return (convolved + own_gain[:, None] * kv_values).astype(jnp.bfloat16)


def featurize(extended, weights, length):
    tap_count = weights.shape[1]
    running = jnp.zeros(extended.shape[:2] + (length,), jnp.float32)
    for lag_idx in range(tap_count):
        offset = tap_count - 1 - lag_idx
        running = running + weights[:, lag_idx, :, None] * extended[
            :, :, offset : offset + length
        ].astype(jnp.float32)
    return running.astype(jnp.bfloat16)


def multiply_round(left_arr, right_arr):
    return (left_arr.astype(jnp.float32) * right_arr.astype(jnp.float32)).astype(jnp.bfloat16)


def local(projected, feat_weight, long_filter, skip_gain, out_values, out_scales):
    if fits(projected, long_filter, out_values):
        return fused(projected, feat_weight, long_filter, skip_gain, out_values, out_scales)
    groups = lax.axis_size("seq")
    tok_rows = projected.shape[1]
    local_ch = projected.shape[2]
    length = tok_rows * groups
    tables = make_tables(length)
    spectrum = forward(long_filter, tables)
    columns = jnp.transpose(projected, (0, 2, 1))
    rim_width = KS - 1
    prior_rows = passed_along(columns[:, :, tok_rows - rim_width :], "seq", 1)
    featured = featurize(jnp.concatenate([prior_rows, columns], axis=2), feat_weight, tok_rows)
    regrouped = lax.all_to_all(featured, "seq", split_axis=1, concat_axis=2, tiled=True)
    gated_kv = multiply_round(regrouped[1], regrouped[2])
    filtered = long_mix(gated_kv, spectrum, skip_gain, tables)
    gated = multiply_round(regrouped[0], filtered)
    gated_home = lax.all_to_all(gated, "seq", split_axis=1, concat_axis=0, tiled=True)
    block_count = local_ch // BLK
    out_width = out_values.shape[1]
    stacked = gated_home.reshape(block_count, BLK, tok_rows)
    weight_blocks = out_values.reshape(block_count, BLK, out_width)
    scale_cols = jnp.repeat(out_scales, BLK, axis=1)
    products = jnp.einsum(
        "bkn,bkt->bnt", weight_blocks, stacked, preferred_element_type=jnp.float32
    )
    summed = lax.psum_scatter(
        jnp.sum(products * scale_cols[:, :, None], axis=0).astype(jnp.bfloat16),
        "tensor",
        scatter_dimension=0,
        tiled=True,
    )
    return jnp.transpose(summed, (1, 0))


def solution(mesh):
    return jax.shard_map(
        local,
        mesh=mesh,
        in_specs=(
            P(None, "seq", "tensor"),
            P(None, None, "tensor"),
            P(("tensor", "seq"), None),
            P(("tensor", "seq")),
            P("tensor", None),
            P("tensor", None),
        ),
        out_specs=P("seq", "tensor"),
        check_vma=False,
    )
```

```python
import functools
import math

import jax
import jax.numpy as jnp
import ml_dtypes
import numpy as np
from jax import lax
from jax.experimental import pallas as pl
from jax.experimental.pallas import tpu as pltpu
from jax.sharding import PartitionSpec as P

KS = 7
BLK = 128
LANES = 128
RIM = 16
SUB = 16
CHUNK = 64
MESH_ID = pl.DeviceIdType.MESH
BF16 = jnp.bfloat16
F32 = jnp.float32


def dft_tables(groups, rows):
    whole = 2 * groups * rows
    kept = groups + 1
    padded = kept + kept % 2
    n_a = np.arange(groups)
    k_a = np.arange(kept)
    r = np.arange(rows)
    turns = k_a[:, None, None] * (n_a[None, :, None] * rows + r[None, None, :]) % whole
    angles = turns * (2.0 * np.pi / whole)
    parts = np.stack([np.cos(angles), -np.sin(angles)], axis=1)
    blocks = parts.reshape(kept, 2, groups, rows // SUB, SUB)
    first = np.zeros((rows // SUB, padded, 2, SUB, groups, SUB))
    last = np.zeros((rows // SUB, groups, SUB, padded, 2, SUB))
    weight = np.full((kept,), 2.0 / whole)
    weight[0] = weight[-1] = 1.0 / whole
    for lo in range(SUB):
        cut = blocks[:, :, :, :, lo]
        first[:, :kept, :, lo, :, lo] = cut.transpose(3, 0, 1, 2)
        last[:, :, lo, :kept, :, lo] = (cut * weight[:, None, None, None]).transpose(3, 2, 0, 1)
    first = first.reshape(rows // SUB, padded * 2 * SUB, groups * SUB)
    last = last.reshape(rows // SUB, groups * SUB, padded * 2 * SUB)
    inner = (r[:, None] * r[None, :] % rows) * (2.0 * np.pi / rows)
    cos, sin = np.cos(inner), np.sin(inner)
    ahead = np.block([[cos, sin], [-sin, cos]])
    back = np.block([[cos, -sin], [sin, cos]])
    return [x.astype(ml_dtypes.bfloat16) for x in (first, ahead, back, last)]


def return_pieces(rows):
    return [(start, CHUNK) for start in range(0, rows, CHUNK)]


def projected_pieces(rows):
    return [(0, rows // 2)] + [(start, CHUNK) for start in range(rows // 2, rows, CHUNK)]


def dot(a, b):
    return jnp.dot(a, b, preferred_element_type=F32)


def fused_kernel(
    groups,
    rows,
    proj,
    taps_hbm,
    filt,
    gain,
    weights,
    scales,
    t_first,
    t_ahead,
    t_back,
    t_last,
    out,
    pb,
    taps,
    rim_out,
    rim_in,
    g_out,
    u_in,
    v_out,
    f_in,
    feat_q,
    fl,
    ft,
    x1,
    spec,
    m_first,
    m_ahead,
    m_back,
    m_last,
    w,
    gated,
    part_own,
    part_out,
    part_in,
    loc_sem,
    halo_sem,
    send_sem,
    recv_u,
    recv_f,
    recv_p,
):
    me = lax.axis_index("seq")
    mine = lax.axis_index("tensor")
    other = 1 - mine
    chunks = rows // CHUNK
    length = groups * rows
    half = part_own.shape[1]

    load_k = pltpu.make_async_copy(proj, pb.at[:, pl.ds(RIM, rows)], loc_sem.at[0])
    load_k.start()
    load_taps = pltpu.make_async_copy(taps_hbm, taps, loc_sem.at[7])
    load_taps.start()

    barrier = pltpu.get_barrier_semaphore()

    @pl.loop(1, groups)
    def _(step):
        peer = lax.rem(me + step, groups)
        pl.semaphore_signal(barrier, inc=1, device_id=(peer, mine), device_id_type=MESH_ID)

    pl.semaphore_signal(barrier, inc=1, device_id=(me, other), device_id_type=MESH_ID)
    pl.semaphore_wait(barrier, groups)

    def halo(src, dst, slot):
        return pltpu.make_async_remote_copy(
            src_ref=src,
            dst_ref=dst,
            send_sem=halo_sem.at[slot],
            recv_sem=halo_sem.at[slot + 1],
            device_id=(lax.rem(me + 1, groups), mine),
            device_id_type=MESH_ID,
        )

    halo_kv = halo(rim_out, rim_in, 0)
    halo_q = halo(proj.at[0, pl.ds(rows - RIM, RIM)], pb.at[0, pl.ds(0, RIM)], 2)

    @pl.when(me == 0)
    def _():
        pb[:, 0:RIM, :] = jnp.zeros((pb.shape[0], RIM, pb.shape[2]), BF16)

    load_k.wait()
    few = RIM // 2

    @pl.when(me < groups - 1)
    def _():
        ends = [pb[p, rows : rows + RIM, :].astype(F32)[few:] for p in (1, 2)]
        rim_out[...] = jnp.concatenate(ends, axis=0).astype(BF16)
        halo_kv.start()

    load_taps.wait()
    loads = [
        pltpu.make_async_copy(src, dst, loc_sem.at[1 + i])
        for i, (src, dst) in enumerate(
            (
                (filt, fl),
                (t_first, m_first),
                (t_ahead, m_ahead),
                (t_back, m_back),
                (t_last, m_last),
                (weights, w),
            )
        )
    ]
    for load in loads:
        load.start()

    def featured(p, q, j):
        lanes = pl.ds(pl.multiple_of(j * LANES, LANES), LANES)
        x = pb[p, pl.ds(pl.multiple_of(q * CHUNK, CHUNK), CHUNK + RIM), lanes].astype(F32)
        run = None
        for lag in range(KS):
            term = taps[p, lag : lag + 1, lanes] * x[RIM - lag : RIM - lag + CHUNK]
            run = term if run is None else run + term
        return run.astype(BF16)

    def rows_of(q):
        return pl.ds(pl.multiple_of(q * CHUNK, CHUNK), CHUNK)

    def spread(src, dst, at, q, recv):
        @pl.loop(1, groups)
        def _(step):
            peer = lax.rem(me + step, groups)
            pltpu.make_async_remote_copy(
                src_ref=src.at[peer, at],
                dst_ref=dst.at[me, at],
                send_sem=send_sem.at[recv],
                recv_sem=(recv_u if recv == 0 else recv_f).at[q],
                device_id=(peer, mine),
                device_id_type=MESH_ID,
            ).start()

        dst[me, at, :] = src[me, at, :]

    def await_chunk(dst, at, q, sem):
        view = dst.at[pl.ds(0, groups - 1), at]
        pltpu.make_async_copy(view, view, sem.at[q]).wait()

    def feature_chunk(q):
        @pl.loop(0, groups)
        def _(j):
            k = featured(1, q, j).astype(F32)
            v = featured(2, q, j).astype(F32)
            g_out[j, rows_of(q), :] = (k * v).astype(BF16)

        spread(g_out, u_in, rows_of(q), q, 0)

    @pl.loop(1, chunks)
    def _(q):
        feature_chunk(q)

    @pl.when(me > 0)
    def _():
        halo_kv.wait_recv()
        both = rim_in[...].astype(F32)
        blank = jnp.zeros((few, pb.shape[2]), F32)
        for p in (1, 2):
            own = both[(p - 1) * few : p * few]
            pb[p, 0:RIM, :] = jnp.concatenate([blank, own], axis=0).astype(BF16)

    feature_chunk(0)

    loads[0].wait()

    @pl.loop(0, groups, unroll=4)
    def _(a):
        for part in range(rows // LANES):
            start = pl.multiple_of(a * rows + part * LANES, LANES)
            ft[a, part * LANES : (part + 1) * LANES, :] = fl[:, pl.ds(start, LANES)].astype(BF16).T

    for load in loads[1:5]:
        load.wait()

    slabs = x1.shape[0]
    pairs = slabs // 4

    def first_stage(src, s):
        at = pl.ds(pl.multiple_of(s * SUB, SUB), SUB)
        block = src[:, at, :].reshape(groups * SUB, LANES)
        x1[:, at, :] = dot(m_first[s], block).astype(BF16).reshape(slabs, SUB, LANES)

    def pair_of(j):
        left = x1[pl.ds(4 * j, 2)].reshape(2 * rows, LANES)
        right = x1[pl.ds(4 * j + 2, 2)].reshape(2 * rows, LANES)
        return jnp.concatenate([left, right], axis=1)

    @pl.loop(0, rows // SUB, unroll=4)
    def _(s):
        first_stage(ft, s)

    for j in range(pairs):
        spec[j] = dot(m_ahead[...], pair_of(j))

    loads[5].wait()
    cuts = w.shape[1] // BLK

    @pl.loop(0, w.shape[0] // BLK)
    def _(b):
        at = pl.ds(pl.multiple_of(b * BLK, BLK), BLK)
        for n in range(cuts):
            cols = slice(n * BLK, (n + 1) * BLK)
            scale = jnp.full((BLK, BLK), scales[b, n], F32).astype(BF16)
            w[at, cols] = w[at, cols] * scale

    per_chunk = CHUNK // SUB

    @pl.loop(0, chunks)
    def _(i):
        q = lax.rem(i + 1, chunks)
        await_chunk(u_in, rows_of(q), q, recv_u)

        @pl.loop(0, per_chunk, unroll=per_chunk)
        def _(s):
            first_stage(u_in, q * per_chunk + s)

    @pl.when(me < groups - 1)
    def _():
        halo_q.start()

    for j in range(pairs):
        values = dot(m_ahead[...], pair_of(j))
        re_u, im_u = values[:rows], values[rows:]
        re_h, im_h = spec[j, 0:rows, :], spec[j, rows : 2 * rows, :]
        product = jnp.concatenate(
            [re_u * re_h - im_u * im_h, re_u * im_h + im_u * re_h], axis=0
        ).astype(BF16)
        z = dot(m_back[...], product).astype(BF16)
        x1[pl.ds(4 * j, 2)] = z[:, :LANES].reshape(2, rows, LANES)
        x1[pl.ds(4 * j + 2, 2)] = z[:, LANES:].reshape(2, rows, LANES)

    pieces = return_pieces(rows)
    for q, (start, count) in enumerate(pieces):
        for s in range(start // SUB, (start + count) // SUB):
            at = pl.ds(s * SUB, SUB)
            conv = dot(m_last[s], x1[:, at, :].reshape(slabs * SUB, LANES))
            direct = gain[...] * u_in[:, at, :].reshape(groups * SUB, LANES).astype(F32)
            v_out[:, at, :] = (conv + direct).astype(BF16).reshape(groups, SUB, LANES)
        spread(v_out, f_in, pl.ds(start, count), q, 1)

    @pl.when(me > 0)
    def _():
        halo_q.wait_recv()

    @pl.loop(0, chunks)
    def _(q):
        @pl.loop(0, groups, unroll=4)
        def _(j):
            feat_q[j, rows_of(q), :] = featured(0, q, j)

    def swap(q, at):
        return pltpu.make_async_remote_copy(
            src_ref=part_out.at[at],
            dst_ref=part_in.at[at],
            send_sem=send_sem.at[2],
            recv_sem=recv_p.at[q],
            device_id=(me, other),
            device_id_type=MESH_ID,
        )

    theirs = pl.ds(pl.multiple_of(other * half, half), half)
    ours = pl.ds(pl.multiple_of(mine * half, half), half)
    groups_of_rows = projected_pieces(rows)
    for q, (start, count) in enumerate(groups_of_rows):
        at = pl.ds(start, count)
        for i, (low, size) in enumerate(pieces):
            if start <= low < start + count:
                await_chunk(f_in, pl.ds(low, size), i, recv_f)
        for j in range(groups):
            product = feat_q[j, at, :].astype(F32) * f_in[j, at, :].astype(F32)
            gated[0:count, j * LANES : (j + 1) * LANES] = product.astype(BF16)
        part_out[at, :] = dot(gated[0:count, :], w[:, theirs]).astype(BF16)
        swap(q, at).start()
        part_own[at, :] = dot(gated[0:count, :], w[:, ours]).astype(BF16)

    for q, (start, count) in enumerate(groups_of_rows):
        at = pl.ds(start, count)
        swap(q, at).wait_recv()
        total = part_own[at, :].astype(F32) + part_in[at, :].astype(F32)
        out[at, :] = total.astype(BF16)

    @pl.when(me < groups - 1)
    def _():
        halo_kv.wait_send()
        halo_q.wait_send()

    sent = g_out.at[pl.ds(0, groups - 1)]
    pltpu.make_async_copy(sent, sent, send_sem.at[0]).wait()
    sent = v_out.at[pl.ds(0, groups - 1)]
    pltpu.make_async_copy(sent, sent, send_sem.at[1]).wait()
    pltpu.make_async_copy(part_out, part_out, send_sem.at[2]).wait()


def fused(projected, feat_weight, long_filter, skip_gain, out_values, out_scales):
    groups = lax.axis_size("seq")
    rows, local_ch = projected.shape[1:]
    out_width = out_values.shape[1]
    half = out_width // 2
    tables = dft_tables(groups, rows)
    slabs = tables[0].shape[1] // SUB
    hbm = pl.BlockSpec(memory_space=pl.ANY)
    vmem = pl.BlockSpec(memory_space=pltpu.VMEM)
    smem = pl.BlockSpec(memory_space=pltpu.SMEM)
    block = pltpu.VMEM((groups, rows, LANES), BF16)
    chunks = rows // CHUNK
    return pl.pallas_call(
        functools.partial(fused_kernel, groups, rows),
        out_shape=jax.ShapeDtypeStruct((rows, half), BF16),
        in_specs=[hbm, hbm, hbm, vmem, hbm, smem, hbm, hbm, hbm, hbm],
        out_specs=vmem,
        scratch_shapes=[
            pltpu.VMEM((3, RIM + rows, local_ch), BF16),
            pltpu.VMEM(feat_weight.shape, F32),
            pltpu.VMEM((RIM, local_ch), BF16),
            pltpu.VMEM((RIM, local_ch), BF16),
            block,
            block,
            block,
            block,
            block,
            pltpu.VMEM(long_filter.shape, F32),
            block,
            pltpu.VMEM((slabs, rows, LANES), BF16),
            pltpu.VMEM((slabs // 4, 2 * rows, 2 * LANES), F32),
            pltpu.VMEM(tables[0].shape, BF16),
            pltpu.VMEM(tables[1].shape, BF16),
            pltpu.VMEM(tables[2].shape, BF16),
            pltpu.VMEM(tables[3].shape, BF16),
            pltpu.VMEM(out_values.shape, BF16),
            pltpu.VMEM((rows // 2, local_ch), BF16),
            pltpu.VMEM((rows, half), BF16),
            pltpu.VMEM((rows, half), BF16),
            pltpu.VMEM((rows, half), BF16),
            pltpu.SemaphoreType.DMA((8,)),
            pltpu.SemaphoreType.DMA((4,)),
            pltpu.SemaphoreType.DMA((3,)),
            pltpu.SemaphoreType.DMA((chunks,)),
            pltpu.SemaphoreType.DMA((len(return_pieces(rows)),)),
            pltpu.SemaphoreType.DMA((len(projected_pieces(rows)),)),
        ],
        compiler_params=pltpu.CompilerParams(
            collective_id=0, has_side_effects=True, vmem_limit_bytes=58 * 2**20
        ),
        cost_estimate=pl.CostEstimate(
            flops=10 * 10**9, bytes_accessed=32 * 2**20, transcendentals=0
        ),
    )(
        projected,
        feat_weight,
        long_filter,
        skip_gain.reshape(1, -1),
        out_values,
        out_scales,
        *[jnp.asarray(x) for x in tables],
    )


def fits(projected, long_filter, out_values):
    groups = lax.axis_size("seq")
    rows, local_ch = projected.shape[1:]
    return (
        lax.axis_size("tensor") == 2
        and long_filter.shape[0] == LANES
        and local_ch == groups * LANES
        and rows == 2 * LANES
        and groups == SUB
        and out_values.shape[1] % (2 * LANES) == 0
    )


TRIPLE = lax.Precision.HIGH


def passed_along(x, axis, by):
    size = lax.axis_size(axis)
    pairs = [(i, i + by) for i in range(size) if 0 <= i + by < size]
    return lax.ppermute(x, axis, pairs)


def split_length(whole):
    for candidate in range(2, whole + 1, 2):
        if whole % candidate == 0 and candidate * candidate >= whole:
            return (candidate, whole // candidate)
    return (whole, 1)


def angle_pair(row_count, col_count, period):
    row_ids = lax.broadcasted_iota(jnp.int32, (row_count, col_count), 0)
    col_ids = lax.broadcasted_iota(jnp.int32, (row_count, col_count), 1)
    angles = (row_ids * col_ids % period).astype(jnp.float32) * (2.0 * math.pi / period)
    return (jnp.cos(angles), jnp.sin(angles))


def make_tables(length):
    whole = 2 * length
    size_a, size_b = split_length(whole)
    return (
        angle_pair(size_a, size_a, size_a),
        angle_pair(size_b, size_b, size_b),
        angle_pair(size_a, size_b, whole),
        size_a,
        size_b,
    )


def right_mul(signal, matrix):
    return jnp.einsum("ckn,nm->ckm", signal, matrix, precision=TRIPLE)


def forward(signal, tables):
    (cos_a, sin_a), (cos_b, sin_b), (cos_t, sin_t), size_a, size_b = tables
    half_a = size_a // 2
    blocks = signal.reshape(signal.shape[0], half_a, size_b)
    real_a = jnp.einsum("kn,cnb->ckb", cos_a[:, :half_a], blocks, precision=TRIPLE)
    imag_a = -jnp.einsum("kn,cnb->ckb", sin_a[:, :half_a], blocks, precision=TRIPLE)
    real_t = real_a * cos_t + imag_a * sin_t
    imag_t = imag_a * cos_t - real_a * sin_t
    real_f = right_mul(real_t, cos_b) + right_mul(imag_t, sin_b)
    imag_f = right_mul(imag_t, cos_b) - right_mul(real_t, sin_b)
    return (real_f, imag_f)


def inverse(real_f, imag_f, tables):
    (cos_a, sin_a), (cos_b, sin_b), (cos_t, sin_t), size_a, size_b = tables
    half_a = size_a // 2
    real_z = right_mul(real_f, cos_b) - right_mul(imag_f, sin_b)
    imag_z = right_mul(imag_f, cos_b) + right_mul(real_f, sin_b)
    real_w = real_z * cos_t - imag_z * sin_t
    imag_w = imag_z * cos_t + real_z * sin_t
    out_half = jnp.einsum("nk,ckb->cnb", cos_a[:half_a, :], real_w, precision=TRIPLE) - jnp.einsum(
        "nk,ckb->cnb", sin_a[:half_a, :], imag_w, precision=TRIPLE
    )
    return out_half.reshape(out_half.shape[0], half_a * size_b) * (1.0 / (size_a * size_b))


def long_mix(gated_kv, spectrum, own_gain, tables):
    kv_values = gated_kv.astype(jnp.float32)
    real_u, imag_u = forward(kv_values, tables)
    real_h, imag_h = spectrum
    real_p = real_u * real_h - imag_u * imag_h
    imag_p = real_u * imag_h + imag_u * real_h
    convolved = inverse(real_p, imag_p, tables)
    return (convolved + own_gain[:, None] * kv_values).astype(jnp.bfloat16)


def featurize(extended, weights, length):
    tap_count = weights.shape[1]
    running = jnp.zeros(extended.shape[:2] + (length,), jnp.float32)
    for lag_idx in range(tap_count):
        offset = tap_count - 1 - lag_idx
        running = running + weights[:, lag_idx, :, None] * extended[
            :, :, offset : offset + length
        ].astype(jnp.float32)
    return running.astype(jnp.bfloat16)


def multiply_round(left_arr, right_arr):
    return (left_arr.astype(jnp.float32) * right_arr.astype(jnp.float32)).astype(jnp.bfloat16)


def local(projected, feat_weight, long_filter, skip_gain, out_values, out_scales):
    if fits(projected, long_filter, out_values):
        return fused(projected, feat_weight, long_filter, skip_gain, out_values, out_scales)
    groups = lax.axis_size("seq")
    tok_rows = projected.shape[1]
    local_ch = projected.shape[2]
    length = tok_rows * groups
    tables = make_tables(length)
    spectrum = forward(long_filter, tables)
    columns = jnp.transpose(projected, (0, 2, 1))
    rim_width = KS - 1
    prior_rows = passed_along(columns[:, :, tok_rows - rim_width :], "seq", 1)
    featured = featurize(jnp.concatenate([prior_rows, columns], axis=2), feat_weight, tok_rows)
    regrouped = lax.all_to_all(featured, "seq", split_axis=1, concat_axis=2, tiled=True)
    gated_kv = multiply_round(regrouped[1], regrouped[2])
    filtered = long_mix(gated_kv, spectrum, skip_gain, tables)
    gated = multiply_round(regrouped[0], filtered)
    gated_home = lax.all_to_all(gated, "seq", split_axis=1, concat_axis=0, tiled=True)
    block_count = local_ch // BLK
    out_width = out_values.shape[1]
    stacked = gated_home.reshape(block_count, BLK, tok_rows)
    weight_blocks = out_values.reshape(block_count, BLK, out_width)
    scale_cols = jnp.repeat(out_scales, BLK, axis=1)
    products = jnp.einsum(
        "bkn,bkt->bnt", weight_blocks, stacked, preferred_element_type=jnp.float32
    )
    summed = lax.psum_scatter(
        jnp.sum(products * scale_cols[:, :, None], axis=0).astype(jnp.bfloat16),
        "tensor",
        scatter_dimension=0,
        tiled=True,
    )
    return jnp.transpose(summed, (1, 0))


def solution(mesh):
    return jax.shard_map(
        local,
        mesh=mesh,
        in_specs=(
            P(None, "seq", "tensor"),
            P(None, None, "tensor"),
            P(("tensor", "seq"), None),
            P(("tensor", "seq")),
            P("tensor", None),
            P("tensor", None),
        ),
        out_specs=P("seq", "tensor"),
        check_vma=False,
    )
```

```python
import functools
import math

import jax
import jax.numpy as jnp
import ml_dtypes
import numpy as np
from jax import lax
from jax.experimental import pallas as pl
from jax.experimental.pallas import tpu as pltpu
from jax.sharding import PartitionSpec as P

KS = 7
BLK = 128
LANES = 128
RIM = 16
SUB = 16
CHUNK = 64
MESH_ID = pl.DeviceIdType.MESH
BF16 = jnp.bfloat16
F32 = jnp.float32


def dft_tables(groups, rows):
    whole = 2 * groups * rows
    kept = groups + 1
    padded = kept + kept % 2
    n_a = np.arange(groups)
    k_a = np.arange(kept)
    r = np.arange(rows)
    turns = k_a[:, None, None] * (n_a[None, :, None] * rows + r[None, None, :]) % whole
    angles = turns * (2.0 * np.pi / whole)
    parts = np.stack([np.cos(angles), -np.sin(angles)], axis=1)
    blocks = parts.reshape(kept, 2, groups, rows // SUB, SUB)
    first = np.zeros((rows // SUB, padded, 2, SUB, groups, SUB))
    last = np.zeros((rows // SUB, groups, SUB, padded, 2, SUB))
    weight = np.full((kept,), 2.0 / whole)
    weight[0] = weight[-1] = 1.0 / whole
    for lo in range(SUB):
        cut = blocks[:, :, :, :, lo]
        first[:, :kept, :, lo, :, lo] = cut.transpose(3, 0, 1, 2)
        last[:, :, lo, :kept, :, lo] = (cut * weight[:, None, None, None]).transpose(3, 2, 0, 1)
    first = first.reshape(rows // SUB, padded * 2 * SUB, groups * SUB)
    last = last.reshape(rows // SUB, groups * SUB, padded * 2 * SUB)
    inner = (r[:, None] * r[None, :] % rows) * (2.0 * np.pi / rows)
    cos, sin = np.cos(inner), np.sin(inner)
    ahead = np.block([[cos, sin], [-sin, cos]])
    back = np.block([[cos, -sin], [sin, cos]])
    return [x.astype(ml_dtypes.bfloat16) for x in (first, ahead, back, last)]


def return_pieces(rows):
    return [(start, CHUNK) for start in range(0, rows, CHUNK)]


def projected_pieces(rows):
    return [(0, rows // 2)] + [(start, CHUNK) for start in range(rows // 2, rows, CHUNK)]


def dot(a, b):
    return jnp.dot(a, b, preferred_element_type=F32)


def fused_kernel(
    groups,
    rows,
    proj,
    taps_hbm,
    filt,
    gain,
    weights,
    scales,
    t_first,
    t_ahead,
    t_back,
    t_last,
    out,
    pb,
    taps,
    rim_out,
    rim_in,
    g_out,
    u_in,
    v_out,
    f_in,
    feat_q,
    fl,
    ft,
    x1,
    spec,
    m_first,
    m_ahead,
    m_back,
    m_last,
    w,
    gated,
    part_own,
    part_out,
    part_in,
    loc_sem,
    halo_sem,
    send_sem,
    recv_u,
    recv_f,
    recv_p,
):
    me = lax.axis_index("seq")
    mine = lax.axis_index("tensor")
    other = 1 - mine
    chunks = rows // CHUNK
    length = groups * rows
    half = part_own.shape[1]

    load_k = pltpu.make_async_copy(proj, pb.at[:, pl.ds(RIM, rows)], loc_sem.at[0])
    load_k.start()
    load_taps = pltpu.make_async_copy(taps_hbm, taps, loc_sem.at[7])
    load_taps.start()

    barrier = pltpu.get_barrier_semaphore()

    @pl.loop(1, groups)
    def _(step):
        peer = lax.rem(me + step, groups)
        pl.semaphore_signal(barrier, inc=1, device_id=(peer, mine), device_id_type=MESH_ID)

    pl.semaphore_signal(barrier, inc=1, device_id=(me, other), device_id_type=MESH_ID)
    pl.semaphore_wait(barrier, groups)

    def halo(src, dst, slot):
        return pltpu.make_async_remote_copy(
            src_ref=src,
            dst_ref=dst,
            send_sem=halo_sem.at[slot],
            recv_sem=halo_sem.at[slot + 1],
            device_id=(lax.rem(me + 1, groups), mine),
            device_id_type=MESH_ID,
        )

    halo_kv = halo(rim_out, rim_in, 0)
    halo_q = halo(proj.at[0, pl.ds(rows - RIM, RIM)], pb.at[0, pl.ds(0, RIM)], 2)

    @pl.when(me == 0)
    def _():
        pb[:, 0:RIM, :] = jnp.zeros((pb.shape[0], RIM, pb.shape[2]), BF16)

    load_k.wait()
    few = RIM // 2

    @pl.when(me < groups - 1)
    def _():
        ends = [pb[p, rows : rows + RIM, :].astype(F32)[few:] for p in (1, 2)]
        rim_out[...] = jnp.concatenate(ends, axis=0).astype(BF16)
        halo_kv.start()

    load_taps.wait()
    loads = [
        pltpu.make_async_copy(src, dst, loc_sem.at[1 + i])
        for i, (src, dst) in enumerate(
            (
                (filt, fl),
                (t_first, m_first),
                (t_ahead, m_ahead),
                (t_back, m_back),
                (t_last, m_last),
                (weights, w),
            )
        )
    ]
    for load in loads:
        load.start()

    def featured(p, q, j):
        lanes = pl.ds(pl.multiple_of(j * LANES, LANES), LANES)
        x = pb[p, pl.ds(pl.multiple_of(q * CHUNK, CHUNK), CHUNK + RIM), lanes].astype(F32)
        run = None
        for lag in range(KS):
            term = taps[p, lag : lag + 1, lanes] * x[RIM - lag : RIM - lag + CHUNK]
            run = term if run is None else run + term
        return run.astype(BF16)

    def rows_of(q):
        return pl.ds(pl.multiple_of(q * CHUNK, CHUNK), CHUNK)

    def spread(src, dst, at, q, recv):
        @pl.loop(1, groups)
        def _(step):
            peer = lax.rem(me + step, groups)
            pltpu.make_async_remote_copy(
                src_ref=src.at[peer, at],
                dst_ref=dst.at[me, at],
                send_sem=send_sem.at[recv],
                recv_sem=(recv_u if recv == 0 else recv_f).at[q],
                device_id=(peer, mine),
                device_id_type=MESH_ID,
            ).start()

        dst[me, at, :] = src[me, at, :]

    def await_chunk(dst, at, q, sem):
        view = dst.at[pl.ds(0, groups - 1), at]
        pltpu.make_async_copy(view, view, sem.at[q]).wait()

    def feature_chunk(q):
        @pl.loop(0, groups)
        def _(j):
            k = featured(1, q, j).astype(F32)
            v = featured(2, q, j).astype(F32)
            g_out[j, rows_of(q), :] = (k * v).astype(BF16)

        spread(g_out, u_in, rows_of(q), q, 0)

    @pl.loop(1, chunks)
    def _(q):
        feature_chunk(q)

    @pl.when(me > 0)
    def _():
        halo_kv.wait_recv()
        both = rim_in[...].astype(F32)
        blank = jnp.zeros((few, pb.shape[2]), F32)
        for p in (1, 2):
            own = both[(p - 1) * few : p * few]
            pb[p, 0:RIM, :] = jnp.concatenate([blank, own], axis=0).astype(BF16)

    feature_chunk(0)

    loads[0].wait()

    @pl.loop(0, groups, unroll=4)
    def _(a):
        for part in range(rows // LANES):
            start = pl.multiple_of(a * rows + part * LANES, LANES)
            ft[a, part * LANES : (part + 1) * LANES, :] = fl[:, pl.ds(start, LANES)].astype(BF16).T

    for load in loads[1:5]:
        load.wait()

    slabs = x1.shape[0]
    pairs = slabs // 4

    def first_stage(src, s):
        at = pl.ds(pl.multiple_of(s * SUB, SUB), SUB)
        block = src[:, at, :].reshape(groups * SUB, LANES)
        x1[:, at, :] = dot(m_first[s], block).astype(BF16).reshape(slabs, SUB, LANES)

    def pair_of(j):
        left = x1[pl.ds(4 * j, 2)].reshape(2 * rows, LANES)
        right = x1[pl.ds(4 * j + 2, 2)].reshape(2 * rows, LANES)
        return jnp.concatenate([left, right], axis=1)

    @pl.loop(0, rows // SUB, unroll=4)
    def _(s):
        first_stage(ft, s)

    for j in range(pairs):
        spec[j] = dot(m_ahead[...], pair_of(j))

    per_chunk = CHUNK // SUB

    @pl.loop(0, chunks)
    def _(i):
        q = lax.rem(i + 1, chunks)
        await_chunk(u_in, rows_of(q), q, recv_u)

        @pl.loop(0, per_chunk, unroll=per_chunk)
        def _(s):
            first_stage(u_in, q * per_chunk + s)

    @pl.when(me < groups - 1)
    def _():
        halo_q.start()

    for j in range(pairs):
        values = dot(m_ahead[...], pair_of(j))
        re_u, im_u = values[:rows], values[rows:]
        re_h, im_h = spec[j, 0:rows, :], spec[j, rows : 2 * rows, :]
        product = jnp.concatenate(
            [re_u * re_h - im_u * im_h, re_u * im_h + im_u * re_h], axis=0
        ).astype(BF16)
        z = dot(m_back[...], product).astype(BF16)
        x1[pl.ds(4 * j, 2)] = z[:, :LANES].reshape(2, rows, LANES)
        x1[pl.ds(4 * j + 2, 2)] = z[:, LANES:].reshape(2, rows, LANES)

    pieces = return_pieces(rows)
    for q, (start, count) in enumerate(pieces):
        for s in range(start // SUB, (start + count) // SUB):
            at = pl.ds(s * SUB, SUB)
            conv = dot(m_last[s], x1[:, at, :].reshape(slabs * SUB, LANES))
            direct = gain[...] * u_in[:, at, :].reshape(groups * SUB, LANES).astype(F32)
            v_out[:, at, :] = (conv + direct).astype(BF16).reshape(groups, SUB, LANES)
        spread(v_out, f_in, pl.ds(start, count), q, 1)

    loads[5].wait()
    cuts = w.shape[1] // BLK

    @pl.loop(0, w.shape[0] // BLK)
    def _(b):
        at = pl.ds(pl.multiple_of(b * BLK, BLK), BLK)
        for n in range(cuts):
            cols = slice(n * BLK, (n + 1) * BLK)
            scale = jnp.full((BLK, BLK), scales[b, n], F32).astype(BF16)
            w[at, cols] = w[at, cols] * scale

    @pl.when(me > 0)
    def _():
        halo_q.wait_recv()

    @pl.loop(0, chunks)
    def _(q):
        @pl.loop(0, groups, unroll=4)
        def _(j):
            feat_q[j, rows_of(q), :] = featured(0, q, j)

    def swap(q, at):
        return pltpu.make_async_remote_copy(
            src_ref=part_out.at[at],
            dst_ref=part_in.at[at],
            send_sem=send_sem.at[2],
            recv_sem=recv_p.at[q],
            device_id=(me, other),
            device_id_type=MESH_ID,
        )

    theirs = pl.ds(pl.multiple_of(other * half, half), half)
    ours = pl.ds(pl.multiple_of(mine * half, half), half)
    groups_of_rows = projected_pieces(rows)
    for q, (start, count) in enumerate(groups_of_rows):
        at = pl.ds(start, count)
        for i, (low, size) in enumerate(pieces):
            if start <= low < start + count:
                await_chunk(f_in, pl.ds(low, size), i, recv_f)
        for j in range(groups):
            product = feat_q[j, at, :].astype(F32) * f_in[j, at, :].astype(F32)
            gated[0:count, j * LANES : (j + 1) * LANES] = product.astype(BF16)
        part_out[at, :] = dot(gated[0:count, :], w[:, theirs]).astype(BF16)
        swap(q, at).start()
        part_own[at, :] = dot(gated[0:count, :], w[:, ours]).astype(BF16)

    for q, (start, count) in enumerate(groups_of_rows):
        at = pl.ds(start, count)
        swap(q, at).wait_recv()
        total = part_own[at, :].astype(F32) + part_in[at, :].astype(F32)
        out[at, :] = total.astype(BF16)

    @pl.when(me < groups - 1)
    def _():
        halo_kv.wait_send()
        halo_q.wait_send()

    sent = g_out.at[pl.ds(0, groups - 1)]
    pltpu.make_async_copy(sent, sent, send_sem.at[0]).wait()
    sent = v_out.at[pl.ds(0, groups - 1)]
    pltpu.make_async_copy(sent, sent, send_sem.at[1]).wait()
    pltpu.make_async_copy(part_out, part_out, send_sem.at[2]).wait()


def fused(projected, feat_weight, long_filter, skip_gain, out_values, out_scales):
    groups = lax.axis_size("seq")
    rows, local_ch = projected.shape[1:]
    out_width = out_values.shape[1]
    half = out_width // 2
    tables = dft_tables(groups, rows)
    slabs = tables[0].shape[1] // SUB
    hbm = pl.BlockSpec(memory_space=pl.ANY)
    vmem = pl.BlockSpec(memory_space=pltpu.VMEM)
    smem = pl.BlockSpec(memory_space=pltpu.SMEM)
    block = pltpu.VMEM((groups, rows, LANES), BF16)
    chunks = rows // CHUNK
    return pl.pallas_call(
        functools.partial(fused_kernel, groups, rows),
        out_shape=jax.ShapeDtypeStruct((rows, half), BF16),
        in_specs=[hbm, hbm, hbm, vmem, hbm, smem, hbm, hbm, hbm, hbm],
        out_specs=vmem,
        scratch_shapes=[
            pltpu.VMEM((3, RIM + rows, local_ch), BF16),
            pltpu.VMEM(feat_weight.shape, F32),
            pltpu.VMEM((RIM, local_ch), BF16),
            pltpu.VMEM((RIM, local_ch), BF16),
            block,
            block,
            block,
            block,
            block,
            pltpu.VMEM(long_filter.shape, F32),
            block,
            pltpu.VMEM((slabs, rows, LANES), BF16),
            pltpu.VMEM((slabs // 4, 2 * rows, 2 * LANES), F32),
            pltpu.VMEM(tables[0].shape, BF16),
            pltpu.VMEM(tables[1].shape, BF16),
            pltpu.VMEM(tables[2].shape, BF16),
            pltpu.VMEM(tables[3].shape, BF16),
            pltpu.VMEM(out_values.shape, BF16),
            pltpu.VMEM((rows // 2, local_ch), BF16),
            pltpu.VMEM((rows, half), BF16),
            pltpu.VMEM((rows, half), BF16),
            pltpu.VMEM((rows, half), BF16),
            pltpu.SemaphoreType.DMA((8,)),
            pltpu.SemaphoreType.DMA((4,)),
            pltpu.SemaphoreType.DMA((3,)),
            pltpu.SemaphoreType.DMA((chunks,)),
            pltpu.SemaphoreType.DMA((len(return_pieces(rows)),)),
            pltpu.SemaphoreType.DMA((len(projected_pieces(rows)),)),
        ],
        compiler_params=pltpu.CompilerParams(
            collective_id=0, has_side_effects=True, vmem_limit_bytes=58 * 2**20
        ),
        cost_estimate=pl.CostEstimate(
            flops=10 * 10**9, bytes_accessed=32 * 2**20, transcendentals=0
        ),
    )(
        projected,
        feat_weight,
        long_filter,
        skip_gain.reshape(1, -1),
        out_values,
        out_scales,
        *[jnp.asarray(x) for x in tables],
    )


def fits(projected, long_filter, out_values):
    groups = lax.axis_size("seq")
    rows, local_ch = projected.shape[1:]
    return (
        lax.axis_size("tensor") == 2
        and long_filter.shape[0] == LANES
        and local_ch == groups * LANES
        and rows == 2 * LANES
        and groups == SUB
        and out_values.shape[1] % (2 * LANES) == 0
    )


TRIPLE = lax.Precision.HIGH


def passed_along(x, axis, by):
    size = lax.axis_size(axis)
    pairs = [(i, i + by) for i in range(size) if 0 <= i + by < size]
    return lax.ppermute(x, axis, pairs)


def split_length(whole):
    for candidate in range(2, whole + 1, 2):
        if whole % candidate == 0 and candidate * candidate >= whole:
            return (candidate, whole // candidate)
    return (whole, 1)


def angle_pair(row_count, col_count, period):
    row_ids = lax.broadcasted_iota(jnp.int32, (row_count, col_count), 0)
    col_ids = lax.broadcasted_iota(jnp.int32, (row_count, col_count), 1)
    angles = (row_ids * col_ids % period).astype(jnp.float32) * (2.0 * math.pi / period)
    return (jnp.cos(angles), jnp.sin(angles))


def make_tables(length):
    whole = 2 * length
    size_a, size_b = split_length(whole)
    return (
        angle_pair(size_a, size_a, size_a),
        angle_pair(size_b, size_b, size_b),
        angle_pair(size_a, size_b, whole),
        size_a,
        size_b,
    )


def right_mul(signal, matrix):
    return jnp.einsum("ckn,nm->ckm", signal, matrix, precision=TRIPLE)


def forward(signal, tables):
    (cos_a, sin_a), (cos_b, sin_b), (cos_t, sin_t), size_a, size_b = tables
    half_a = size_a // 2
    blocks = signal.reshape(signal.shape[0], half_a, size_b)
    real_a = jnp.einsum("kn,cnb->ckb", cos_a[:, :half_a], blocks, precision=TRIPLE)
    imag_a = -jnp.einsum("kn,cnb->ckb", sin_a[:, :half_a], blocks, precision=TRIPLE)
    real_t = real_a * cos_t + imag_a * sin_t
    imag_t = imag_a * cos_t - real_a * sin_t
    real_f = right_mul(real_t, cos_b) + right_mul(imag_t, sin_b)
    imag_f = right_mul(imag_t, cos_b) - right_mul(real_t, sin_b)
    return (real_f, imag_f)


def inverse(real_f, imag_f, tables):
    (cos_a, sin_a), (cos_b, sin_b), (cos_t, sin_t), size_a, size_b = tables
    half_a = size_a // 2
    real_z = right_mul(real_f, cos_b) - right_mul(imag_f, sin_b)
    imag_z = right_mul(imag_f, cos_b) + right_mul(real_f, sin_b)
    real_w = real_z * cos_t - imag_z * sin_t
    imag_w = imag_z * cos_t + real_z * sin_t
    out_half = jnp.einsum("nk,ckb->cnb", cos_a[:half_a, :], real_w, precision=TRIPLE) - jnp.einsum(
        "nk,ckb->cnb", sin_a[:half_a, :], imag_w, precision=TRIPLE
    )
    return out_half.reshape(out_half.shape[0], half_a * size_b) * (1.0 / (size_a * size_b))


def long_mix(gated_kv, spectrum, own_gain, tables):
    kv_values = gated_kv.astype(jnp.float32)
    real_u, imag_u = forward(kv_values, tables)
    real_h, imag_h = spectrum
    real_p = real_u * real_h - imag_u * imag_h
    imag_p = real_u * imag_h + imag_u * real_h
    convolved = inverse(real_p, imag_p, tables)
    return (convolved + own_gain[:, None] * kv_values).astype(jnp.bfloat16)


def featurize(extended, weights, length):
    tap_count = weights.shape[1]
    running = jnp.zeros(extended.shape[:2] + (length,), jnp.float32)
    for lag_idx in range(tap_count):
        offset = tap_count - 1 - lag_idx
        running = running + weights[:, lag_idx, :, None] * extended[
            :, :, offset : offset + length
        ].astype(jnp.float32)
    return running.astype(jnp.bfloat16)


def multiply_round(left_arr, right_arr):
    return (left_arr.astype(jnp.float32) * right_arr.astype(jnp.float32)).astype(jnp.bfloat16)


def local(projected, feat_weight, long_filter, skip_gain, out_values, out_scales):
    if fits(projected, long_filter, out_values):
        return fused(projected, feat_weight, long_filter, skip_gain, out_values, out_scales)
    groups = lax.axis_size("seq")
    tok_rows = projected.shape[1]
    local_ch = projected.shape[2]
    length = tok_rows * groups
    tables = make_tables(length)
    spectrum = forward(long_filter, tables)
    columns = jnp.transpose(projected, (0, 2, 1))
    rim_width = KS - 1
    prior_rows = passed_along(columns[:, :, tok_rows - rim_width :], "seq", 1)
    featured = featurize(jnp.concatenate([prior_rows, columns], axis=2), feat_weight, tok_rows)
    regrouped = lax.all_to_all(featured, "seq", split_axis=1, concat_axis=2, tiled=True)
    gated_kv = multiply_round(regrouped[1], regrouped[2])
    filtered = long_mix(gated_kv, spectrum, skip_gain, tables)
    gated = multiply_round(regrouped[0], filtered)
    gated_home = lax.all_to_all(gated, "seq", split_axis=1, concat_axis=0, tiled=True)
    block_count = local_ch // BLK
    out_width = out_values.shape[1]
    stacked = gated_home.reshape(block_count, BLK, tok_rows)
    weight_blocks = out_values.reshape(block_count, BLK, out_width)
    scale_cols = jnp.repeat(out_scales, BLK, axis=1)
    products = jnp.einsum(
        "bkn,bkt->bnt", weight_blocks, stacked, preferred_element_type=jnp.float32
    )
    summed = lax.psum_scatter(
        jnp.sum(products * scale_cols[:, :, None], axis=0).astype(jnp.bfloat16),
        "tensor",
        scatter_dimension=0,
        tiled=True,
    )
    return jnp.transpose(summed, (1, 0))


def solution(mesh):
    return jax.shard_map(
        local,
        mesh=mesh,
        in_specs=(
            P(None, "seq", "tensor"),
            P(None, None, "tensor"),
            P(("tensor", "seq"), None),
            P(("tensor", "seq")),
            P("tensor", None),
            P("tensor", None),
        ),
        out_specs=P("seq", "tensor"),
        check_vma=False,
    )
```
